512 devices in a mesh: gx: 8 (over y), gy: 8 (over z), gz: 8 (over x, core).
Axes of the slice: x: 4, y: 8, z: 8, core: 2. Of those that a mesh axis runs over, the one named last changes fastest.
Arguments:
- couplings: float32 [18, 64, 64, 1024], P(None, 'gx', 'gy', 'gz'), may hold values from 0.05 to 2
- diagonal: float32 [3, 64, 64, 1024], P(None, 'gx', 'gy', 'gz'), may hold values from 0.01 to 0.1
- right_side: float32 [3, 64, 64, 1024], P(None, 'gx', 'gy', 'gz'), may hold values from -6 to 6
- guess: float32 [3, 64, 64, 1024], P(None, 'gx', 'gy', 'gz'), may hold values from -4 to 4
Outputs:
- solution: float32 [3, 64, 64, 1024], P(None, 'gx', 'gy', 'gz')
The draws below stay inside these ranges and needn't reach their ends.
All inputs are finite; a program needn't handle non-finite values.
Results may differ from the reference program's by a relative error of at most 0.00011.
Values sent between devices are 32-bit elements; how exact they have to be, the bound alone decides.
No kernel may reach another device: no remote copies, remote signals or barrier semaphores. Data moves between devices by JAX's collectives and lax.ppermute only.
A program may use at most 128 MiB of HBM per device.

```python
import math
import jax
import jax.numpy as jnp

LEVELS = 4
SWEEPS = 2
COARSE_SWEEPS = 8
NX = 64
NY = 64
NZ = 1024


def smooth_field(base_key, number):
    field_key = jax.random.fold_in(base_key, number)
    freq_key, angle_key, sign_key = jax.random.split(field_key, 3)
    freqs = jax.random.uniform(freq_key, (3, 3), jnp.float32, 0.5, 2.0)
    signs = jnp.where(jax.random.bernoulli(sign_key, 0.5, (3, 3)), 1.0, -1.0).astype(jnp.float32)
    freqs = freqs * signs
    angles = jax.random.uniform(angle_key, (3,), jnp.float32, 0.0, 2.0 * math.pi)
    coord_x = (jnp.arange(NX, dtype=jnp.float32) + 0.5) / NX
    coord_y = (jnp.arange(NY, dtype=jnp.float32) + 0.5) / NY
    coord_z = (jnp.arange(NZ, dtype=jnp.float32) + 0.5) / NZ
    result = jnp.zeros((NX, NY, NZ), jnp.float32)
    for wave in range(3):
        argument = freqs[wave, 0] * coord_x[:, None, None] + freqs[wave, 1] * coord_y[None, :, None] + freqs[wave, 2] * coord_z[None, None, :]
        result = result + jnp.cos(2.0 * math.pi * argument + angles[wave])
    return result / math.sqrt(1.5)


def draw_couplings(key, part):
    field_key = jax.random.fold_in(key, 1101)
    rough_key = jax.random.fold_in(key, 1102)
    sharpness = 3.0
    low_log = math.log(0.05)
    span_log = math.log(2.0) - math.log(0.05)
    planes = []
    for equation in range(3):
        fields = jnp.stack([smooth_field(field_key, 3 * equation + axis_number) for axis_number in range(3)])
        shares = jax.nn.softmax(sharpness * fields, axis=0)
        for axis_number in range(3):
            for side in range(2):
                uniform_part = jax.random.uniform(jax.random.fold_in(rough_key, 6 * equation + 2 * axis_number + side), (NX, NY, NZ), jnp.float32, 0.0, 1.0)
                exponent = 0.76 * shares[axis_number] + 0.24 * uniform_part
                planes.append(jnp.exp(low_log + span_log * exponent))
    return jnp.stack(planes).astype(jnp.float32)


def draw_diagonal(key, part):
    field_key = jax.random.fold_in(key, 2201)
    rough_key = jax.random.fold_in(key, 2202)
    power = 3.0
    planes = []
    for equation in range(3):
        region = jax.nn.sigmoid(2.0 * smooth_field(field_key, equation)) ** power
        uniform_part = jax.random.uniform(jax.random.fold_in(rough_key, equation), (NX, NY, NZ), jnp.float32, 0.0, 1.0)
        exponent = 0.68 * region + 0.32 * uniform_part
        planes.append(0.01 * jnp.exp(math.log(10.0) * exponent))
    return jnp.stack(planes).astype(jnp.float32)


def shard_levels(stream_key, shape, cuts, low, top_value):
    level = 1.0
    for dim, parts in cuts:
        steps = jax.random.uniform(jax.random.fold_in(jax.random.fold_in(stream_key, 6), dim), (parts,), jnp.float32, low / len(cuts), top_value / len(cuts))
        level = level * jnp.repeat(jnp.exp(steps), shape[dim] // parts).reshape((-1,) + (1,) * (len(shape) - 1 - dim))
    return level


def normal_values(key, shape, deviation, most, shards=(), held_as=jnp.bfloat16):
    gain = shard_levels(key, shape, shards, -0.22, 0.18) if shards else 1.0
    values = jax.random.normal(key, shape, jnp.float32) * deviation * gain
    return jnp.minimum(jnp.maximum(values, -most), most).astype(held_as)


def setup_inputs(seed: int = 0) -> dict:
    streams_of = jax.random.split(jax.random.key(seed), 5)
    couplings = draw_couplings(jax.random.fold_in(streams_of[4], 71), 0)
    diagonal = draw_diagonal(jax.random.fold_in(streams_of[4], 71), 0)
    right_side = normal_values(streams_of[2], (3, NX, NY, NZ), 1.0, 6.0, ((1, 8), (2, 8), (3, 8)), jnp.float32)
    guess = normal_values(streams_of[3], (3, NX, NY, NZ), 0.5, 4.0, ((1, 8), (2, 8), (3, 8)), jnp.float32)
    return {"couplings": couplings, "diagonal": diagonal, "right_side": right_side, "guess": guess}


damping = 0.8


def pad_zero(field):
    return jnp.pad(field, ((0, 0), (1, 1), (1, 1), (1, 1)))


def operate(field, padded, weights, total):
    near = [padded[:, 2:, 1:-1, 1:-1], padded[:, :-2, 1:-1, 1:-1],
            padded[:, 1:-1, 2:, 1:-1], padded[:, 1:-1, :-2, 1:-1],
            padded[:, 1:-1, 1:-1, 2:], padded[:, 1:-1, 1:-1, :-2]]
    offdiag = weights[:, 0] * near[0]
    for index in range(1, 6):
        offdiag = offdiag + weights[:, index] * near[index]
    return total * field - offdiag


def coarsen(array):
    shape = array.shape
    count = len(shape)
    blocks = array.reshape(shape[:-3] + (shape[-3] // 2, 2, shape[-2] // 2, 2, shape[-1] // 2, 2))
    return jnp.mean(blocks, axis=(count - 2, count, count + 2))


def refine(array):
    return jnp.repeat(jnp.repeat(jnp.repeat(array, 2, axis=-3), 2, axis=-2), 2, axis=-1)


def hierarchy(couplings, diagonal):
    weights = couplings.reshape((3, 6) + diagonal.shape[1:])
    local_diag = diagonal
    result = []
    for level in range(LEVELS):
        if level > 0:
            weights = coarsen(weights) * 0.25
            local_diag = coarsen(local_diag)
        result.append((weights, local_diag + jnp.sum(weights, axis=1)))
    return result


def reference(couplings, diagonal, right_side, guess):
    levels = hierarchy(couplings, diagonal)

    def cycle(level, field, rhs):
        weights, total = levels[level]

        def sweep(value):
            return value + damping * (rhs - operate(value, pad_zero(value), weights, total)) / total

        if level == LEVELS - 1:
            for step in range(COARSE_SWEEPS):
                field = sweep(field)
            return field
        for step in range(SWEEPS):
            field = sweep(field)
        resid = rhs - operate(field, pad_zero(field), weights, total)
        coarse_rhs = coarsen(resid)
        correction = cycle(level + 1, jnp.zeros_like(coarse_rhs), coarse_rhs)
        field = field + refine(correction)
        for step in range(SWEEPS):
            field = sweep(field)
        return field

    return cycle(0, guess, right_side)
```

```python
import jax
import jax.numpy as jnp
from jax import lax
from jax.experimental import pallas as pl
from jax.experimental.pallas import tpu as pltpu
from jax.sharding import PartitionSpec as P


F32 = jnp.float32
LANES = 128
STATIC = 21
HALO2 = 20
MEANS = 84


def rolled(value, shift, axis):
    shift %= value.shape[axis]
    return value if shift == 0 else pltpu.roll(value, shift, axis)


def lanes_of(rows):
    return lax.broadcasted_iota(jnp.int32, (rows, LANES), 1)


def pair_matrix(weight):
    fine = lax.broadcasted_iota(jnp.int32, (LANES, LANES), 0)
    coarse = lax.broadcasted_iota(jnp.int32, (LANES, LANES), 1)
    return jnp.where((fine >> 1) == coarse, F32(weight), F32(0))


def exact_dot(left, right):
    return jnp.dot(left, right, precision=lax.Precision.HIGHEST, preferred_element_type=F32)


def call(body, name, outs, args, scratch=(), scalars=()):
    vmem = pl.BlockSpec(memory_space=pltpu.VMEM)
    smem = pl.BlockSpec(memory_space=pltpu.SMEM)
    return pl.pallas_call(
        body,
        name=name,
        out_shape=[jax.ShapeDtypeStruct((rows, LANES), F32) for rows in outs],
        in_specs=[smem] * len(scalars) + [vmem] * len(args),
        out_specs=[vmem] * len(outs),
        scratch_shapes=[pltpu.VMEM((rows, LANES), F32) for rows in scratch],
        compiler_params=pltpu.CompilerParams(vmem_limit_bytes=40 * 1024 * 1024),
    )(*scalars, *args)


class Stream:
    def __init__(self, count, rows, planes, halo, reach):
        self.count, self.rows, self.planes, self.halo, self.reach = count, rows, planes, halo, reach

    def extent(self, depth):
        return self.reach - depth

    def halo_rows(self):
        return self.halo * self.count * self.rows

    def grown_rows(self):
        return (self.planes + 2 * self.halo) * self.count * 16


FINE = [Stream(STATIC, 8, 8, 2, 2), Stream(3, 8, 8, 3, 3), Stream(1, 8, 8, 3, 3), Stream(1, 8, 8, 3, 3)]
MIDDLE = [Stream(18, 4, 4, 3, 4), Stream(3, 4, 4, 4, 5), Stream(3, 8, 8, 2, 2), Stream(1, 8, 8, 2, 2), Stream(1, 8, 8, 2, 2)]


def x_rows(streams):
    return sum(s.halo_rows() for s in streams)


def y_pieces(streams):
    offset = 0
    pieces = []
    for depth in range(1, 1 + max(s.halo for s in streams)):
        for index, s in enumerate(streams):
            if depth <= s.halo:
                planes = s.planes + 2 * s.extent(depth)
                pieces.append((index, depth, offset))
                offset += planes * s.count
    return pieces, offset


def y_rows(streams):
    total = y_pieces(streams)[1]
    return -(-total // 8) * 8


def pack_x(streams, mains, up, down):
    offset = 0
    for s, main in zip(streams, mains):
        size = s.halo_rows()
        whole = s.planes * s.count * s.rows
        up[pl.ds(offset, size), :] = main[pl.ds(whole - size, size), :]
        down[pl.ds(offset, size), :] = main[pl.ds(0, size), :]
        offset += size


def pack_y(streams, mains, low, high, up, down):
    starts = [sum(s.halo_rows() for s in streams[:i]) for i in range(len(streams))]
    pieces, total = y_pieces(streams)
    padded = y_rows(streams)
    for out, upward in ((up, True), (down, False)):
        if padded > total:
            out[pl.ds(padded - 8, 8), :] = jnp.zeros((8, LANES), F32)
        for index, depth, offset in pieces:
            s = streams[index]
            row = s.rows - depth if upward else depth - 1
            beyond = s.extent(depth)
            side = beyond * s.count
            middle = s.planes * s.count
            if beyond:
                first = starts[index] + (s.halo - beyond) * s.count * s.rows + row
                out[pl.ds(offset, side), :] = low[pl.ds(first, side, s.rows), :]
            out[pl.ds(offset + side, middle), :] = mains[index][pl.ds(row, middle, s.rows), :]
            if beyond:
                out[pl.ds(offset + side + middle, side), :] = high[pl.ds(starts[index] + row, side, s.rows), :]


def grow(streams, mains, low, high, below, above, grown):
    starts = [sum(s.halo_rows() for s in streams[:i]) for i in range(len(streams))]
    for index, s in enumerate(streams):
        out = grown[index]
        out[...] = jnp.zeros(out.shape, F32)
        edge = s.halo * s.count
        middle = s.planes * s.count
        for source, base, first, number in (
            (low, starts[index], 0, edge),
            (mains[index], 0, edge, middle),
            (high, starts[index], edge + middle, edge),
        ):
            if s.rows == 8:
                for tile in range(number):
                    out[pl.ds((first + tile) * 16, 8), :] = source[pl.ds(base + tile * 8, 8), :]
            else:
                for row in range(s.rows):
                    out[pl.ds(first * 16 + row, number, 16), :] = source[pl.ds(base + row, number, s.rows), :]
    for index, depth, offset in y_pieces(streams)[0]:
        s = streams[index]
        beyond = s.extent(depth)
        number = (s.planes + 2 * beyond) * s.count
        first = (s.halo - beyond) * s.count * 16
        grown[index][pl.ds(first + s.rows + depth - 1, number, 16), :] = above[pl.ds(offset, number), :]
        grown[index][pl.ds(first + 16 - depth, number, 16), :] = below[pl.ds(offset, number), :]


def prepare(c, d, b, g, stat, field, total, zup, zdown, coef1, scale1, total1, summed, means1, half2, sum2, sum3):
    lane = lanes_of(8)
    for x in range(8):
        up = jnp.zeros((8, LANES), F32)
        down = jnp.zeros((8, LANES), F32)
        packed = []
        for e in range(3):
            w = [c[6 * e + k, x] for k in range(6)]
            tot = d[e, x] + (((w[0] + w[1]) + (w[2] + w[3])) + (w[4] + w[5]))
            inverse = 0.8 / tot
            for k in range(6):
                packed.append((6 * e + k, w[k] * inverse))
            packed.append((18 + e, b[e, x] * inverse))
            field[pl.ds((x * 3 + e) * 8, 8), :] = g[e, x]
            total[pl.ds((x * 3 + e) * 8, 8), :] = tot * 1.25
        for a, value in packed:
            stat[pl.ds((x * STATIC + a) * 8, 8), :] = value
            inside = (lane >= 2 * a) & (lane < 2 * a + 2)
            up = jnp.where(inside, rolled(value, 2 * a + 2, 1), up)
            down = jnp.where(inside, rolled(value, 2 * a, 1), down)
        for e in range(3):
            base = 42 + 3 * e
            inside = (lane >= base) & (lane < base + 3)
            up = jnp.where(inside, rolled(g[e, x], base + 3, 1), up)
            down = jnp.where(inside, rolled(g[e, x], base, 1), down)
        zup[pl.ds(x * 8, 8), :] = up
        zdown[pl.ds(x * 8, 8), :] = down

    halve = pair_matrix(0.125)
    for x in range(4):
        for a in range(STATIC):
            one = c[a, 2 * x] + c[a, 2 * x + 1] if a < 18 else d[a - 18, 2 * x] + d[a - 18, 2 * x + 1]
            summed[pl.ds((x * STATIC + a) * 8, 8), :] = one
    means1[...] = exact_dot(summed[pl.ds(0, 336, 2), :] + summed[pl.ds(1, 336, 2), :], halve)
    for x in range(4):
        for e in range(3):
            w = [0.25 * means1[pl.ds((x * STATIC + 6 * e + k) * 4, 4), :] for k in range(6)]
            tot = means1[pl.ds((x * STATIC + 18 + e) * 4, 4), :] + (((w[0] + w[1]) + (w[2] + w[3])) + (w[4] + w[5]))
            tot = jnp.where(tot > 0, tot, F32(1))
            inverse = 0.8 / tot
            for k in range(6):
                coef1[pl.ds((x * 18 + 6 * e + k) * 4, 4), :] = w[k] * inverse
            scale1[pl.ds((x * 3 + e) * 4, 4), :] = inverse
            total1[pl.ds((x * 3 + e) * 4, 4), :] = tot * 1.25
    half2[...] = means1[pl.ds(0, 168, 2), :] + means1[pl.ds(1, 168, 2), :]
    for i in range(2):
        sum2[pl.ds(42 * i, 42), :] = half2[pl.ds(84 * i, 42), :] + half2[pl.ds(84 * i + 42, 42), :]
    sum2[pl.ds(0, MEANS), :] = exact_dot(sum2[...], halve)[:MEANS]
    sum3[pl.ds(0, 42), :] = sum2[pl.ds(0, 42), :] + sum2[pl.ds(42, 42), :]
    sum3[pl.ds(42, 6), :] = jnp.zeros((6, LANES), F32)
    means3 = exact_dot(sum3[pl.ds(0, 24, 2), :] + sum3[pl.ds(1, 24, 2), :], halve)
    sum2[pl.ds(0, STATIC), :] = sum2[pl.ds(0, STATIC), :] + rolled(means3, 32, 1)[:STATIC]
    zup[pl.ds(64, MEANS), :] = sum2[pl.ds(0, MEANS), :]
    zdown[pl.ds(64, MEANS), :] = sum2[pl.ds(0, MEANS), :]


def prepare_whole(c, d, b, g, stat, field, total, zup, zdown, coef1, scale1, total1, summed, means1, half2, sum2, sum3):
    sum2[pl.ds(80, 8), :] = jnp.zeros((8, LANES), F32)
    prepare(c, d, b, g, stat, field, total, zup, zdown, coef1, scale1, total1, summed, means1, half2, sum2, sum3)
    for out in (zup, zdown):
        out[pl.ds(148, 4), :] = jnp.zeros((4, LANES), F32)


Z_ROWS = 152


def fine_x(stat, field, zlow, zhigh, zown, up, down, gathered):
    pack_x(FINE, [stat, field, zlow, zhigh], up, down)
    lane = lanes_of(MEANS)
    low, own, high = (ref[pl.ds(64, MEANS), :] for ref in (zlow, zown, zhigh))
    value = jnp.zeros((MEANS, LANES), F32)
    for source, shift, first, last in (
        (low, -12, 0, 20),
        (own, 20, 20, 52),
        (high, 52, 52, 72),
        (low, 34, 72, 82),
        (own, 50, 82, 98),
        (high, 66, 98, 108),
    ):
        value = jnp.where((lane >= first) & (lane < last), rolled(source, shift, 1), value)
    gathered[pl.ds(0, MEANS), :] = value
    gathered[pl.ds(MEANS, 4), :] = jnp.zeros((4, LANES), F32)


def fine_y(stat, field, zlow, zhigh, low, high, up, down):
    pack_y(FINE, [stat, field, zlow, zhigh], low, high, up, down)


def z_near(tiles):
    if len(tiles) == 1:
        return [rolled(tiles[0], -1, 1)], [rolled(tiles[0], 1, 1)]
    lane = lanes_of(tiles[0].shape[0])
    ahead = [rolled(t, -1, 1) for t in tiles]
    behind = [rolled(t, 1, 1) for t in tiles]
    last, first = lane == LANES - 1, lane == 0
    plus = [jnp.where(last, ahead[1], ahead[0]), jnp.where(last, ahead[0], ahead[1])]
    minus = [jnp.where(first, behind[1], behind[0]), jnp.where(first, behind[0], behind[1])]
    return plus, minus


def swept(x, value, coef, tiles):
    plus, minus = z_near(value[x])
    out = []
    for t in range(tiles):
        v = value[x][t]
        near = [value[x + 1][t], value[x - 1][t], rolled(v, -1, 0), rolled(v, 1, 0), plus[t], minus[t]]
        terms = [coef(x, k, t) * near[k] for k in range(6)]
        out.append((0.2 * v + coef(x, 6, t)) + (((terms[0] + terms[1]) + (terms[2] + terms[3])) + (terms[4] + terms[5])))
    return out


def side_tile(zlow, zhigh, row, base, width):
    lane = lanes_of(16)
    high = rolled(zhigh[pl.ds(row, 16), :], -base, 1)
    low = rolled(zlow[pl.ds(row, 16), :], -width - base, 1)
    return jnp.where(lane < width, high, jnp.where(lane >= LANES - width, low, F32(0)))


def fine_coef(stat, zlow, zhigh, e):
    cache = {}

    def coef(x, k, t):
        a = 6 * e + k if k < 6 else 18 + e
        if t == 0:
            return stat[pl.ds(((x + 2) * STATIC + a) * 16, 16), :]
        if (x, k) not in cache:
            cache[x, k] = side_tile(zlow, zhigh, (x + 3) * 16, 2 * a, 2)
        return cache[x, k]

    return coef


def fine_sweeps(stat0, field0, zlow0, zhigh0, low, high, below, above, total, coef1, scale1,
                stat, zlow, zhigh, field2, middle, zup, zdown, field, sums):
    grow(FINE, [stat0, field0, zlow0, zhigh0], low, high, below, above, [stat, field, zlow, zhigh])
    for e in range(3):
        coef = fine_coef(stat, zlow, zhigh, e)
        value = {}
        for x in range(-3, 11):
            value[x] = [
                field[pl.ds(((x + 3) * 3 + e) * 16, 16), :],
                side_tile(zlow, zhigh, (x + 3) * 16, 42 + 3 * e, 3),
            ]
        value = {x: swept(x, value, coef, 2) for x in range(-2, 10)}
        value = {x: swept(x, value, coef, 2) for x in range(-1, 9)}
        resid = []
        for x in range(8):
            now = value[x][0]
            field2[pl.ds((x * 3 + e) * 8, 8), :] = now[:8]
            change = swept(x, value, coef, 1)[0] - now
            resid.append(change[:8] * total[pl.ds((x * 3 + e) * 8, 8), :])
        for x in range(4):
            sums[pl.ds((x * 3 + e) * 8, 8), :] = resid[2 * x] + resid[2 * x + 1]
    right = exact_dot(sums[pl.ds(0, 48, 2), :] + sums[pl.ds(1, 48, 2), :], pair_matrix(0.125))
    middle[pl.ds(0, 288), :] = coef1[...]
    middle[pl.ds(288, 48), :] = right * scale1[...]
    lane = lanes_of(48)
    up = jnp.zeros((48, LANES), F32)
    down = jnp.zeros((48, LANES), F32)
    for group in range(7):
        value = middle[pl.ds(48 * group, 48), :]
        inside = (lane >= 4 * group) & (lane < 4 * group + 4)
        up = jnp.where(inside, rolled(value, 4 * group - 60, 1), up)
        down = jnp.where(inside, rolled(value, 4 * group, 1), down)
    zup[pl.ds(64, 48), :] = up
    zdown[pl.ds(64, 48), :] = down
    lane = lanes_of(8)
    for x in range(8):
        up = jnp.zeros((8, LANES), F32)
        down = jnp.zeros((8, LANES), F32)
        for e in range(3):
            value = field2[pl.ds((x * 3 + e) * 8, 8), :]
            inside = (lane >= 2 * e) & (lane < 2 * e + 2)
            up = jnp.where(inside, rolled(value, 2 * e + 2, 1), up)
            down = jnp.where(inside, rolled(value, 2 * e, 1), down)
        zup[pl.ds(x * 8, 8), :] = up
        zdown[pl.ds(x * 8, 8), :] = down


def middle_x(middle, field, zlow, zhigh, coef, right, up, down):
    lane = lanes_of(48)
    low, high = zlow[pl.ds(64, 48), :], zhigh[pl.ds(64, 48), :]
    for group in range(7):
        value = middle[pl.ds(48 * group, 48), :]
        value = jnp.where((lane >= 64) & (lane < 68), rolled(high, 64 - 4 * group, 1), value)
        value = jnp.where(lane >= 124, rolled(low, 124 - 4 * group, 1), value)
        if group < 6:
            coef[pl.ds(48 * group, 48), :] = value
        else:
            right[...] = value
    pack_x(MIDDLE, [coef, right, field, zlow, zhigh], up, down)


def middle_y(coef, right, field, zlow, zhigh, low, high, up, down):
    pack_y(MIDDLE, [coef, right, field, zlow, zhigh], low, high, up, down)


def middle_coef(coef, right, e):
    def get(x, k, t):
        if k < 6:
            return coef[pl.ds(((x + 3) * 18 + 6 * e + k) * 16, 16), :]
        return right[pl.ds(((x + 4) * 3 + e) * 16, 16), :]

    return get


def middle_sweeps(coef0, right0, field0, zlow0, zhigh0, low, high, below, above, total1,
                  coef, right, field, zlow, zhigh, error, coarse, sums):
    grow(MIDDLE, [coef0, right0, field0, zlow0, zhigh0], low, high, below, above, [coef, right, field, zlow, zhigh])
    for e in range(3):
        get = middle_coef(coef, right, e)
        value = {x: [get(x, 6, 0)] for x in range(-4, 8)}
        value = {x: swept(x, value, get, 1) for x in range(-3, 7)}
        for x in range(-3, 7):
            error[pl.ds(((x + 3) * 3 + e) * 16, 16), :] = value[x][0]
        resid = []
        for x in range(4):
            change = swept(x, value, get, 1)[0] - value[x][0]
            resid.append(change[:4] * total1[pl.ds((x * 3 + e) * 4, 4), :])
        for i in range(2):
            sums[pl.ds((i * 3 + e) * 4, 4), :] = resid[2 * i] + resid[2 * i + 1]
    sums[pl.ds(24, 8), :] = jnp.zeros((8, LANES), F32)
    coarse[...] = exact_dot(sums[pl.ds(0, 16, 2), :] + sums[pl.ds(1, 16, 2), :], pair_matrix(0.125))


def spread(coarse, zlow, zhigh, out, wide):
    lane = lanes_of(16)
    value = jnp.where(lane < HALO2, rolled(zlow[...], -12, 1), F32(0))
    value = jnp.where((lane >= 20) & (lane < 52), rolled(coarse[...], 20, 1), value)
    value = jnp.where((lane >= 52) & (lane < 72), rolled(zhigh[...], 52, 1), value)
    wide[...] = value
    lane = lanes_of(8)
    first, second = wide[pl.ds(0, 8), :], wide[pl.ds(6, 8), :]
    block = jnp.where(lane < 64, first, rolled(second, 64, 1))
    tail = jnp.zeros((1, LANES), F32)
    lane = lanes_of(1)
    for row in range(12):
        inside = (lane >= 8 * row) & (lane < 8 * row + 8)
        tail = jnp.where(inside, rolled(wide[pl.ds(row, 1), :], 8 * row - 64, 1), tail)
    rows = lax.broadcasted_iota(jnp.int32, (8, LANES), 0)
    block = jnp.where(rows < 6, block, jnp.where(rows == 6, jnp.broadcast_to(tail, (8, LANES)), F32(0)))
    for copy in range(out.shape[0] // 8):
        out[pl.ds(copy * 8, 8), :] = block


def coarse_levels(gx, gy, me_x, me_y, packed, means, coef, total, coef3, error2, rows6):
    planes = 2 * gx
    lane = lanes_of(gy)
    used = lane < 72
    row = lax.broadcasted_iota(jnp.int32, (gy, LANES), 0)
    first_row, last_row = row == 0, row == gy - 1
    zero = jnp.zeros((gy, LANES), F32)

    def place(x, e, j):
        return (x * 3 + e) * 2 + j

    for g in range(gx):
        blocks = [packed[pl.ds(g * gy * 8 + r, gy, 8), :] for r in range(7)]
        for i in range(2):
            x = 2 * g + i
            for e in range(3):
                for j in range(2):

                    def mean(a):
                        return jnp.where(used, means[pl.ds(g * gy * 88 + i * 42 + a * 2 + j, gy, 88), :], F32(0))

                    w = [mean(6 * e + k) * 0.0625 for k in range(6)]
                    tot = mean(18 + e) + (((w[0] + w[1]) + (w[2] + w[3])) + (w[4] + w[5]))
                    tot = jnp.where(tot > 0, tot, F32(1))
                    inverse = 0.8 / tot
                    r = (i * 3 + e) * 2 + j
                    right = blocks[r] if r < 6 else rolled(blocks[r - 6], 64, 1)
                    right = jnp.where(lane < 64, right, rolled(blocks[6], 64 - 8 * r, 1))
                    right = jnp.where(used, right, F32(0))
                    base = place(x, e, j)
                    for k in range(6):
                        coef[pl.ds((base * 7 + k) * gy, gy), :] = w[k] * inverse
                    coef[pl.ds((base * 7 + 6) * gy, gy), :] = right * inverse
                    total[pl.ds(base * gy, gy), :] = tot * 1.25
        for e in range(3):

            def mean3(a):
                value = rolled(means[pl.ds(g * gy * 88 + a, gy, 88), :], -72, 1)
                return jnp.where(lane < 36, value, F32(0))

            w = [mean3(6 * e + k) * 0.015625 for k in range(6)]
            tot = mean3(18 + e) + (((w[0] + w[1]) + (w[2] + w[3])) + (w[4] + w[5]))
            inverse = 0.8 / jnp.where(tot > 0, tot, F32(1))
            for k in range(6):
                coef3[pl.ds(((g * 3 + e) * 7 + k) * gy, gy), :] = w[k] * inverse
            coef3[pl.ds(((g * 3 + e) * 7 + 6) * gy, gy), :] = inverse

    def sweep2(value, x, e, j):
        base = place(x, e, j)
        v = value[x, j]
        near = [
            value[x + 1, j] if x + 1 < planes else None,
            value[x - 1, j] if x > 0 else None,
            value[x, 1] if j == 0 else jnp.where(last_row, zero, rolled(value[x, 0], -1, 0)),
            value[x, 0] if j == 1 else jnp.where(first_row, zero, rolled(value[x, 1], 1, 0)),
            rolled(v, -1, 1),
            rolled(v, 1, 1),
        ]
        out = 0.2 * v + coef[pl.ds((base * 7 + 6) * gy, gy), :]
        for k in range(6):
            if near[k] is not None:
                out = out + coef[pl.ds((base * 7 + k) * gy, gy), :] * near[k]
        return out

    cells = [(x, j) for x in range(planes) for j in range(2)]
    halve, double = pair_matrix(0.125), None
    fine = lax.broadcasted_iota(jnp.int32, (LANES, LANES), 1)
    coarse = lax.broadcasted_iota(jnp.int32, (LANES, LANES), 0)
    double = jnp.where((fine >> 1) == coarse, F32(1), F32(0))
    for ref in (error2,):
        ref[...] = jnp.zeros(ref.shape, F32)
    before, sums = [], []
    for e in range(3):
        value = {(x, j): coef[pl.ds((place(x, e, j) * 7 + 6) * gy, gy), :] for x, j in cells}
        value = {(x, j): sweep2(value, x, e, j) for x, j in cells}
        before.append(value)
        resid = {
            (x, j): (sweep2(value, x, e, j) - value[x, j]) * total[pl.ds(place(x, e, j) * gy, gy), :] for x, j in cells
        }
        for g in range(gx):
            sums.append(
                (resid[2 * g, 0] + resid[2 * g, 1]) + (resid[2 * g + 1, 0] + resid[2 * g + 1, 1])
            )
    right3 = exact_dot(jnp.concatenate(sums, axis=0), halve)
    found = []
    for e in range(3):

        def coef_of(g, k):
            return coef3[pl.ds(((g * 3 + e) * 7 + k) * gy, gy), :]

        right = [right3[(e * gx + g) * gy : (e * gx + g + 1) * gy] * coef_of(g, 6) for g in range(gx)]
        value = right
        for step in range(7):
            new = []
            for g in range(gx):
                v = value[g]
                out = 0.2 * v + right[g]
                if g + 1 < gx:
                    out = out + coef_of(g, 0) * value[g + 1]
                if g > 0:
                    out = out + coef_of(g, 1) * value[g - 1]
                out = out + coef_of(g, 2) * jnp.where(last_row, zero, rolled(v, -1, 0))
                out = out + coef_of(g, 3) * jnp.where(first_row, zero, rolled(v, 1, 0))
                out = out + coef_of(g, 4) * rolled(v, -1, 1)
                out = out + coef_of(g, 5) * rolled(v, 1, 1)
                new.append(out)
            value = new
        found.extend(value)
    refined = exact_dot(jnp.concatenate(found, axis=0), double)
    for e in range(3):
        value = {
            (x, j): before[e][x, j] + refined[(e * gx + x // 2) * gy : (e * gx + x // 2 + 1) * gy] for x, j in cells
        }
        for step in range(2):
            value = {(x, j): sweep2(value, x, e, j) for x, j in cells}
        for x, j in cells:
            error2[pl.ds(place(x + 2, e, j) * (gy + 16) + 8, gy), :] = value[x, j]
    for plane in range(6):
        for e in range(3):
            for step, j, target in ((0, 0, 0), (0, 1, 1), (1, 0, 2), (1, 1, 3), (-1, 0, 6), (-1, 1, 7)):
                start = (((2 * me_x + plane) * 3 + e) * 2 + j) * (gy + 16) + 8 + me_y + step
                rows6[pl.ds((plane * 3 + e) * 8 + target, 1), :] = error2[pl.ds(start, 1), :]
            rows6[pl.ds((plane * 3 + e) * 8 + 4, 2), :] = jnp.zeros((2, LANES), F32)


def finish(gx, gy, place, packed, means, error1, coef1, right1, stat, zlow0, zhigh0, field2, zlow2, zhigh2, out,
           coef2, total2, coef3, error2, rows6, fine2, rows1, fine1):
    coarse_levels(gx, gy, place[0], place[1], packed, means, coef2, total2, coef3, error2, rows6)

    source = lax.broadcasted_iota(jnp.int32, (LANES, LANES), 0)
    target = lax.broadcasted_iota(jnp.int32, (LANES, LANES), 1)
    cell = jnp.where(target >= 96, target - LANES, target)
    wanted = (cell >= -4) & (cell < 68) & ((cell >> 1) + HALO2 == source)
    widened = exact_dot(rows6[...], jnp.where(wanted, F32(1), F32(0)))
    fine2[pl.ds(0, 144, 2), :] = widened
    fine2[pl.ds(1, 144, 2), :] = widened

    row = lax.broadcasted_iota(jnp.int32, (8, LANES), 0)
    for e in range(3):
        get = middle_coef(coef1, right1, e)
        value = {}
        for x in range(-3, 7):
            value[x] = [
                error1[pl.ds(((x + 3) * 3 + e) * 16, 16), :] + fine2[pl.ds(((x // 2 + 2) * 3 + e) * 16, 16), :]
            ]
        value = {x: swept(x, value, get, 1) for x in range(-2, 6)}
        value = {x: swept(x, value, get, 1) for x in range(-1, 5)}
        for x in range(-1, 5):
            whole = value[x][0]
            rows1[pl.ds(((x + 1) * 3 + e) * 8, 8), :] = jnp.where(row == 7, whole[8:], whole[:8])

    inner = jnp.where((target >> 1) == source, F32(1), F32(0))
    outer = jnp.where((target < 2) & (source == 64), F32(1), F32(0))
    outer = jnp.where((target >= 126) & (source == 127), F32(1), outer)
    for tile, matrix in ((0, inner), (1, outer)):
        widened = exact_dot(rows1[...], matrix)
        fine1[pl.ds(288 * tile, 144, 2), :] = widened
        fine1[pl.ds(288 * tile + 1, 144, 2), :] = widened

    for e in range(3):
        get = fine_coef(stat, zlow0, zhigh0, e)
        value = {}
        for x in range(-2, 10):
            start = ((x // 2 + 1) * 3 + e) * 16
            value[x] = [
                field2[pl.ds(((x + 2) * 3 + e) * 16, 16), :] + fine1[pl.ds(start, 16), :],
                side_tile(zlow2, zhigh2, (x + 2) * 16, 2 * e, 2) + fine1[pl.ds(288 + start, 16), :],
            ]
        value = {x: swept(x, value, get, 2) for x in range(-1, 9)}
        for x in range(8):
            out[e, x] = swept(x, value, get, 1)[0][:8]


def both_ways(axis, up, down):
    devices = lax.axis_size(axis)
    pairs = [(i, i + 1) for i in range(devices - 1)]
    return lax.ppermute(up, axis, pairs), lax.ppermute(down, axis, [(b, a) for a, b in pairs])


def per_device(couplings, diagonal, right_side, guess):
    gx, gy = lax.axis_size("gx"), lax.axis_size("gy")
    place = jnp.stack([lax.axis_index("gx"), lax.axis_index("gy")]).astype(jnp.int32)

    stat, field, total, zup, zdown, coef1, scale1, total1 = call(
        prepare_whole, "prepare", [1344, 192, 192, Z_ROWS, Z_ROWS, 288, 48, 48],
        [couplings, diagonal, right_side, guess], scratch=[672, 336, 168, 88, 48],
    )
    zlow, zhigh = both_ways("gz", zup, zdown)
    xup, xdown, shared = call(
        fine_x, "fine_x", [x_rows(FINE), x_rows(FINE), 88], [stat, field, zlow, zhigh, zup]
    )
    means = lax.all_gather(shared, ("gx", "gy"), tiled=True)
    xlow, xhigh = both_ways("gx", xup, xdown)
    yup, ydown = call(
        fine_y, "fine_y", [y_rows(FINE)] * 2, [stat, field, zlow, zhigh, xlow, xhigh]
    )
    ylow, yhigh = both_ways("gy", yup, ydown)
    stat_grown, zlow_grown, zhigh_grown, field2, middle, zup, zdown = call(
        fine_sweeps, "fine_sweeps",
        [FINE[0].grown_rows(), FINE[2].grown_rows(), FINE[3].grown_rows(), 192, 336, 112, 112],
        [stat, field, zlow, zhigh, xlow, xhigh, ylow, yhigh, total, coef1, scale1],
        scratch=[FINE[1].grown_rows(), 96],
    )

    zlow, zhigh = both_ways("gz", zup, zdown)
    coef1, right1, xup, xdown = call(
        middle_x, "middle_x", [288, 48, x_rows(MIDDLE), x_rows(MIDDLE)], [middle, field2, zlow, zhigh]
    )
    xlow, xhigh = both_ways("gx", xup, xdown)
    yup, ydown = call(
        middle_y, "middle_y", [y_rows(MIDDLE)] * 2, [coef1, right1, field2, zlow, zhigh, xlow, xhigh]
    )
    ylow, yhigh = both_ways("gy", yup, ydown)
    coef1, right1, field2, zlow2, zhigh2, error1, coarse = call(
        middle_sweeps, "middle_sweeps", [s.grown_rows() for s in MIDDLE] + [480, 16],
        [coef1, right1, field2, zlow, zhigh, xlow, xhigh, ylow, yhigh, total1], scratch=[32],
    )

    zlow, zhigh = both_ways("gz", coarse, coarse)
    (packed,) = call(spread, "spread", [gx * gy * 8], [coarse, zlow, zhigh], scratch=[16])
    packed = lax.all_to_all(packed.reshape(gx * gy, 8, LANES), ("gx", "gy"), 0, 0).reshape(gx * gy * 8, LANES)

    vmem = pl.BlockSpec(memory_space=pltpu.VMEM)
    args = [packed, means, error1, coef1, right1, stat_grown, zlow_grown, zhigh_grown, field2, zlow2, zhigh2]
    tiles = 12 * gx * gy
    scratch = [tiles * 7, tiles, gx * 21 * gy, (2 * gx + 4) * 6 * (gy + 16), 144, 288, 144, 576]
    return pl.pallas_call(
        lambda *refs: finish(gx, gy, *refs),
        name="finish",
        out_shape=jax.ShapeDtypeStruct(guess.shape, F32),
        in_specs=[pl.BlockSpec(memory_space=pltpu.SMEM)] + [vmem] * len(args),
        out_specs=vmem,
        scratch_shapes=[pltpu.VMEM((rows, LANES), F32) for rows in scratch],
        compiler_params=pltpu.CompilerParams(vmem_limit_bytes=40 * 1024 * 1024),
    )(place, *args)


def solution(mesh):
    spec = P(None, "gx", "gy", "gz")
    return jax.shard_map(per_device, mesh=mesh, in_specs=(spec,) * 4, out_specs=spec, check_vma=False)
```

```python
import jax
import jax.numpy as jnp
from jax import lax
from jax.experimental import pallas as pl
from jax.experimental.pallas import tpu as pltpu
from jax.sharding import PartitionSpec as P


F32 = jnp.float32
LANES = 128
GRANT = 40 * 1024 * 1024
FAR = 49152
STATIC = 21
HALO2 = 20
SHARED = 64
MEANS = 84


def rolled(value, shift, axis):
    shift %= value.shape[axis]
    return value if shift == 0 else pltpu.roll(value, shift, axis)


def lanes_of(rows):
    return lax.broadcasted_iota(jnp.int32, (rows, LANES), 1)


def pair_matrix(weight):
    fine = lax.broadcasted_iota(jnp.int32, (LANES, LANES), 0)
    coarse = lax.broadcasted_iota(jnp.int32, (LANES, LANES), 1)
    return jnp.where((fine >> 1) == coarse, F32(weight), F32(0))


def exact_dot(left, right):
    return jnp.dot(left, right, precision=lax.Precision.HIGHEST, preferred_element_type=F32)


def call(body, name, outs, args, scratch=(), far_args=(), far_outs=(), copies=0, grant=GRANT):
    vmem = pl.BlockSpec(memory_space=pltpu.VMEM)
    far = pl.BlockSpec(memory_space=pltpu.HBM)
    semaphores = [pltpu.SemaphoreType.DMA((copies,))] if copies else []
    return pl.pallas_call(
        body,
        name=name,
        out_shape=[jax.ShapeDtypeStruct((rows, LANES), F32) for rows in (*outs, *far_outs)],
        in_specs=[far] * len(far_args) + [vmem] * len(args),
        out_specs=[vmem] * len(outs) + [far] * len(far_outs),
        scratch_shapes=[pltpu.VMEM(r if isinstance(r, tuple) else (r, LANES), F32) for r in scratch] + semaphores,
        compiler_params=pltpu.CompilerParams(vmem_limit_bytes=grant),
    )(*far_args, *args)


class Stream:
    def __init__(self, count, rows, planes, halo, reach):
        self.count, self.rows, self.planes, self.halo, self.reach = count, rows, planes, halo, reach

    def extent(self, depth):
        return self.reach - depth

    def halo_rows(self):
        return self.halo * self.count * self.rows

    def grown_rows(self):
        return (self.planes + 2 * self.halo) * self.count * 16


FINE = [Stream(STATIC, 8, 8, 2, 2), Stream(3, 8, 8, 3, 3), Stream(1, 8, 8, 3, 3), Stream(1, 8, 8, 3, 3)]
MIDDLE = [Stream(18, 4, 4, 3, 4), Stream(3, 4, 4, 4, 5), Stream(3, 8, 8, 2, 2), Stream(1, 8, 8, 2, 2), Stream(1, 8, 8, 2, 2)]


def x_rows(streams):
    return sum(s.halo_rows() for s in streams)


def y_pieces(streams):
    offset = 0
    pieces = []
    for depth in range(1, 1 + max(s.halo for s in streams)):
        for index, s in enumerate(streams):
            if depth <= s.halo:
                planes = s.planes + 2 * s.extent(depth)
                pieces.append((index, depth, offset))
                offset += planes * s.count
    return pieces, offset


def y_rows(streams):
    total = y_pieces(streams)[1]
    return -(-total // 8) * 8


def pack_x(streams, mains, up, down):
    offset = 0
    for s, main in zip(streams, mains):
        size = s.halo_rows()
        whole = s.planes * s.count * s.rows
        up[pl.ds(offset, size), :] = main[pl.ds(whole - size, size), :]
        down[pl.ds(offset, size), :] = main[pl.ds(0, size), :]
        offset += size


def pack_y(streams, mains, low, high, up, down):
    starts = [sum(s.halo_rows() for s in streams[:i]) for i in range(len(streams))]
    pieces, total = y_pieces(streams)
    padded = y_rows(streams)
    for out, upward in ((up, True), (down, False)):
        if padded > total:
            out[pl.ds(padded - 8, 8), :] = jnp.zeros((8, LANES), F32)
        for index, depth, offset in pieces:
            s = streams[index]
            row = s.rows - depth if upward else depth - 1
            beyond = s.extent(depth)
            side = beyond * s.count
            middle = s.planes * s.count
            if beyond:
                first = starts[index] + (s.halo - beyond) * s.count * s.rows + row
                out[pl.ds(offset, side), :] = low[pl.ds(first, side, s.rows), :]
            out[pl.ds(offset + side, middle), :] = mains[index][pl.ds(row, middle, s.rows), :]
            if beyond:
                out[pl.ds(offset + side + middle, side), :] = high[pl.ds(starts[index] + row, side, s.rows), :]


def grow(streams, mains, low, high, below, above, grown):
    starts = [sum(s.halo_rows() for s in streams[:i]) for i in range(len(streams))]
    for index, s in enumerate(streams):
        out = grown[index]
        out[...] = jnp.zeros(out.shape, F32)
        edge = s.halo * s.count
        middle = s.planes * s.count
        for source, base, first, number in (
            (low, starts[index], 0, edge),
            (mains[index], 0, edge, middle),
            (high, starts[index], edge + middle, edge),
        ):
            if s.rows == 8:
                for tile in range(number):
                    out[pl.ds((first + tile) * 16, 8), :] = source[pl.ds(base + tile * 8, 8), :]
            else:
                for row in range(s.rows):
                    out[pl.ds(first * 16 + row, number, 16), :] = source[pl.ds(base + row, number, s.rows), :]
    for index, depth, offset in y_pieces(streams)[0]:
        s = streams[index]
        beyond = s.extent(depth)
        number = (s.planes + 2 * beyond) * s.count
        first = (s.halo - beyond) * s.count * 16
        grown[index][pl.ds(first + s.rows + depth - 1, number, 16), :] = above[pl.ds(offset, number), :]
        grown[index][pl.ds(first + 16 - depth, number, 16), :] = below[pl.ds(offset, number), :]


def prepare(c, d, b, g, stat, field, total, zup, zdown, coef1, scale1, total1, summed, means1, half2, sum2, sum3):
    lane = lanes_of(8)
    for x in range(8):
        up = jnp.zeros((8, LANES), F32)
        down = jnp.zeros((8, LANES), F32)
        packed = []
        for e in range(3):
            w = [c[6 * e + k, x] for k in range(6)]
            tot = d[e, x] + (((w[0] + w[1]) + (w[2] + w[3])) + (w[4] + w[5]))
            inverse = 0.8 / tot
            for k in range(6):
                packed.append((6 * e + k, w[k] * inverse))
            packed.append((18 + e, b[e, x] * inverse))
            field[pl.ds((x * 3 + e) * 8, 8), :] = g[e, x]
            total[pl.ds((x * 3 + e) * 8, 8), :] = tot * 1.25
        for a, value in packed:
            stat[pl.ds((x * STATIC + a) * 8, 8), :] = value
            inside = (lane >= 2 * a) & (lane < 2 * a + 2)
            up = jnp.where(inside, rolled(value, 2 * a + 2, 1), up)
            down = jnp.where(inside, rolled(value, 2 * a, 1), down)
        for e in range(3):
            base = 42 + 3 * e
            inside = (lane >= base) & (lane < base + 3)
            up = jnp.where(inside, rolled(g[e, x], base + 3, 1), up)
            down = jnp.where(inside, rolled(g[e, x], base, 1), down)
        zup[pl.ds(x * 8, 8), :] = up
        zdown[pl.ds(x * 8, 8), :] = down

    halve = pair_matrix(0.125)
    for x in range(4):
        for a in range(STATIC):
            one = c[a, 2 * x] + c[a, 2 * x + 1] if a < 18 else d[a - 18, 2 * x] + d[a - 18, 2 * x + 1]
            summed[pl.ds((x * STATIC + a) * 8, 8), :] = one
    means1[...] = exact_dot(summed[pl.ds(0, 336, 2), :] + summed[pl.ds(1, 336, 2), :], halve)
    for x in range(4):
        for e in range(3):
            w = [0.25 * means1[pl.ds((x * STATIC + 6 * e + k) * 4, 4), :] for k in range(6)]
            tot = means1[pl.ds((x * STATIC + 18 + e) * 4, 4), :] + (((w[0] + w[1]) + (w[2] + w[3])) + (w[4] + w[5]))
            tot = jnp.where(tot > 0, tot, F32(1))
            inverse = 0.8 / tot
            for k in range(6):
                coef1[pl.ds((x * 18 + 6 * e + k) * 4, 4), :] = w[k] * inverse
            scale1[pl.ds((x * 3 + e) * 4, 4), :] = inverse
            total1[pl.ds((x * 3 + e) * 4, 4), :] = tot * 1.25
    half2[...] = means1[pl.ds(0, 168, 2), :] + means1[pl.ds(1, 168, 2), :]
    for i in range(2):
        sum2[pl.ds(42 * i, 42), :] = half2[pl.ds(84 * i, 42), :] + half2[pl.ds(84 * i + 42, 42), :]
    sum2[pl.ds(0, MEANS), :] = exact_dot(sum2[...], halve)[:MEANS]
    sum3[pl.ds(0, 42), :] = sum2[pl.ds(0, 42), :] + sum2[pl.ds(42, 42), :]
    sum3[pl.ds(42, 6), :] = jnp.zeros((6, LANES), F32)
    means3 = exact_dot(sum3[pl.ds(0, 24, 2), :] + sum3[pl.ds(1, 24, 2), :], halve)
    sum2[pl.ds(0, STATIC), :] = sum2[pl.ds(0, STATIC), :] + rolled(means3, 32, 1)[:STATIC]
    zup[pl.ds(64, MEANS), :] = sum2[pl.ds(0, MEANS), :]
    zdown[pl.ds(64, MEANS), :] = sum2[pl.ds(0, MEANS), :]


def prepare_whole(c_far, d_far, b_far, g_far, stat, field, total, zup, zdown, coef1, scale1, total1,
                  c, d, b, g, summed, means1, half2, sum2, sum3, arrived):
    copies = [
        pltpu.make_async_copy(far, near, arrived.at[i])
        for i, (far, near) in enumerate(((c_far, c), (d_far, d), (b_far, b), (g_far, g)))
    ]
    for copy in copies:
        copy.start()
    sum2[pl.ds(80, 8), :] = jnp.zeros((8, LANES), F32)
    for out in (zup, zdown):
        out[pl.ds(144, 8), :] = jnp.zeros((8, LANES), F32)
    for copy in copies:
        copy.wait()
    prepare(c, d, b, g, stat, field, total, zup, zdown, coef1, scale1, total1, summed, means1, half2, sum2, sum3)


Z_ROWS = 152


def fine_x(stat, field, zlow, zhigh, up, down):
    pack_x(FINE, [stat, field, zlow, zhigh], up, down)


def share(zlow, zhigh, zown, shared, wide):
    lane = lanes_of(MEANS)
    low, own, high = (ref[pl.ds(64, MEANS), :] for ref in (zlow, zown, zhigh))
    value = jnp.zeros((MEANS, LANES), F32)
    for source, shift, first, last in (
        (low, -12, 0, 20),
        (own, 20, 20, 52),
        (high, 52, 52, 72),
        (low, 34, 72, 82),
        (own, 50, 82, 98),
        (high, 66, 98, 108),
    ):
        value = jnp.where((lane >= first) & (lane < last), rolled(source, shift, 1), value)
    wide[pl.ds(80, 16), :] = jnp.zeros((16, LANES), F32)
    wide[pl.ds(0, MEANS), :] = value
    lane = lanes_of(48)
    body = jnp.where(lane < 64, wide[pl.ds(0, 48), :], rolled(wide[pl.ds(42, 48), :], 64, 1))
    lane = lanes_of(8)
    tail = jnp.zeros((8, LANES), F32)
    third = jnp.zeros((8, LANES), F32)
    for group in range(11):
        value = wide[pl.ds(8 * group, 8), :]
        inside = (lane >= 8 * group) & (lane < 8 * group + 8)
        tail = jnp.where(inside, rolled(value, 8 * group - 64, 1), tail)
        if group < 3:
            inside = (lane >= 36 * group) & (lane < 36 * group + 36)
            third = jnp.where(inside, rolled(value, 36 * group - 72, 1), third)
    shared[pl.ds(0, 48), :] = body
    shared[pl.ds(48, 8), :] = tail
    shared[pl.ds(56, 8), :] = third


def fine_y(stat, field, zlow, zhigh, low, high, up, down):
    pack_y(FINE, [stat, field, zlow, zhigh], low, high, up, down)


def z_near(tiles):
    if len(tiles) == 1:
        return [rolled(tiles[0], -1, 1)], [rolled(tiles[0], 1, 1)]
    lane = lanes_of(tiles[0].shape[0])
    ahead = [rolled(t, -1, 1) for t in tiles]
    behind = [rolled(t, 1, 1) for t in tiles]
    last, first = lane == LANES - 1, lane == 0
    plus = [jnp.where(last, ahead[1], ahead[0]), jnp.where(last, ahead[0], ahead[1])]
    minus = [jnp.where(first, behind[1], behind[0]), jnp.where(first, behind[0], behind[1])]
    return plus, minus


def swept(x, value, coef, tiles):
    plus, minus = z_near(value[x])
    out = []
    for t in range(tiles):
        v = value[x][t]
        near = [value[x + 1][t], value[x - 1][t], rolled(v, -1, 0), rolled(v, 1, 0), plus[t], minus[t]]
        terms = [coef(x, k, t) * near[k] for k in range(6)]
        out.append((0.2 * v + coef(x, 6, t)) + (((terms[0] + terms[1]) + (terms[2] + terms[3])) + (terms[4] + terms[5])))
    return out


def both_sides(zlow, zhigh, sides):
    for tile in range(sides.shape[0] // 16):
        rows = pl.ds(tile * 16, 16)
        sides[rows, :] = jnp.where(lanes_of(16) < 64, zhigh[rows, :], rolled(zlow[rows, :], 64, 1))


def side_tile(sides, row, base, width):
    lane = lanes_of(16)
    packed = sides[pl.ds(row, 16), :]
    high = rolled(packed, -base, 1)
    low = rolled(packed, -width - base - 64, 1)
    return jnp.where(lane < width, high, jnp.where(lane >= LANES - width, low, F32(0)))


def fine_coef(stat, sides, e):
    cache = {}

    def coef(x, k, t):
        a = 6 * e + k if k < 6 else 18 + e
        if t == 0:
            return stat[pl.ds(((x + 2) * STATIC + a) * 16, 16), :]
        if (x, k) not in cache:
            cache[x, k] = side_tile(sides, (x + 3) * 16, 2 * a, 2)
        return cache[x, k]

    return coef


def fine_sweeps(stat0, field0, zlow0, zhigh0, low, high, below, above, total, coef1, scale1,
                sides, field2, middle, zup, zdown, stat_far, stat, field, zlow, zhigh, sums, left):
    grow(FINE, [stat0, field0, zlow0, zhigh0], low, high, below, above, [stat, field, zlow, zhigh])
    keep = pltpu.make_async_copy(stat, stat_far.at[pl.ds(0, stat.shape[0]), :], left.at[0])
    keep.start()
    both_sides(zlow, zhigh, sides)
    for e in range(3):
        coef = fine_coef(stat, sides, e)
        value = {}
        for x in range(-3, 11):
            value[x] = [
                field[pl.ds(((x + 3) * 3 + e) * 16, 16), :],
                side_tile(sides, (x + 3) * 16, 42 + 3 * e, 3),
            ]
        value = {x: swept(x, value, coef, 2) for x in range(-2, 10)}
        value = {x: swept(x, value, coef, 2) for x in range(-1, 9)}
        resid = []
        for x in range(8):
            now = value[x][0]
            field2[pl.ds((x * 3 + e) * 8, 8), :] = now[:8]
            change = swept(x, value, coef, 1)[0] - now
            resid.append(change[:8] * total[pl.ds((x * 3 + e) * 8, 8), :])
        for x in range(4):
            sums[pl.ds((x * 3 + e) * 8, 8), :] = resid[2 * x] + resid[2 * x + 1]
    right = exact_dot(sums[pl.ds(0, 48, 2), :] + sums[pl.ds(1, 48, 2), :], pair_matrix(0.125))
    middle[pl.ds(0, 288), :] = coef1[...]
    middle[pl.ds(288, 48), :] = right * scale1[...]
    lane = lanes_of(48)
    up = jnp.zeros((48, LANES), F32)
    down = jnp.zeros((48, LANES), F32)
    for group in range(7):
        value = middle[pl.ds(48 * group, 48), :]
        inside = (lane >= 4 * group) & (lane < 4 * group + 4)
        up = jnp.where(inside, rolled(value, 4 * group - 60, 1), up)
        down = jnp.where(inside, rolled(value, 4 * group, 1), down)
    zup[pl.ds(64, 48), :] = up
    zdown[pl.ds(64, 48), :] = down
    lane = lanes_of(8)
    for x in range(8):
        up = jnp.zeros((8, LANES), F32)
        down = jnp.zeros((8, LANES), F32)
        for e in range(3):
            value = field2[pl.ds((x * 3 + e) * 8, 8), :]
            inside = (lane >= 2 * e) & (lane < 2 * e + 2)
            up = jnp.where(inside, rolled(value, 2 * e + 2, 1), up)
            down = jnp.where(inside, rolled(value, 2 * e, 1), down)
        zup[pl.ds(x * 8, 8), :] = up
        zdown[pl.ds(x * 8, 8), :] = down
    keep.wait()


def middle_x(middle, field, zlow, zhigh, coef, right, up, down):
    lane = lanes_of(48)
    low, high = zlow[pl.ds(64, 48), :], zhigh[pl.ds(64, 48), :]
    for group in range(7):
        value = middle[pl.ds(48 * group, 48), :]
        value = jnp.where((lane >= 64) & (lane < 68), rolled(high, 64 - 4 * group, 1), value)
        value = jnp.where(lane >= 124, rolled(low, 124 - 4 * group, 1), value)
        if group < 6:
            coef[pl.ds(48 * group, 48), :] = value
        else:
            right[...] = value
    pack_x(MIDDLE, [coef, right, field, zlow, zhigh], up, down)


def middle_y(coef, right, field, zlow, zhigh, low, high, up, down):
    pack_y(MIDDLE, [coef, right, field, zlow, zhigh], low, high, up, down)


def middle_coef(coef, right, e):
    def get(x, k, t):
        if k < 6:
            return coef[pl.ds(((x + 3) * 18 + 6 * e + k) * 16, 16), :]
        return right[pl.ds(((x + 4) * 3 + e) * 16, 16), :]

    return get


def middle_sweeps(coef0, right0, field0, zlow0, zhigh0, low, high, below, above, total1,
                  right, field, sides, error, coarse, coef_far, coef, zlow, zhigh, sums, left):
    grow(MIDDLE, [coef0, right0, field0, zlow0, zhigh0], low, high, below, above, [coef, right, field, zlow, zhigh])
    keep = pltpu.make_async_copy(coef, coef_far.at[pl.ds(0, coef.shape[0]), :], left.at[0])
    keep.start()
    both_sides(zlow, zhigh, sides)
    for e in range(3):
        get = middle_coef(coef, right, e)
        value = {x: [get(x, 6, 0)] for x in range(-4, 8)}
        value = {x: swept(x, value, get, 1) for x in range(-3, 7)}
        for x in range(-3, 7):
            error[pl.ds(((x + 3) * 3 + e) * 16, 16), :] = value[x][0]
        resid = []
        for x in range(4):
            change = swept(x, value, get, 1)[0] - value[x][0]
            resid.append(change[:4] * total1[pl.ds((x * 3 + e) * 4, 4), :])
        for i in range(2):
            sums[pl.ds((i * 3 + e) * 4, 4), :] = resid[2 * i] + resid[2 * i + 1]
    sums[pl.ds(24, 8), :] = jnp.zeros((8, LANES), F32)
    coarse[...] = exact_dot(sums[pl.ds(0, 16, 2), :] + sums[pl.ds(1, 16, 2), :], pair_matrix(0.125))
    keep.wait()


def spread(coarse, zlow, zhigh, out, wide):
    lane = lanes_of(16)
    value = jnp.where(lane < HALO2, rolled(zlow[...], -12, 1), F32(0))
    value = jnp.where((lane >= 20) & (lane < 52), rolled(coarse[...], 20, 1), value)
    value = jnp.where((lane >= 52) & (lane < 72), rolled(zhigh[...], 52, 1), value)
    wide[...] = value
    lane = lanes_of(8)
    first, second = wide[pl.ds(0, 8), :], wide[pl.ds(6, 8), :]
    block = jnp.where(lane < 64, first, rolled(second, 64, 1))
    tail = jnp.zeros((1, LANES), F32)
    lane = lanes_of(1)
    for row in range(12):
        inside = (lane >= 8 * row) & (lane < 8 * row + 8)
        tail = jnp.where(inside, rolled(wide[pl.ds(row, 1), :], 8 * row - 64, 1), tail)
    rows = lax.broadcasted_iota(jnp.int32, (8, LANES), 0)
    block = jnp.where(rows < 6, block, jnp.where(rows == 6, jnp.broadcast_to(tail, (8, LANES)), F32(0)))
    for copy in range(out.shape[0] // 8):
        out[pl.ds(copy * 8, 8), :] = block


def coarse_place(x, e, j):
    return (x * 3 + e) * 2 + j


def coarse_coefs(gx, gy, shared, arrivals, coef, scale, total, coef3):
    lane = lanes_of(gy)
    used = lane < 72
    for g in range(gx):
        arrivals[g].wait()

        def rows(r):
            return shared[pl.ds(g * gy * SHARED + r, gy, SHARED), :]

        tails = [rows(48 + r) for r in range(8)]
        thirds = [rows(56 + r) for r in range(8)]

        def settle(w, d):
            tot = d + (((w[0] + w[1]) + (w[2] + w[3])) + (w[4] + w[5]))
            tot = jnp.where(tot > 0, tot, F32(1))
            return tot, 0.8 / tot

        for e in range(3):
            for j in range(2):
                pairs = {a: rows(a * 2 + j) for a in [6 * e + k for k in range(6)] + [18 + e]}
                for i in range(2):

                    def mean(a):
                        r = i * 42 + a * 2 + j
                        value = pairs[a] if i == 0 else rolled(pairs[a], 64, 1)
                        value = jnp.where(lane < 64, value, rolled(tails[r % 8], 64 - 8 * (r // 8), 1))
                        return jnp.where(used, value, F32(0))

                    w = [mean(6 * e + k) * 0.0625 for k in range(6)]
                    tot, inverse = settle(w, mean(18 + e))
                    base = coarse_place(2 * g + i, e, j)
                    for k in range(6):
                        coef[pl.ds((base * 6 + k) * gy, gy), :] = w[k] * inverse
                    scale[pl.ds(base * gy, gy), :] = inverse
                    total[pl.ds(base * gy, gy), :] = tot * 1.25

            def mean3(a):
                return jnp.where(lane < 36, rolled(thirds[a % 8], -36 * (a // 8), 1), F32(0))

            w = [mean3(6 * e + k) * 0.015625 for k in range(6)]
            tot, inverse = settle(w, mean3(18 + e))
            for k in range(6):
                coef3[pl.ds(((g * 3 + e) * 7 + k) * gy, gy), :] = w[k] * inverse
            coef3[pl.ds(((g * 3 + e) * 7 + 6) * gy, gy), :] = inverse


def coarse_levels(gx, gy, me_x, me_y, packed, coef, scale, total, coef3, right2, error2, rows6):
    planes = 2 * gx
    place = coarse_place
    lane = lanes_of(gy)
    used = lane < 72
    row = lax.broadcasted_iota(jnp.int32, (gy, LANES), 0)
    first_row, last_row = row == 0, row == gy - 1
    zero = jnp.zeros((gy, LANES), F32)

    for g in range(gx):
        blocks = [packed[pl.ds(g * gy * 8 + r, gy, 8), :] for r in range(7)]
        for i in range(2):
            for e in range(3):
                for j in range(2):
                    r = (i * 3 + e) * 2 + j
                    right = blocks[r] if r < 6 else rolled(blocks[r - 6], 64, 1)
                    right = jnp.where(lane < 64, right, rolled(blocks[6], 64 - 8 * r, 1))
                    base = place(2 * g + i, e, j) * gy
                    right2[pl.ds(base, gy), :] = jnp.where(used, right, F32(0)) * scale[pl.ds(base, gy), :]

    def sweep2(value, x, e, j):
        base = place(x, e, j)
        v = value[x, j]
        near = [
            value[x + 1, j] if x + 1 < planes else None,
            value[x - 1, j] if x > 0 else None,
            value[x, 1] if j == 0 else jnp.where(last_row, zero, rolled(value[x, 0], -1, 0)),
            value[x, 0] if j == 1 else jnp.where(first_row, zero, rolled(value[x, 1], 1, 0)),
            rolled(v, -1, 1),
            rolled(v, 1, 1),
        ]
        out = 0.2 * v + right2[pl.ds(base * gy, gy), :]
        for k in range(6):
            if near[k] is not None:
                out = out + coef[pl.ds((base * 6 + k) * gy, gy), :] * near[k]
        return out

    cells = [(x, j) for x in range(planes) for j in range(2)]
    halve = pair_matrix(0.125)
    fine = lax.broadcasted_iota(jnp.int32, (LANES, LANES), 1)
    coarse = lax.broadcasted_iota(jnp.int32, (LANES, LANES), 0)
    double = jnp.where((fine >> 1) == coarse, F32(1), F32(0))
    error2[...] = jnp.zeros(error2.shape, F32)
    before, sums = [], []
    for e in range(3):
        value = {(x, j): right2[pl.ds(place(x, e, j) * gy, gy), :] for x, j in cells}
        value = {(x, j): sweep2(value, x, e, j) for x, j in cells}
        before.append(value)
        resid = {
            (x, j): (sweep2(value, x, e, j) - value[x, j]) * total[pl.ds(place(x, e, j) * gy, gy), :] for x, j in cells
        }
        for g in range(gx):
            sums.append(
                (resid[2 * g, 0] + resid[2 * g, 1]) + (resid[2 * g + 1, 0] + resid[2 * g + 1, 1])
            )
    right3 = exact_dot(jnp.concatenate(sums, axis=0), halve)
    found = []
    for e in range(3):

        def coef_of(g, k):
            return coef3[pl.ds(((g * 3 + e) * 7 + k) * gy, gy), :]

        right = [right3[(e * gx + g) * gy : (e * gx + g + 1) * gy] * coef_of(g, 6) for g in range(gx)]
        value = right
        for step in range(7):
            new = []
            for g in range(gx):
                v = value[g]
                out = 0.2 * v + right[g]
                if g + 1 < gx:
                    out = out + coef_of(g, 0) * value[g + 1]
                if g > 0:
                    out = out + coef_of(g, 1) * value[g - 1]
                out = out + coef_of(g, 2) * jnp.where(last_row, zero, rolled(v, -1, 0))
                out = out + coef_of(g, 3) * jnp.where(first_row, zero, rolled(v, 1, 0))
                out = out + coef_of(g, 4) * rolled(v, -1, 1)
                out = out + coef_of(g, 5) * rolled(v, 1, 1)
                new.append(out)
            value = new
        found.extend(value)
    refined = exact_dot(jnp.concatenate(found, axis=0), double)
    for e in range(3):
        value = {
            (x, j): before[e][x, j] + refined[(e * gx + x // 2) * gy : (e * gx + x // 2 + 1) * gy] for x, j in cells
        }
        for step in range(2):
            value = {(x, j): sweep2(value, x, e, j) for x, j in cells}
        for x, j in cells:
            error2[pl.ds(place(x + 2, e, j) * (gy + 16) + 8, gy), :] = value[x, j]
    for plane in range(6):
        for e in range(3):
            for step, j, target in ((0, 0, 0), (0, 1, 1), (1, 0, 2), (1, 1, 3), (-1, 0, 6), (-1, 1, 7)):
                start = (((2 * me_x + plane) * 3 + e) * 2 + j) * (gy + 16) + 8 + me_y + step
                rows6[pl.ds((plane * 3 + e) * 8 + target, 1), :] = error2[pl.ds(start, 1), :]
            rows6[pl.ds((plane * 3 + e) * 8 + 4, 2), :] = jnp.zeros((2, LANES), F32)


def finish(gx, gy, shared_far, coef1_far, stat_far, packed, error1, right1, sides0, field2, sides2, out,
           shared, coef1, stat, coef2, scale2, total2, coef3, right2, error2, rows6, fine2, rows1, fine1, arrived):
    chunk = gy * SHARED
    arrivals = [
        pltpu.make_async_copy(shared_far.at[pl.ds(g * chunk, chunk), :], shared.at[pl.ds(g * chunk, chunk), :], arrived.at[g])
        for g in range(gx)
    ]
    later = [
        pltpu.make_async_copy(coef1_far.at[pl.ds(0, coef1.shape[0]), :], coef1, arrived.at[gx]),
        pltpu.make_async_copy(stat_far.at[pl.ds(0, stat.shape[0]), :], stat, arrived.at[gx + 1]),
    ]
    for copy in arrivals + later:
        copy.start()
    coarse_coefs(gx, gy, shared, arrivals, coef2, scale2, total2, coef3)
    me_x, me_y = lax.axis_index("gx"), lax.axis_index("gy")
    coarse_levels(gx, gy, me_x, me_y, packed, coef2, scale2, total2, coef3, right2, error2, rows6)
    for copy in later:
        copy.wait()

    source = lax.broadcasted_iota(jnp.int32, (LANES, LANES), 0)
    target = lax.broadcasted_iota(jnp.int32, (LANES, LANES), 1)
    cell = jnp.where(target >= 96, target - LANES, target)
    wanted = (cell >= -4) & (cell < 68) & ((cell >> 1) + HALO2 == source)
    widened = exact_dot(rows6[...], jnp.where(wanted, F32(1), F32(0)))
    fine2[pl.ds(0, 144, 2), :] = widened
    fine2[pl.ds(1, 144, 2), :] = widened

    row = lax.broadcasted_iota(jnp.int32, (8, LANES), 0)
    for e in range(3):
        get = middle_coef(coef1, right1, e)
        value = {}
        for x in range(-3, 7):
            value[x] = [
                error1[pl.ds(((x + 3) * 3 + e) * 16, 16), :] + fine2[pl.ds(((x // 2 + 2) * 3 + e) * 16, 16), :]
            ]
        value = {x: swept(x, value, get, 1) for x in range(-2, 6)}
        value = {x: swept(x, value, get, 1) for x in range(-1, 5)}
        for x in range(-1, 5):
            whole = value[x][0]
            rows1[pl.ds(((x + 1) * 3 + e) * 8, 8), :] = jnp.where(row == 7, whole[8:], whole[:8])

    inner = jnp.where((target >> 1) == source, F32(1), F32(0))
    outer = jnp.where((target < 2) & (source == 64), F32(1), F32(0))
    outer = jnp.where((target >= 126) & (source == 127), F32(1), outer)
    for tile, matrix in ((0, inner), (1, outer)):
        widened = exact_dot(rows1[...], matrix)
        fine1[pl.ds(288 * tile, 144, 2), :] = widened
        fine1[pl.ds(288 * tile + 1, 144, 2), :] = widened

    for e in range(3):
        get = fine_coef(stat, sides0, e)
        value = {}
        for x in range(-2, 10):
            start = ((x // 2 + 1) * 3 + e) * 16
            value[x] = [
                field2[pl.ds(((x + 2) * 3 + e) * 16, 16), :] + fine1[pl.ds(start, 16), :],
                side_tile(sides2, (x + 2) * 16, 2 * e, 2) + fine1[pl.ds(288 + start, 16), :],
            ]
        value = {x: swept(x, value, get, 2) for x in range(-1, 9)}
        for x in range(8):
            out[e, x] = swept(x, value, get, 1)[0][:8]


def both_ways(axis, up, down):
    devices = lax.axis_size(axis)
    pairs = [(i, i + 1) for i in range(devices - 1)]
    return lax.ppermute(up, axis, pairs), lax.ppermute(down, axis, [(b, a) for a, b in pairs])


def to_all(value, devices):
    blocks = value.reshape(devices, value.shape[0] // devices, LANES)
    return lax.all_to_all(blocks, ("gx", "gy"), 0, 0).reshape(value.shape)


def per_device(couplings, diagonal, right_side, guess):
    gx, gy = lax.axis_size("gx"), lax.axis_size("gy")
    inputs = (couplings, diagonal, right_side, guess)

    stat, field, total, zup, zdown, coef1, scale1, total1 = call(
        prepare_whole, "prepare", [1344, 192, 192, Z_ROWS, Z_ROWS, 288, 48, 48], [], far_args=inputs,
        scratch=[value.shape for value in inputs] + [672, 336, 168, 88, 48], copies=4,
    )
    zlow, zhigh = both_ways("gz", zup, zdown)
    xup, xdown = call(fine_x, "fine_x", [x_rows(FINE)] * 2, [stat, field, zlow, zhigh])
    (shared,) = call(share, "share", [SHARED], [zlow, zhigh, zup], scratch=[96])
    shared = to_all(jnp.broadcast_to(shared[None], (gx * gy, SHARED, LANES)).reshape(-1, LANES), gx * gy)
    xlow, xhigh = both_ways("gx", xup, xdown)
    yup, ydown = call(fine_y, "fine_y", [y_rows(FINE)] * 2, [stat, field, zlow, zhigh, xlow, xhigh])
    ylow, yhigh = both_ways("gy", yup, ydown)
    sides0, field2, middle, zup, zdown, stat = call(
        fine_sweeps, "fine_sweeps", [FINE[2].grown_rows(), 192, 336, 112, 112],
        [stat, field, zlow, zhigh, xlow, xhigh, ylow, yhigh, total, coef1, scale1],
        far_outs=[FAR], scratch=[s.grown_rows() for s in FINE] + [96], copies=1,
    )

    zlow, zhigh = both_ways("gz", zup, zdown)
    coef1, right1, xup, xdown = call(
        middle_x, "middle_x", [288, 48, x_rows(MIDDLE), x_rows(MIDDLE)], [middle, field2, zlow, zhigh]
    )
    xlow, xhigh = both_ways("gx", xup, xdown)
    yup, ydown = call(
        middle_y, "middle_y", [y_rows(MIDDLE)] * 2, [coef1, right1, field2, zlow, zhigh, xlow, xhigh]
    )
    ylow, yhigh = both_ways("gy", yup, ydown)
    right1, field2, sides2, error1, coarse, coef1 = call(
        middle_sweeps, "middle_sweeps", [s.grown_rows() for s in MIDDLE[1:4]] + [480, 16],
        [coef1, right1, field2, zlow, zhigh, xlow, xhigh, ylow, yhigh, total1],
        far_outs=[FAR], scratch=[MIDDLE[i].grown_rows() for i in (0, 3, 4)] + [32], copies=1,
    )

    zlow, zhigh = both_ways("gz", coarse, coarse)
    (packed,) = call(spread, "spread", [gx * gy * 8], [coarse, zlow, zhigh], scratch=[16])
    packed, shared = lax.optimization_barrier((packed, shared))
    packed = to_all(packed, gx * gy)

    tiles = 12 * gx * gy
    vmem = pl.BlockSpec(memory_space=pltpu.VMEM)
    far = pl.BlockSpec(memory_space=pltpu.HBM)
    near = [packed, error1, right1, sides0, field2, sides2]
    scratch = [gx * gy * SHARED, MIDDLE[0].grown_rows(), FINE[0].grown_rows(), tiles * 6, tiles, tiles, gx * 21 * gy]
    scratch += [tiles, (2 * gx + 4) * 6 * (gy + 16), 144, 288, 144, 576]
    return pl.pallas_call(
        lambda *refs: finish(gx, gy, *refs),
        name="finish",
        out_shape=jax.ShapeDtypeStruct(guess.shape, F32),
        in_specs=[far] * 3 + [vmem] * len(near),
        out_specs=vmem,
        scratch_shapes=[pltpu.VMEM((rows, LANES), F32) for rows in scratch] + [pltpu.SemaphoreType.DMA((gx + 2,))],
        compiler_params=pltpu.CompilerParams(vmem_limit_bytes=GRANT),
    )(shared, coef1, stat, *near)


def solution(mesh):
    spec = P(None, "gx", "gy", "gz")
    return jax.shard_map(per_device, mesh=mesh, in_specs=(spec,) * 4, out_specs=spec, check_vma=False)
```

```python
import jax
import jax.numpy as jnp
from jax import lax
from jax.experimental import pallas as pl
from jax.experimental.pallas import tpu as pltpu
from jax.sharding import PartitionSpec as P


F32 = jnp.float32
LANES = 128
GRANT = 40 * 1024 * 1024
FAR = 49152
STATIC = 21
WIDE = 42
HALO2 = 20
SHARED = 64
MEANS = 84


def rolled(value, shift, axis):
    shift %= value.shape[axis]
    return value if shift == 0 else pltpu.roll(value, shift, axis)


def lanes_of(rows):
    return lax.broadcasted_iota(jnp.int32, (rows, LANES), 1)


def pair_matrix(weight):
    fine = lax.broadcasted_iota(jnp.int32, (LANES, LANES), 0)
    coarse = lax.broadcasted_iota(jnp.int32, (LANES, LANES), 1)
    return jnp.where((fine >> 1) == coarse, F32(weight), F32(0))


def exact_dot(left, right):
    return jnp.dot(left, right, precision=lax.Precision.HIGHEST, preferred_element_type=F32)


def call(body, name, outs, args, scratch=(), far_args=(), far_outs=(), copies=0, grant=GRANT):
    vmem = pl.BlockSpec(memory_space=pltpu.VMEM)
    far = pl.BlockSpec(memory_space=pltpu.HBM)
    semaphores = [pltpu.SemaphoreType.DMA((copies,))] if copies else []
    return pl.pallas_call(
        body,
        name=name,
        out_shape=[jax.ShapeDtypeStruct((rows, LANES), F32) for rows in (*outs, *far_outs)],
        in_specs=[far] * len(far_args) + [vmem] * len(args),
        out_specs=[vmem] * len(outs) + [far] * len(far_outs),
        scratch_shapes=[pltpu.VMEM(r if isinstance(r, tuple) else (r, LANES), F32) for r in scratch] + semaphores,
        compiler_params=pltpu.CompilerParams(vmem_limit_bytes=grant),
    )(*far_args, *args)


class Stream:
    def __init__(self, count, rows, planes, halo, reach):
        self.count, self.rows, self.planes, self.halo, self.reach = count, rows, planes, halo, reach

    def extent(self, depth):
        return self.reach - depth

    def halo_rows(self):
        return self.halo * self.count * self.rows

    def grown_rows(self):
        return (self.planes + 2 * self.halo) * self.count * 16


FINE = [Stream(STATIC, 8, 8, 2, 2), Stream(3, 8, 8, 3, 3), Stream(1, 8, 8, 3, 3), Stream(1, 8, 8, 3, 3)]
MIDDLE = [Stream(18, 4, 4, 3, 4), Stream(3, 4, 4, 4, 5), Stream(3, 8, 8, 2, 2), Stream(1, 8, 8, 2, 2), Stream(1, 8, 8, 2, 2)]
MIDDLE += [Stream(18, 4, 4, 1, 1), Stream(3, 4, 4, 2, 2)]


def x_rows(streams):
    return sum(s.halo_rows() for s in streams)


def y_pieces(streams):
    offset = 0
    pieces = []
    for depth in range(1, 1 + max(s.halo for s in streams)):
        for index, s in enumerate(streams):
            if depth <= s.halo:
                planes = s.planes + 2 * s.extent(depth)
                pieces.append((index, depth, offset))
                offset += planes * s.count
    return pieces, offset


def y_rows(streams):
    total = y_pieces(streams)[1]
    return -(-total // 8) * 8


def pack_x(streams, mains, up, down):
    offset = 0
    for s, main in zip(streams, mains):
        size = s.halo_rows()
        whole = s.planes * s.count * s.rows
        up[pl.ds(offset, size), :] = main[pl.ds(whole - size, size), :]
        down[pl.ds(offset, size), :] = main[pl.ds(0, size), :]
        offset += size


def pack_y(streams, mains, low, high, up, down):
    starts = [sum(s.halo_rows() for s in streams[:i]) for i in range(len(streams))]
    pieces, total = y_pieces(streams)
    padded = y_rows(streams)
    for out, upward in ((up, True), (down, False)):
        if padded > total:
            out[pl.ds(padded - 8, 8), :] = jnp.zeros((8, LANES), F32)
        for index, depth, offset in pieces:
            s = streams[index]
            row = s.rows - depth if upward else depth - 1
            beyond = s.extent(depth)
            side = beyond * s.count
            middle = s.planes * s.count
            if beyond:
                first = starts[index] + (s.halo - beyond) * s.count * s.rows + row
                out[pl.ds(offset, side), :] = low[pl.ds(first, side, s.rows), :]
            out[pl.ds(offset + side, middle), :] = mains[index][pl.ds(row, middle, s.rows), :]
            if beyond:
                out[pl.ds(offset + side + middle, side), :] = high[pl.ds(starts[index] + row, side, s.rows), :]


def grow(streams, mains, low, high, below, above, grown):
    starts = [sum(s.halo_rows() for s in streams[:i]) for i in range(len(streams))]
    for index, s in enumerate(streams):
        out = grown[index]
        out[...] = jnp.zeros(out.shape, F32)
        edge = s.halo * s.count
        middle = s.planes * s.count
        for source, base, first, number in (
            (low, starts[index], 0, edge),
            (mains[index], 0, edge, middle),
            (high, starts[index], edge + middle, edge),
        ):
            if s.rows == 8:
                for tile in range(number):
                    out[pl.ds((first + tile) * 16, 8), :] = source[pl.ds(base + tile * 8, 8), :]
            else:
                for row in range(s.rows):
                    out[pl.ds(first * 16 + row, number, 16), :] = source[pl.ds(base + row, number, s.rows), :]
    for index, depth, offset in y_pieces(streams)[0]:
        s = streams[index]
        beyond = s.extent(depth)
        number = (s.planes + 2 * beyond) * s.count
        first = (s.halo - beyond) * s.count * 16
        grown[index][pl.ds(first + s.rows + depth - 1, number, 16), :] = above[pl.ds(offset, number), :]
        grown[index][pl.ds(first + 16 - depth, number, 16), :] = below[pl.ds(offset, number), :]


def prepare(c, d, b, g, stat, field, total, zup, zdown, coef1, scale1, total1, summed, means1, half2, sum2, sum3):
    lane = lanes_of(8)
    for x in range(8):
        up = jnp.zeros((8, LANES), F32)
        down = jnp.zeros((8, LANES), F32)
        packed = []
        for e in range(3):
            w = [c[6 * e + k, x] for k in range(6)]
            tot = d[e, x] + (((w[0] + w[1]) + (w[2] + w[3])) + (w[4] + w[5]))
            inverse = 0.8 / tot
            for k in range(6):
                packed.append((6 * e + k, w[k] * inverse))
            packed.append((18 + e, b[e, x] * inverse))
            field[pl.ds((x * 3 + e) * 8, 8), :] = g[e, x]
            total[pl.ds((x * 3 + e) * 8, 8), :] = tot * 1.25
        for a, value in packed:
            stat[pl.ds((x * STATIC + a) * 8, 8), :] = value
            inside = (lane >= 2 * a) & (lane < 2 * a + 2)
            up = jnp.where(inside, rolled(value, 2 * a + 2, 1), up)
            down = jnp.where(inside, rolled(value, 2 * a, 1), down)
        for e in range(3):
            base = 42 + 3 * e
            inside = (lane >= base) & (lane < base + 3)
            up = jnp.where(inside, rolled(g[e, x], base + 3, 1), up)
            down = jnp.where(inside, rolled(g[e, x], base, 1), down)
        zup[pl.ds(x * 8, 8), :] = up
        zdown[pl.ds(x * 8, 8), :] = down

    halve = pair_matrix(0.125)
    for x in range(4):
        for a in range(STATIC):
            one = c[a, 2 * x] + c[a, 2 * x + 1] if a < 18 else d[a - 18, 2 * x] + d[a - 18, 2 * x + 1]
            summed[pl.ds((x * STATIC + a) * 8, 8), :] = one
    means1[...] = exact_dot(summed[pl.ds(0, 336, 2), :] + summed[pl.ds(1, 336, 2), :], halve)
    for x in range(4):
        for e in range(3):
            w = [0.25 * means1[pl.ds((x * STATIC + 6 * e + k) * 4, 4), :] for k in range(6)]
            tot = means1[pl.ds((x * STATIC + 18 + e) * 4, 4), :] + (((w[0] + w[1]) + (w[2] + w[3])) + (w[4] + w[5]))
            tot = jnp.where(tot > 0, tot, F32(1))
            inverse = 0.8 / tot
            for k in range(6):
                coef1[pl.ds((x * 18 + 6 * e + k) * 4, 4), :] = w[k] * inverse
            scale1[pl.ds((x * 3 + e) * 4, 4), :] = inverse
            total1[pl.ds((x * 3 + e) * 4, 4), :] = tot * 1.25
    half2[...] = means1[pl.ds(0, 168, 2), :] + means1[pl.ds(1, 168, 2), :]
    for i in range(2):
        sum2[pl.ds(42 * i, 42), :] = half2[pl.ds(84 * i, 42), :] + half2[pl.ds(84 * i + 42, 42), :]
    sum2[pl.ds(0, MEANS), :] = exact_dot(sum2[...], halve)[:MEANS]
    sum3[pl.ds(0, 42), :] = sum2[pl.ds(0, 42), :] + sum2[pl.ds(42, 42), :]
    sum3[pl.ds(42, 6), :] = jnp.zeros((6, LANES), F32)
    means3 = exact_dot(sum3[pl.ds(0, 24, 2), :] + sum3[pl.ds(1, 24, 2), :], halve)
    sum2[pl.ds(0, STATIC), :] = sum2[pl.ds(0, STATIC), :] + rolled(means3, 32, 1)[:STATIC]
    zup[pl.ds(64, MEANS), :] = sum2[pl.ds(0, MEANS), :]
    zdown[pl.ds(64, MEANS), :] = sum2[pl.ds(0, MEANS), :]


def prepare_whole(c_far, d_far, b_far, g_far, stat, field, total, zup, zdown, coef1, scale1, total1,
                  c, d, b, g, summed, means1, half2, sum2, sum3, arrived):
    copies = [
        pltpu.make_async_copy(far, near, arrived.at[i])
        for i, (far, near) in enumerate(((c_far, c), (d_far, d), (b_far, b), (g_far, g)))
    ]
    for copy in copies:
        copy.start()
    sum2[pl.ds(80, 8), :] = jnp.zeros((8, LANES), F32)
    for out in (zup, zdown):
        out[pl.ds(144, 8), :] = jnp.zeros((8, LANES), F32)
    for copy in copies:
        copy.wait()
    prepare(c, d, b, g, stat, field, total, zup, zdown, coef1, scale1, total1, summed, means1, half2, sum2, sum3)


Z_ROWS = 152


def fine_x(stat, field, zlow, zhigh, up, down):
    pack_x(FINE, [stat, field, zlow, zhigh], up, down)


def share(zlow, zhigh, zown, shared, wide):
    lane = lanes_of(MEANS)
    low, own, high = (ref[pl.ds(64, MEANS), :] for ref in (zlow, zown, zhigh))
    value = jnp.zeros((MEANS, LANES), F32)
    for source, shift, first, last in (
        (low, -12, 0, 20),
        (own, 20, 20, 52),
        (high, 52, 52, 72),
        (low, 34, 72, 82),
        (own, 50, 82, 98),
        (high, 66, 98, 108),
    ):
        value = jnp.where((lane >= first) & (lane < last), rolled(source, shift, 1), value)
    wide[pl.ds(80, 16), :] = jnp.zeros((16, LANES), F32)
    wide[pl.ds(0, MEANS), :] = value
    lane = lanes_of(48)
    body = jnp.where(lane < 64, wide[pl.ds(0, 48), :], rolled(wide[pl.ds(42, 48), :], 64, 1))
    lane = lanes_of(8)
    tail = jnp.zeros((8, LANES), F32)
    third = jnp.zeros((8, LANES), F32)
    for group in range(11):
        value = wide[pl.ds(8 * group, 8), :]
        inside = (lane >= 8 * group) & (lane < 8 * group + 8)
        tail = jnp.where(inside, rolled(value, 8 * group - 64, 1), tail)
        if group < 3:
            inside = (lane >= 36 * group) & (lane < 36 * group + 36)
            third = jnp.where(inside, rolled(value, 36 * group - 72, 1), third)
    shared[pl.ds(0, 48), :] = body
    shared[pl.ds(48, 8), :] = tail
    shared[pl.ds(56, 8), :] = third


def fine_y(stat, field, zlow, zhigh, low, high, up, down):
    pack_y(FINE, [stat, field, zlow, zhigh], low, high, up, down)


def z_near(tiles):
    if len(tiles) == 1:
        return [rolled(tiles[0], -1, 1)], [rolled(tiles[0], 1, 1)]
    lane = lanes_of(tiles[0].shape[0])
    ahead = [rolled(t, -1, 1) for t in tiles]
    behind = [rolled(t, 1, 1) for t in tiles]
    last, first = lane == LANES - 1, lane == 0
    plus = [jnp.where(last, ahead[1], ahead[0]), jnp.where(last, ahead[0], ahead[1])]
    minus = [jnp.where(first, behind[1], behind[0]), jnp.where(first, behind[0], behind[1])]
    return plus, minus


def swept(x, value, coef, tiles):
    plus, minus = z_near(value[x])
    out = []
    for t in range(tiles):
        v = value[x][t]
        near = [value[x + 1][t], value[x - 1][t], rolled(v, -1, 0), rolled(v, 1, 0), plus[t], minus[t]]
        terms = [coef(x, k, t) * near[k] for k in range(6)]
        out.append((0.2 * v + coef(x, 6, t)) + (((terms[0] + terms[1]) + (terms[2] + terms[3])) + (terms[4] + terms[5])))
    return out


def both_sides(zlow, zhigh, sides):
    for tile in range(sides.shape[0] // 16):
        rows = pl.ds(tile * 16, 16)
        sides[rows, :] = jnp.where(lanes_of(16) < 64, zhigh[rows, :], rolled(zlow[rows, :], 64, 1))


def side_tile(sides, row, base, width):
    lane = lanes_of(16)
    packed = sides[pl.ds(row, 16), :]
    high = rolled(packed, -base, 1)
    low = rolled(packed, -width - base - 64, 1)
    return jnp.where(lane < width, high, jnp.where(lane >= LANES - width, low, F32(0)))


def fine_coef(stat, sides, e):
    cache = {}

    def coef(x, k, t):
        a = 6 * e + k if k < 6 else 18 + e
        if t == 0:
            return stat[pl.ds(((x + 2) * STATIC + a) * 16, 16), :]
        if (x, k) not in cache:
            cache[x, k] = side_tile(sides, (x + 3) * 16, 2 * a, 2)
        return cache[x, k]

    return coef


def fine_sweeps(stat0, field0, zlow0, zhigh0, low, high, below, above, total, coef1, scale1, total1,
                stat, sides, field2, middle, zup, zdown, field, zlow, zhigh, sums):
    grow(FINE, [stat0, field0, zlow0, zhigh0], low, high, below, above, [stat, field, zlow, zhigh])
    both_sides(zlow, zhigh, sides)
    for e in range(3):
        coef = fine_coef(stat, sides, e)
        value = {}
        for x in range(-3, 11):
            value[x] = [
                field[pl.ds(((x + 3) * 3 + e) * 16, 16), :],
                side_tile(sides, (x + 3) * 16, 42 + 3 * e, 3),
            ]
        value = {x: swept(x, value, coef, 2) for x in range(-2, 10)}
        value = {x: swept(x, value, coef, 2) for x in range(-1, 9)}
        resid = []
        for x in range(8):
            now = value[x][0]
            field2[pl.ds((x * 3 + e) * 8, 8), :] = now[:8]
            change = swept(x, value, coef, 1)[0] - now
            resid.append(change[:8] * total[pl.ds((x * 3 + e) * 8, 8), :])
        for x in range(4):
            sums[pl.ds((x * 3 + e) * 8, 8), :] = resid[2 * x] + resid[2 * x + 1]
    right = exact_dot(sums[pl.ds(0, 48, 2), :] + sums[pl.ds(1, 48, 2), :], pair_matrix(0.125))
    middle[pl.ds(0, 288), :] = coef1[...]
    middle[pl.ds(288, 48), :] = right * scale1[...]
    middle[pl.ds(336, 48), :] = total1[...]
    lane = lanes_of(128)
    up = jnp.zeros((128, LANES), F32)
    down = jnp.zeros((128, LANES), F32)
    for group in range(3):
        value = middle[pl.ds(128 * group, 128), :]
        inside = (lane >= WIDE * group) & (lane < WIDE * group + WIDE)
        up = jnp.where(inside, rolled(value, WIDE * group + WIDE - 64, 1), up)
        down = jnp.where(inside, rolled(value, WIDE * group, 1), down)
    zup[pl.ds(64, 128), :] = up
    zdown[pl.ds(64, 128), :] = down
    lane = lanes_of(8)
    for x in range(8):
        up = jnp.zeros((8, LANES), F32)
        down = jnp.zeros((8, LANES), F32)
        for e in range(3):
            value = field2[pl.ds((x * 3 + e) * 8, 8), :]
            inside = (lane >= 2 * e) & (lane < 2 * e + 2)
            up = jnp.where(inside, rolled(value, 2 * e + 2, 1), up)
            down = jnp.where(inside, rolled(value, 2 * e, 1), down)
        zup[pl.ds(x * 8, 8), :] = up
        zdown[pl.ds(x * 8, 8), :] = down


def middle_x(middle, field, zlow, zhigh, coef, right, side_coef, side_right, side_total, up, down):
    lane = lanes_of(128)
    low, high = zlow[pl.ds(64, 128), :], zhigh[pl.ds(64, 128), :]
    for group in range(3):
        own = middle[pl.ds(128 * group, 128), :]
        main = jnp.where((lane >= 64) & (lane < 68), rolled(high, 64 - WIDE * group, 1), own)
        main = jnp.where(lane >= 124, rolled(low, 128 - WIDE - WIDE * group, 1), main)
        side = jnp.where(lane < 2, rolled(own, -62, 1), F32(0))
        side = jnp.where((lane >= 2) & (lane < 2 + WIDE), rolled(high, 2 - WIDE * group, 1), side)
        side = jnp.where((lane >= 64) & (lane < 64 + WIDE), rolled(low, 64 - WIDE * group, 1), side)
        side = jnp.where((lane >= 106) & (lane < 108), rolled(own, 106, 1), side)
        if group < 2:
            coef[pl.ds(128 * group, 128), :] = main
            side_coef[pl.ds(128 * group, 128), :] = side
        else:
            coef[pl.ds(256, 32), :] = main[:32]
            side_coef[pl.ds(256, 32), :] = side[:32]
            right[...] = main[32:80]
            side_right[...] = side[32:80]
            side_total[...] = side[80:]
    pack_x(MIDDLE, [coef, right, field, zlow, zhigh, side_coef, side_right], up, down)


def middle_y(coef, right, field, zlow, zhigh, side_coef, side_right, low, high, up, down):
    pack_y(MIDDLE, [coef, right, field, zlow, zhigh, side_coef, side_right], low, high, up, down)


def middle_coef(coef, right, e):
    def get(x, k, t):
        if k < 6:
            return coef[pl.ds(((x + 3) * 18 + 6 * e + k) * 16, 16), :]
        return right[pl.ds(((x + 4) * 3 + e) * 16, 16), :]

    return get


def middle_sweeps(coef0, right0, field0, zlow0, zhigh0, side_coef0, side_right0, low, high, below, above, total1, side_total,
                  right, field, sides, error, packed, coef_far, coef, zlow, zhigh, side_coef, side_right, sums, side_sums,
                  wide, left):
    grow(MIDDLE, [coef0, right0, field0, zlow0, zhigh0, side_coef0, side_right0], low, high, below, above,
         [coef, right, field, zlow, zhigh, side_coef, side_right])
    inner = pl.ds(18 * 16, 8 * 18 * 16)
    keep = pltpu.make_async_copy(coef.at[inner, :], coef_far.at[inner, :], left.at[0])
    keep.start()
    both_sides(zlow, zhigh, sides)
    for e in range(3):

        def side_get(x, k, t):
            if k < 6:
                return side_coef[pl.ds(((x + 1) * 18 + 6 * e + k) * 16, 16), :]
            return side_right[pl.ds(((x + 2) * 3 + e) * 16, 16), :]

        get = middle_coef(coef, right, e)
        value = {x: swept(x, {y: [get(y, 6, 0)] for y in (x - 1, x, x + 1)}, get, 1) for x in range(-3, 7)}
        for x in range(-3, 7):
            error[pl.ds(((x + 3) * 3 + e) * 16, 16), :] = value[x][0]
        beside = {x: swept(x, {y: [side_get(y, 6, 0)] for y in (x - 1, x, x + 1)}, side_get, 1) for x in range(-1, 5)}
        for known, coef_of, weight, out in ((value, get, total1, sums), (beside, side_get, side_total, side_sums)):
            resid = []
            for x in range(4):
                change = swept(x, known, coef_of, 1)[0] - known[x][0]
                resid.append(change[:4] * weight[pl.ds((x * 3 + e) * 4, 4), :])
            for i in range(2):
                out[pl.ds((i * 3 + e) * 4, 4), :] = resid[2 * i] + resid[2 * i + 1]
    sums[pl.ds(24, 8), :] = jnp.zeros((8, LANES), F32)
    side_sums[pl.ds(24, 8), :] = jnp.zeros((8, LANES), F32)
    fine = lax.broadcasted_iota(jnp.int32, (LANES, LANES), 0)
    coarse = lax.broadcasted_iota(jnp.int32, (LANES, LANES), 1)
    own = (fine < 64) & ((fine >> 1) + HALO2 == coarse)
    above_own = (fine >= 2) & (fine < 42) & ((fine >> 1) + 51 == coarse)
    below_own = (fine >= 66) & (fine < 106) & ((fine >> 1) - 33 == coarse)
    wide[...] = exact_dot(
        sums[pl.ds(0, 16, 2), :] + sums[pl.ds(1, 16, 2), :], jnp.where(own, F32(0.125), F32(0))
    ) + exact_dot(
        side_sums[pl.ds(0, 16, 2), :] + side_sums[pl.ds(1, 16, 2), :],
        jnp.where(above_own | below_own, F32(0.125), F32(0)),
    )
    spread(wide, packed)
    keep.wait()


def spread(wide, out):
    lane = lanes_of(8)
    first, second = wide[pl.ds(0, 8), :], wide[pl.ds(6, 8), :]
    block = jnp.where(lane < 64, first, rolled(second, 64, 1))
    tail = jnp.zeros((1, LANES), F32)
    lane = lanes_of(1)
    for row in range(12):
        inside = (lane >= 8 * row) & (lane < 8 * row + 8)
        tail = jnp.where(inside, rolled(wide[pl.ds(row, 1), :], 8 * row - 64, 1), tail)
    rows = lax.broadcasted_iota(jnp.int32, (8, LANES), 0)
    block = jnp.where(rows < 6, block, jnp.where(rows == 6, jnp.broadcast_to(tail, (8, LANES)), F32(0)))
    for copy in range(out.shape[0] // 8):
        out[pl.ds(copy * 8, 8), :] = block


def coarse_place(x, e, j):
    return (x * 3 + e) * 2 + j


def coarse_coefs(gx, gy, shared, arrivals, coef, scale, total, coef3):
    lane = lanes_of(gy)
    used = lane < 72
    for g in range(gx):
        arrivals[g].wait()

        def rows(r):
            return shared[pl.ds(g * gy * SHARED + r, gy, SHARED), :]

        tails = [rows(48 + r) for r in range(8)]
        thirds = [rows(56 + r) for r in range(8)]

        def settle(w, d):
            tot = d + (((w[0] + w[1]) + (w[2] + w[3])) + (w[4] + w[5]))
            tot = jnp.where(tot > 0, tot, F32(1))
            return tot, 0.8 / tot

        for e in range(3):
            for j in range(2):
                pairs = {a: rows(a * 2 + j) for a in [6 * e + k for k in range(6)] + [18 + e]}
                for i in range(2):

                    def mean(a):
                        r = i * 42 + a * 2 + j
                        value = pairs[a] if i == 0 else rolled(pairs[a], 64, 1)
                        value = jnp.where(lane < 64, value, rolled(tails[r % 8], 64 - 8 * (r // 8), 1))
                        return jnp.where(used, value, F32(0))

                    w = [mean(6 * e + k) * 0.0625 for k in range(6)]
                    tot, inverse = settle(w, mean(18 + e))
                    base = coarse_place(2 * g + i, e, j)
                    for k in range(6):
                        coef[pl.ds((base * 6 + k) * gy, gy), :] = w[k] * inverse
                    scale[pl.ds(base * gy, gy), :] = inverse
                    total[pl.ds(base * gy, gy), :] = tot * 1.25

            def mean3(a):
                return jnp.where(lane < 36, rolled(thirds[a % 8], -36 * (a // 8), 1), F32(0))

            w = [mean3(6 * e + k) * 0.015625 for k in range(6)]
            tot, inverse = settle(w, mean3(18 + e))
            for k in range(6):
                coef3[pl.ds(((g * 3 + e) * 7 + k) * gy, gy), :] = w[k] * inverse
            coef3[pl.ds(((g * 3 + e) * 7 + 6) * gy, gy), :] = inverse


def coarse_levels(gx, gy, me_x, me_y, packed, coef, scale, total, coef3, right2, error2, rows6):
    planes = 2 * gx
    place = coarse_place
    lane = lanes_of(gy)
    used = lane < 72
    row = lax.broadcasted_iota(jnp.int32, (gy, LANES), 0)
    first_row, last_row = row == 0, row == gy - 1
    zero = jnp.zeros((gy, LANES), F32)

    for g in range(gx):
        blocks = [packed[pl.ds(g * gy * 8 + r, gy, 8), :] for r in range(7)]
        for i in range(2):
            for e in range(3):
                for j in range(2):
                    r = (i * 3 + e) * 2 + j
                    right = blocks[r] if r < 6 else rolled(blocks[r - 6], 64, 1)
                    right = jnp.where(lane < 64, right, rolled(blocks[6], 64 - 8 * r, 1))
                    base = place(2 * g + i, e, j) * gy
                    right2[pl.ds(base, gy), :] = jnp.where(used, right, F32(0)) * scale[pl.ds(base, gy), :]

    def sweep2(value, x, e, j):
        base = place(x, e, j)
        v = value[x, j]
        near = [
            value[x + 1, j] if x + 1 < planes else None,
            value[x - 1, j] if x > 0 else None,
            value[x, 1] if j == 0 else jnp.where(last_row, zero, rolled(value[x, 0], -1, 0)),
            value[x, 0] if j == 1 else jnp.where(first_row, zero, rolled(value[x, 1], 1, 0)),
            rolled(v, -1, 1),
            rolled(v, 1, 1),
        ]
        out = 0.2 * v + right2[pl.ds(base * gy, gy), :]
        for k in range(6):
            if near[k] is not None:
                out = out + coef[pl.ds((base * 6 + k) * gy, gy), :] * near[k]
        return out

    cells = [(x, j) for x in range(planes) for j in range(2)]
    halve = pair_matrix(0.125)
    fine = lax.broadcasted_iota(jnp.int32, (LANES, LANES), 1)
    coarse = lax.broadcasted_iota(jnp.int32, (LANES, LANES), 0)
    double = jnp.where((fine >> 1) == coarse, F32(1), F32(0))
    error2[...] = jnp.zeros(error2.shape, F32)
    before, sums = [], []
    for e in range(3):
        value = {(x, j): right2[pl.ds(place(x, e, j) * gy, gy), :] for x, j in cells}
        value = {(x, j): sweep2(value, x, e, j) for x, j in cells}
        before.append(value)
        resid = {
            (x, j): (sweep2(value, x, e, j) - value[x, j]) * total[pl.ds(place(x, e, j) * gy, gy), :] for x, j in cells
        }
        for g in range(gx):
            sums.append(
                (resid[2 * g, 0] + resid[2 * g, 1]) + (resid[2 * g + 1, 0] + resid[2 * g + 1, 1])
            )
    right3 = exact_dot(jnp.concatenate(sums, axis=0), halve)
    found = []
    for e in range(3):

        def coef_of(g, k):
            return coef3[pl.ds(((g * 3 + e) * 7 + k) * gy, gy), :]

        right = [right3[(e * gx + g) * gy : (e * gx + g + 1) * gy] * coef_of(g, 6) for g in range(gx)]
        value = right
        for step in range(7):
            new = []
            for g in range(gx):
                v = value[g]
                out = 0.2 * v + right[g]
                if g + 1 < gx:
                    out = out + coef_of(g, 0) * value[g + 1]
                if g > 0:
                    out = out + coef_of(g, 1) * value[g - 1]
                out = out + coef_of(g, 2) * jnp.where(last_row, zero, rolled(v, -1, 0))
                out = out + coef_of(g, 3) * jnp.where(first_row, zero, rolled(v, 1, 0))
                out = out + coef_of(g, 4) * rolled(v, -1, 1)
                out = out + coef_of(g, 5) * rolled(v, 1, 1)
                new.append(out)
            value = new
        found.extend(value)
    refined = exact_dot(jnp.concatenate(found, axis=0), double)
    for e in range(3):
        value = {
            (x, j): before[e][x, j] + refined[(e * gx + x // 2) * gy : (e * gx + x // 2 + 1) * gy] for x, j in cells
        }
        for step in range(2):
            value = {(x, j): sweep2(value, x, e, j) for x, j in cells}
        for x, j in cells:
            error2[pl.ds(place(x + 2, e, j) * (gy + 16) + 8, gy), :] = value[x, j]
    for plane in range(6):
        for e in range(3):
            for step, j, target in ((0, 0, 0), (0, 1, 1), (1, 0, 2), (1, 1, 3), (-1, 0, 6), (-1, 1, 7)):
                start = (((2 * me_x + plane) * 3 + e) * 2 + j) * (gy + 16) + 8 + me_y + step
                rows6[pl.ds((plane * 3 + e) * 8 + target, 1), :] = error2[pl.ds(start, 1), :]
            rows6[pl.ds((plane * 3 + e) * 8 + 4, 2), :] = jnp.zeros((2, LANES), F32)


def finish(gx, gy, shared_far, coef1_far, packed, error1, right1, stat, sides0, field2, sides2, out,
           shared, coef1, coef2, scale2, total2, coef3, right2, error2, rows6, fine2, rows1, fine1, arrived):
    chunk = gy * SHARED
    arrivals = [
        pltpu.make_async_copy(shared_far.at[pl.ds(g * chunk, chunk), :], shared.at[pl.ds(g * chunk, chunk), :], arrived.at[g])
        for g in range(gx)
    ]
    inner = pl.ds(18 * 16, 8 * 18 * 16)
    later = [
        pltpu.make_async_copy(coef1_far.at[inner, :], coef1.at[inner, :], arrived.at[gx]),
    ]
    for copy in arrivals + later:
        copy.start()
    coarse_coefs(gx, gy, shared, arrivals, coef2, scale2, total2, coef3)
    me_x, me_y = lax.axis_index("gx"), lax.axis_index("gy")
    coarse_levels(gx, gy, me_x, me_y, packed, coef2, scale2, total2, coef3, right2, error2, rows6)
    for copy in later:
        copy.wait()

    source = lax.broadcasted_iota(jnp.int32, (LANES, LANES), 0)
    target = lax.broadcasted_iota(jnp.int32, (LANES, LANES), 1)
    cell = jnp.where(target >= 96, target - LANES, target)
    wanted = (cell >= -4) & (cell < 68) & ((cell >> 1) + HALO2 == source)
    widened = exact_dot(rows6[...], jnp.where(wanted, F32(1), F32(0)))
    fine2[pl.ds(0, 144, 2), :] = widened
    fine2[pl.ds(1, 144, 2), :] = widened

    row = lax.broadcasted_iota(jnp.int32, (8, LANES), 0)
    for e in range(3):
        get = middle_coef(coef1, right1, e)
        value = {}
        for x in range(-3, 7):
            value[x] = [
                error1[pl.ds(((x + 3) * 3 + e) * 16, 16), :] + fine2[pl.ds(((x // 2 + 2) * 3 + e) * 16, 16), :]
            ]
        value = {x: swept(x, value, get, 1) for x in range(-2, 6)}
        value = {x: swept(x, value, get, 1) for x in range(-1, 5)}
        for x in range(-1, 5):
            whole = value[x][0]
            rows1[pl.ds(((x + 1) * 3 + e) * 8, 8), :] = jnp.where(row == 7, whole[8:], whole[:8])

    inner = jnp.where((target >> 1) == source, F32(1), F32(0))
    outer = jnp.where((target < 2) & (source == 64), F32(1), F32(0))
    outer = jnp.where((target >= 126) & (source == 127), F32(1), outer)
    for tile, matrix in ((0, inner), (1, outer)):
        widened = exact_dot(rows1[...], matrix)
        fine1[pl.ds(288 * tile, 144, 2), :] = widened
        fine1[pl.ds(288 * tile + 1, 144, 2), :] = widened

    for e in range(3):
        get = fine_coef(stat, sides0, e)
        value = {}
        for x in range(-2, 10):
            start = ((x // 2 + 1) * 3 + e) * 16
            value[x] = [
                field2[pl.ds(((x + 2) * 3 + e) * 16, 16), :] + fine1[pl.ds(start, 16), :],
                side_tile(sides2, (x + 2) * 16, 2 * e, 2) + fine1[pl.ds(288 + start, 16), :],
            ]
        value = {x: swept(x, value, get, 2) for x in range(-1, 9)}
        for x in range(8):
            out[e, x] = swept(x, value, get, 1)[0][:8]


def both_ways(axis, up, down):
    devices = lax.axis_size(axis)
    pairs = [(i, i + 1) for i in range(devices - 1)]
    return lax.ppermute(up, axis, pairs), lax.ppermute(down, axis, [(b, a) for a, b in pairs])


def to_all(value, devices):
    blocks = value.reshape(devices, value.shape[0] // devices, LANES)
    return lax.all_to_all(blocks, ("gx", "gy"), 0, 0).reshape(value.shape)


def per_device(couplings, diagonal, right_side, guess):
    gx, gy = lax.axis_size("gx"), lax.axis_size("gy")
    inputs = (couplings, diagonal, right_side, guess)

    stat, field, total, zup, zdown, coef1, scale1, total1 = call(
        prepare_whole, "prepare", [1344, 192, 192, Z_ROWS, Z_ROWS, 288, 48, 48], [], far_args=inputs,
        scratch=[value.shape for value in inputs] + [672, 336, 168, 88, 48], copies=4,
    )
    zlow, zhigh = both_ways("gz", zup, zdown)
    xup, xdown = call(fine_x, "fine_x", [x_rows(FINE)] * 2, [stat, field, zlow, zhigh])
    (shared,) = call(share, "share", [SHARED], [zlow, zhigh, zup], scratch=[96])
    shared = lax.all_gather(shared, ("gx", "gy"), tiled=True)
    xlow, xhigh = both_ways("gx", xup, xdown)
    yup, ydown = call(fine_y, "fine_y", [y_rows(FINE)] * 2, [stat, field, zlow, zhigh, xlow, xhigh])
    ylow, yhigh = both_ways("gy", yup, ydown)
    stat, sides0, field2, middle, zup, zdown = call(
        fine_sweeps, "fine_sweeps", [FINE[0].grown_rows(), FINE[2].grown_rows(), 192, 384, 192, 192],
        [stat, field, zlow, zhigh, xlow, xhigh, ylow, yhigh, total, coef1, scale1, total1],
        scratch=[s.grown_rows() for s in FINE[1:]] + [96],
    )

    zlow, zhigh = both_ways("gz", zup, zdown)
    coef1, right1, side_coef, side_right, side_total, xup, xdown = call(
        middle_x, "middle_x", [288, 48, 288, 48, 48, x_rows(MIDDLE), x_rows(MIDDLE)], [middle, field2, zlow, zhigh]
    )
    xlow, xhigh = both_ways("gx", xup, xdown)
    level1 = [coef1, right1, field2, zlow, zhigh, side_coef, side_right]
    yup, ydown = call(middle_y, "middle_y", [y_rows(MIDDLE)] * 2, [*level1, xlow, xhigh])
    ylow, yhigh = both_ways("gy", yup, ydown)
    right1, field2, sides2, error1, packed, coef1 = call(
        middle_sweeps, "middle_sweeps", [s.grown_rows() for s in MIDDLE[1:4]] + [480, gx * gy * 8],
        [*level1, xlow, xhigh, ylow, yhigh, total1, side_total],
        far_outs=[FAR], scratch=[MIDDLE[i].grown_rows() for i in (0, 3, 4, 5, 6)] + [32, 32, 16], copies=1,
    )
    packed = to_all(packed, gx * gy)

    tiles = 12 * gx * gy
    vmem = pl.BlockSpec(memory_space=pltpu.VMEM)
    far = pl.BlockSpec(memory_space=pltpu.HBM)
    near = [packed, error1, right1, stat, sides0, field2, sides2]
    scratch = [gx * gy * SHARED, MIDDLE[0].grown_rows(), tiles * 6, tiles, tiles, gx * 21 * gy]
    scratch += [tiles, (2 * gx + 4) * 6 * (gy + 16), 144, 288, 144, 576]
    return pl.pallas_call(
        lambda *refs: finish(gx, gy, *refs),
        name="finish",
        out_shape=jax.ShapeDtypeStruct(guess.shape, F32),
        in_specs=[far] * 2 + [vmem] * len(near),
        out_specs=vmem,
        scratch_shapes=[pltpu.VMEM((rows, LANES), F32) for rows in scratch] + [pltpu.SemaphoreType.DMA((gx + 1,))],
        compiler_params=pltpu.CompilerParams(vmem_limit_bytes=GRANT),
    )(shared, coef1, *near)


def solution(mesh):
    spec = P(None, "gx", "gy", "gz")
    return jax.shard_map(per_device, mesh=mesh, in_specs=(spec,) * 4, out_specs=spec, check_vma=False)
```

```python
import jax
import jax.numpy as jnp
from jax import lax
from jax.experimental import pallas as pl
from jax.experimental.pallas import tpu as pltpu
from jax.sharding import PartitionSpec as P


F32 = jnp.float32
LANES = 128
GRANT = 40 * 1024 * 1024
FAR = 49152
STATIC = 21
WIDE = 42
HALO2 = 20
SHARED = 64
MEANS = 84


def rolled(value, shift, axis):
    shift %= value.shape[axis]
    return value if shift == 0 else pltpu.roll(value, shift, axis)


def lanes_of(rows):
    return lax.broadcasted_iota(jnp.int32, (rows, LANES), 1)


def pair_matrix(weight):
    fine = lax.broadcasted_iota(jnp.int32, (LANES, LANES), 0)
    coarse = lax.broadcasted_iota(jnp.int32, (LANES, LANES), 1)
    return jnp.where((fine >> 1) == coarse, F32(weight), F32(0))


def exact_dot(left, right):
    return jnp.dot(left, right, precision=lax.Precision.HIGHEST, preferred_element_type=F32)


def call(body, name, outs, args, scratch=(), far_args=(), far_outs=(), copies=0, grant=GRANT):
    vmem = pl.BlockSpec(memory_space=pltpu.VMEM)
    far = pl.BlockSpec(memory_space=pltpu.HBM)
    semaphores = [pltpu.SemaphoreType.DMA((copies,))] if copies else []
    return pl.pallas_call(
        body,
        name=name,
        out_shape=[jax.ShapeDtypeStruct((rows, LANES), F32) for rows in (*outs, *far_outs)],
        in_specs=[far] * len(far_args) + [vmem] * len(args),
        out_specs=[vmem] * len(outs) + [far] * len(far_outs),
        scratch_shapes=[pltpu.VMEM(r if isinstance(r, tuple) else (r, LANES), F32) for r in scratch] + semaphores,
        compiler_params=pltpu.CompilerParams(vmem_limit_bytes=grant),
    )(*far_args, *args)


class Stream:
    def __init__(self, count, rows, planes, halo, reach):
        self.count, self.rows, self.planes, self.halo, self.reach = count, rows, planes, halo, reach

    def extent(self, depth):
        return self.reach - depth

    def halo_rows(self):
        return self.halo * self.count * self.rows

    def grown_rows(self):
        return (self.planes + 2 * self.halo) * self.count * 16


FINE = [Stream(STATIC, 8, 8, 2, 2), Stream(3, 8, 8, 3, 3), Stream(1, 8, 8, 3, 3), Stream(1, 8, 8, 3, 3)]
MIDDLE = [Stream(18, 4, 4, 3, 4), Stream(3, 4, 4, 4, 5), Stream(3, 8, 8, 2, 2), Stream(1, 8, 8, 2, 2), Stream(1, 8, 8, 2, 2)]
MIDDLE += [Stream(18, 4, 4, 1, 1), Stream(3, 4, 4, 2, 2)]


def x_rows(streams):
    return sum(s.halo_rows() for s in streams)


def y_pieces(streams):
    offset = 0
    pieces = []
    for depth in range(1, 1 + max(s.halo for s in streams)):
        for index, s in enumerate(streams):
            if depth <= s.halo:
                planes = s.planes + 2 * s.extent(depth)
                pieces.append((index, depth, offset))
                offset += planes * s.count
    return pieces, offset


def y_rows(streams):
    total = y_pieces(streams)[1]
    return -(-total // 8) * 8


def pack_x(streams, mains, up, down):
    offset = 0
    for s, main in zip(streams, mains):
        size = s.halo_rows()
        whole = s.planes * s.count * s.rows
        up[pl.ds(offset, size), :] = main[pl.ds(whole - size, size), :]
        down[pl.ds(offset, size), :] = main[pl.ds(0, size), :]
        offset += size


def pack_y(streams, mains, low, high, up, down):
    starts = [sum(s.halo_rows() for s in streams[:i]) for i in range(len(streams))]
    pieces, total = y_pieces(streams)
    padded = y_rows(streams)
    for out, upward in ((up, True), (down, False)):
        if padded > total:
            out[pl.ds(padded - 8, 8), :] = jnp.zeros((8, LANES), F32)
        for index, depth, offset in pieces:
            s = streams[index]
            row = s.rows - depth if upward else depth - 1
            beyond = s.extent(depth)
            side = beyond * s.count
            middle = s.planes * s.count
            if beyond:
                first = starts[index] + (s.halo - beyond) * s.count * s.rows + row
                out[pl.ds(offset, side), :] = low[pl.ds(first, side, s.rows), :]
            out[pl.ds(offset + side, middle), :] = mains[index][pl.ds(row, middle, s.rows), :]
            if beyond:
                out[pl.ds(offset + side + middle, side), :] = high[pl.ds(starts[index] + row, side, s.rows), :]


def grow(streams, mains, low, high, below, above, grown):
    starts = [sum(s.halo_rows() for s in streams[:i]) for i in range(len(streams))]
    for index, s in enumerate(streams):
        out = grown[index]
        out[...] = jnp.zeros(out.shape, F32)
        edge = s.halo * s.count
        middle = s.planes * s.count
        for source, base, first, number in (
            (low, starts[index], 0, edge),
            (mains[index], 0, edge, middle),
            (high, starts[index], edge + middle, edge),
        ):
            if s.rows == 8:
                for tile in range(number):
                    out[pl.ds((first + tile) * 16, 8), :] = source[pl.ds(base + tile * 8, 8), :]
            else:
                for row in range(s.rows):
                    out[pl.ds(first * 16 + row, number, 16), :] = source[pl.ds(base + row, number, s.rows), :]
    for index, depth, offset in y_pieces(streams)[0]:
        s = streams[index]
        beyond = s.extent(depth)
        number = (s.planes + 2 * beyond) * s.count
        first = (s.halo - beyond) * s.count * 16
        grown[index][pl.ds(first + s.rows + depth - 1, number, 16), :] = above[pl.ds(offset, number), :]
        grown[index][pl.ds(first + 16 - depth, number, 16), :] = below[pl.ds(offset, number), :]


def prepare(c, d, b, g, stat, field, total, zup, zdown, coef1, scale1, total1, summed, means1, half2, sum2, sum3):
    lane = lanes_of(8)
    for x in range(8):
        up = jnp.zeros((8, LANES), F32)
        down = jnp.zeros((8, LANES), F32)
        packed = []
        for e in range(3):
            w = [c[6 * e + k, x] for k in range(6)]
            tot = d[e, x] + (((w[0] + w[1]) + (w[2] + w[3])) + (w[4] + w[5]))
            inverse = 0.8 / tot
            for k in range(6):
                packed.append((6 * e + k, w[k] * inverse))
            packed.append((18 + e, b[e, x] * inverse))
            field[pl.ds((x * 3 + e) * 8, 8), :] = g[e, x]
            total[pl.ds((x * 3 + e) * 8, 8), :] = tot * 1.25
        for a, value in packed:
            stat[pl.ds((x * STATIC + a) * 8, 8), :] = value
            inside = (lane >= 2 * a) & (lane < 2 * a + 2)
            up = jnp.where(inside, rolled(value, 2 * a + 2, 1), up)
            down = jnp.where(inside, rolled(value, 2 * a, 1), down)
        for e in range(3):
            base = 42 + 3 * e
            inside = (lane >= base) & (lane < base + 3)
            up = jnp.where(inside, rolled(g[e, x], base + 3, 1), up)
            down = jnp.where(inside, rolled(g[e, x], base, 1), down)
        zup[pl.ds(x * 8, 8), :] = up
        zdown[pl.ds(x * 8, 8), :] = down

    halve = pair_matrix(0.125)
    for x in range(4):
        for a in range(STATIC):
            one = c[a, 2 * x] + c[a, 2 * x + 1] if a < 18 else d[a - 18, 2 * x] + d[a - 18, 2 * x + 1]
            summed[pl.ds((x * STATIC + a) * 8, 8), :] = one
    means1[...] = exact_dot(summed[pl.ds(0, 336, 2), :] + summed[pl.ds(1, 336, 2), :], halve)
    for x in range(4):
        for e in range(3):
            w = [0.25 * means1[pl.ds((x * STATIC + 6 * e + k) * 4, 4), :] for k in range(6)]
            tot = means1[pl.ds((x * STATIC + 18 + e) * 4, 4), :] + (((w[0] + w[1]) + (w[2] + w[3])) + (w[4] + w[5]))
            tot = jnp.where(tot > 0, tot, F32(1))
            inverse = 0.8 / tot
            for k in range(6):
                coef1[pl.ds((x * 18 + 6 * e + k) * 4, 4), :] = w[k] * inverse
            scale1[pl.ds((x * 3 + e) * 4, 4), :] = inverse
            total1[pl.ds((x * 3 + e) * 4, 4), :] = tot * 1.25
    half2[...] = means1[pl.ds(0, 168, 2), :] + means1[pl.ds(1, 168, 2), :]
    for i in range(2):
        sum2[pl.ds(42 * i, 42), :] = half2[pl.ds(84 * i, 42), :] + half2[pl.ds(84 * i + 42, 42), :]
    sum2[pl.ds(0, MEANS), :] = exact_dot(sum2[...], halve)[:MEANS]
    sum3[pl.ds(0, 42), :] = sum2[pl.ds(0, 42), :] + sum2[pl.ds(42, 42), :]
    sum3[pl.ds(42, 6), :] = jnp.zeros((6, LANES), F32)
    means3 = exact_dot(sum3[pl.ds(0, 24, 2), :] + sum3[pl.ds(1, 24, 2), :], halve)
    sum2[pl.ds(0, STATIC), :] = sum2[pl.ds(0, STATIC), :] + rolled(means3, 32, 1)[:STATIC]
    zup[pl.ds(64, MEANS), :] = sum2[pl.ds(0, MEANS), :]
    zdown[pl.ds(64, MEANS), :] = sum2[pl.ds(0, MEANS), :]


def prepare_whole(inputs, stat, field, total, zup, zdown, coef1, scale1, total1, summed, means1, half2, sum2, sum3):
    sum2[pl.ds(80, 8), :] = jnp.zeros((8, LANES), F32)
    for out in (zup, zdown):
        out[pl.ds(144, 8), :] = jnp.zeros((8, LANES), F32)
    c, d, b, g = (inputs.at[pl.ds(first, number)] for first, number in ((0, 18), (18, 3), (21, 3), (24, 3)))
    prepare(c, d, b, g, stat, field, total, zup, zdown, coef1, scale1, total1, summed, means1, half2, sum2, sum3)


Z_ROWS = 152


def fine_x(stat, field, zlow, zhigh, up, down):
    pack_x(FINE, [stat, field, zlow, zhigh], up, down)


def share(zlow, zhigh, zown, shared, wide):
    lane = lanes_of(MEANS)
    low, own, high = (ref[pl.ds(64, MEANS), :] for ref in (zlow, zown, zhigh))
    value = jnp.zeros((MEANS, LANES), F32)
    for source, shift, first, last in (
        (low, -12, 0, 20),
        (own, 20, 20, 52),
        (high, 52, 52, 72),
        (low, 34, 72, 82),
        (own, 50, 82, 98),
        (high, 66, 98, 108),
    ):
        value = jnp.where((lane >= first) & (lane < last), rolled(source, shift, 1), value)
    wide[pl.ds(80, 16), :] = jnp.zeros((16, LANES), F32)
    wide[pl.ds(0, MEANS), :] = value
    lane = lanes_of(48)
    body = jnp.where(lane < 64, wide[pl.ds(0, 48), :], rolled(wide[pl.ds(42, 48), :], 64, 1))
    lane = lanes_of(8)
    tail = jnp.zeros((8, LANES), F32)
    third = jnp.zeros((8, LANES), F32)
    for group in range(11):
        value = wide[pl.ds(8 * group, 8), :]
        inside = (lane >= 8 * group) & (lane < 8 * group + 8)
        tail = jnp.where(inside, rolled(value, 8 * group - 64, 1), tail)
        if group < 3:
            inside = (lane >= 36 * group) & (lane < 36 * group + 36)
            third = jnp.where(inside, rolled(value, 36 * group - 72, 1), third)
    shared[pl.ds(0, 48), :] = body
    shared[pl.ds(48, 8), :] = tail
    shared[pl.ds(56, 8), :] = third


def fine_y(stat, field, zlow, zhigh, low, high, up, down):
    pack_y(FINE, [stat, field, zlow, zhigh], low, high, up, down)


def z_near(tiles):
    if len(tiles) == 1:
        return [rolled(tiles[0], -1, 1)], [rolled(tiles[0], 1, 1)]
    lane = lanes_of(tiles[0].shape[0])
    ahead = [rolled(t, -1, 1) for t in tiles]
    behind = [rolled(t, 1, 1) for t in tiles]
    last, first = lane == LANES - 1, lane == 0
    plus = [jnp.where(last, ahead[1], ahead[0]), jnp.where(last, ahead[0], ahead[1])]
    minus = [jnp.where(first, behind[1], behind[0]), jnp.where(first, behind[0], behind[1])]
    return plus, minus


def swept(x, value, coef, tiles):
    plus, minus = z_near(value[x])
    out = []
    for t in range(tiles):
        v = value[x][t]
        near = [value[x + 1][t], value[x - 1][t], rolled(v, -1, 0), rolled(v, 1, 0), plus[t], minus[t]]
        terms = [coef(x, k, t) * near[k] for k in range(6)]
        out.append((0.2 * v + coef(x, 6, t)) + (((terms[0] + terms[1]) + (terms[2] + terms[3])) + (terms[4] + terms[5])))
    return out


def both_sides(zlow, zhigh, sides):
    for tile in range(sides.shape[0] // 16):
        rows = pl.ds(tile * 16, 16)
        sides[rows, :] = jnp.where(lanes_of(16) < 64, zhigh[rows, :], rolled(zlow[rows, :], 64, 1))


def side_tile(sides, row, base, width):
    lane = lanes_of(16)
    packed = sides[pl.ds(row, 16), :]
    high = rolled(packed, -base, 1)
    low = rolled(packed, -width - base - 64, 1)
    return jnp.where(lane < width, high, jnp.where(lane >= LANES - width, low, F32(0)))


def fine_coef(stat, sides, e):
    cache = {}

    def coef(x, k, t):
        a = 6 * e + k if k < 6 else 18 + e
        if t == 0:
            return stat[pl.ds(((x + 2) * STATIC + a) * 16, 16), :]
        if (x, k) not in cache:
            cache[x, k] = side_tile(sides, (x + 3) * 16, 2 * a, 2)
        return cache[x, k]

    return coef


def fine_sweeps(stat0, field0, zlow0, zhigh0, low, high, below, above, total, coef1, scale1, total1,
                stat, sides, field2, middle, zup, zdown, field, zlow, zhigh, sums):
    grow(FINE, [stat0, field0, zlow0, zhigh0], low, high, below, above, [stat, field, zlow, zhigh])
    both_sides(zlow, zhigh, sides)
    for e in range(3):
        coef = fine_coef(stat, sides, e)
        value = {}
        for x in range(-3, 11):
            value[x] = [
                field[pl.ds(((x + 3) * 3 + e) * 16, 16), :],
                side_tile(sides, (x + 3) * 16, 42 + 3 * e, 3),
            ]
        value = {x: swept(x, value, coef, 2) for x in range(-2, 10)}
        value = {x: swept(x, value, coef, 2) for x in range(-1, 9)}
        resid = []
        for x in range(8):
            now = value[x][0]
            field2[pl.ds((x * 3 + e) * 8, 8), :] = now[:8]
            change = swept(x, value, coef, 1)[0] - now
            resid.append(change[:8] * total[pl.ds((x * 3 + e) * 8, 8), :])
        for x in range(4):
            sums[pl.ds((x * 3 + e) * 8, 8), :] = resid[2 * x] + resid[2 * x + 1]
    right = exact_dot(sums[pl.ds(0, 48, 2), :] + sums[pl.ds(1, 48, 2), :], pair_matrix(0.125))
    middle[pl.ds(0, 288), :] = coef1[...]
    middle[pl.ds(288, 48), :] = right * scale1[...]
    middle[pl.ds(336, 48), :] = total1[...]
    lane = lanes_of(128)
    up = jnp.zeros((128, LANES), F32)
    down = jnp.zeros((128, LANES), F32)
    for group in range(3):
        value = middle[pl.ds(128 * group, 128), :]
        inside = (lane >= WIDE * group) & (lane < WIDE * group + WIDE)
        up = jnp.where(inside, rolled(value, WIDE * group + WIDE - 64, 1), up)
        down = jnp.where(inside, rolled(value, WIDE * group, 1), down)
    zup[pl.ds(64, 128), :] = up
    zdown[pl.ds(64, 128), :] = down
    lane = lanes_of(8)
    for x in range(8):
        up = jnp.zeros((8, LANES), F32)
        down = jnp.zeros((8, LANES), F32)
        for e in range(3):
            value = field2[pl.ds((x * 3 + e) * 8, 8), :]
            inside = (lane >= 2 * e) & (lane < 2 * e + 2)
            up = jnp.where(inside, rolled(value, 2 * e + 2, 1), up)
            down = jnp.where(inside, rolled(value, 2 * e, 1), down)
        zup[pl.ds(x * 8, 8), :] = up
        zdown[pl.ds(x * 8, 8), :] = down


def middle_x(middle, field, zlow, zhigh, coef, right, side_coef, side_right, side_total, up, down):
    lane = lanes_of(128)
    low, high = zlow[pl.ds(64, 128), :], zhigh[pl.ds(64, 128), :]
    for group in range(3):
        own = middle[pl.ds(128 * group, 128), :]
        main = jnp.where((lane >= 64) & (lane < 68), rolled(high, 64 - WIDE * group, 1), own)
        main = jnp.where(lane >= 124, rolled(low, 128 - WIDE - WIDE * group, 1), main)
        side = jnp.where(lane < 2, rolled(own, -62, 1), F32(0))
        side = jnp.where((lane >= 2) & (lane < 2 + WIDE), rolled(high, 2 - WIDE * group, 1), side)
        side = jnp.where((lane >= 64) & (lane < 64 + WIDE), rolled(low, 64 - WIDE * group, 1), side)
        side = jnp.where((lane >= 106) & (lane < 108), rolled(own, 106, 1), side)
        if group < 2:
            coef[pl.ds(128 * group, 128), :] = main
            side_coef[pl.ds(128 * group, 128), :] = side
        else:
            coef[pl.ds(256, 32), :] = main[:32]
            side_coef[pl.ds(256, 32), :] = side[:32]
            right[...] = main[32:80]
            side_right[...] = side[32:80]
            side_total[...] = side[80:]
    pack_x(MIDDLE, [coef, right, field, zlow, zhigh, side_coef, side_right], up, down)


def middle_y(coef, right, field, zlow, zhigh, side_coef, side_right, low, high, up, down):
    pack_y(MIDDLE, [coef, right, field, zlow, zhigh, side_coef, side_right], low, high, up, down)


def middle_coef(coef, right, e):
    def get(x, k, t):
        if k < 6:
            return coef[pl.ds(((x + 3) * 18 + 6 * e + k) * 16, 16), :]
        return right[pl.ds(((x + 4) * 3 + e) * 16, 16), :]

    return get


def middle_sweeps(coef0, right0, field0, zlow0, zhigh0, side_coef0, side_right0, low, high, below, above, total1, side_total,
                  right, field, sides, error, packed, coef_far, coef, zlow, zhigh, side_coef, side_right, sums, side_sums,
                  wide, left):
    grow(MIDDLE, [coef0, right0, field0, zlow0, zhigh0, side_coef0, side_right0], low, high, below, above,
         [coef, right, field, zlow, zhigh, side_coef, side_right])
    inner = pl.ds(18 * 16, 8 * 18 * 16)
    keep = pltpu.make_async_copy(coef.at[inner, :], coef_far.at[inner, :], left.at[0])
    keep.start()
    both_sides(zlow, zhigh, sides)
    for e in range(3):

        def side_get(x, k, t):
            if k < 6:
                return side_coef[pl.ds(((x + 1) * 18 + 6 * e + k) * 16, 16), :]
            return side_right[pl.ds(((x + 2) * 3 + e) * 16, 16), :]

        get = middle_coef(coef, right, e)
        value = {x: swept(x, {y: [get(y, 6, 0)] for y in (x - 1, x, x + 1)}, get, 1) for x in range(-3, 7)}
        for x in range(-3, 7):
            error[pl.ds(((x + 3) * 3 + e) * 16, 16), :] = value[x][0]
        beside = {x: swept(x, {y: [side_get(y, 6, 0)] for y in (x - 1, x, x + 1)}, side_get, 1) for x in range(-1, 5)}
        for known, coef_of, weight, out in ((value, get, total1, sums), (beside, side_get, side_total, side_sums)):
            resid = []
            for x in range(4):
                change = swept(x, known, coef_of, 1)[0] - known[x][0]
                resid.append(change[:4] * weight[pl.ds((x * 3 + e) * 4, 4), :])
            for i in range(2):
                out[pl.ds((i * 3 + e) * 4, 4), :] = resid[2 * i] + resid[2 * i + 1]
    sums[pl.ds(24, 8), :] = jnp.zeros((8, LANES), F32)
    side_sums[pl.ds(24, 8), :] = jnp.zeros((8, LANES), F32)
    fine = lax.broadcasted_iota(jnp.int32, (LANES, LANES), 0)
    coarse = lax.broadcasted_iota(jnp.int32, (LANES, LANES), 1)
    own = (fine < 64) & ((fine >> 1) + HALO2 == coarse)
    above_own = (fine >= 2) & (fine < 42) & ((fine >> 1) + 51 == coarse)
    below_own = (fine >= 66) & (fine < 106) & ((fine >> 1) - 33 == coarse)
    wide[...] = exact_dot(
        sums[pl.ds(0, 16, 2), :] + sums[pl.ds(1, 16, 2), :], jnp.where(own, F32(0.125), F32(0))
    ) + exact_dot(
        side_sums[pl.ds(0, 16, 2), :] + side_sums[pl.ds(1, 16, 2), :],
        jnp.where(above_own | below_own, F32(0.125), F32(0)),
    )
    spread(wide, packed)
    keep.wait()


def spread(wide, out):
    lane = lanes_of(8)
    first, second = wide[pl.ds(0, 8), :], wide[pl.ds(6, 8), :]
    block = jnp.where(lane < 64, first, rolled(second, 64, 1))
    tail = jnp.zeros((1, LANES), F32)
    lane = lanes_of(1)
    for row in range(12):
        inside = (lane >= 8 * row) & (lane < 8 * row + 8)
        tail = jnp.where(inside, rolled(wide[pl.ds(row, 1), :], 8 * row - 64, 1), tail)
    rows = lax.broadcasted_iota(jnp.int32, (8, LANES), 0)
    block = jnp.where(rows < 6, block, jnp.where(rows == 6, jnp.broadcast_to(tail, (8, LANES)), F32(0)))
    for copy in range(out.shape[0] // 8):
        out[pl.ds(copy * 8, 8), :] = block


def coarse_parts(gx, gy):
    each = 4 * gx * gy
    sizes = [3 * each, 3 * each, 6 * each, 6 * each, 6 * each, 21 * gx * gy]
    return [(sum(sizes[:i]), size) for i, size in enumerate(sizes)]


def coarse_coefs(gx, gy, shared, table_far, table, left):
    (scale_at, _), (total_at, _), (coef_at, _), _, _, (coef3_at, size3) = coarse_parts(gx, gy)
    lane = lanes_of(gy)
    used = lane < 72
    for g in range(gx):

        def rows(r):
            return shared[pl.ds(g * gy * SHARED + r, gy, SHARED), :]

        tails = [rows(48 + r) for r in range(8)]
        thirds = [rows(56 + r) for r in range(8)]

        def settle(w, d):
            tot = d + (((w[0] + w[1]) + (w[2] + w[3])) + (w[4] + w[5]))
            tot = jnp.where(tot > 0, tot, F32(1))
            return tot, 0.8 / tot

        for e in range(3):
            for j in range(2):
                pairs = {a: rows(a * 2 + j) for a in [6 * e + k for k in range(6)] + [18 + e]}
                for i in range(2):

                    def mean(a):
                        r = i * 42 + a * 2 + j
                        value = pairs[a] if i == 0 else rolled(pairs[a], 64, 1)
                        value = jnp.where(lane < 64, value, rolled(tails[r % 8], 64 - 8 * (r // 8), 1))
                        return jnp.where(used, value, F32(0))

                    w = [mean(6 * e + k) * 0.0625 for k in range(6)]
                    tot, inverse = settle(w, mean(18 + e))
                    base = (e * 2 * gx + 2 * g + i) * 2 + j
                    for k in range(6):
                        table[pl.ds(coef_at + (base * 6 + k) * gy, gy), :] = w[k] * inverse
                    table[pl.ds(scale_at + base * gy, gy), :] = inverse
                    table[pl.ds(total_at + base * gy, gy), :] = tot * 1.25

            def mean3(a):
                return jnp.where(lane < 36, rolled(thirds[a % 8], -36 * (a // 8), 1), F32(0))

            w = [mean3(6 * e + k) * 0.015625 for k in range(6)]
            tot, inverse = settle(w, mean3(18 + e))
            for k in range(6):
                table[pl.ds(coef3_at + ((g * 3 + e) * 7 + k) * gy, gy), :] = w[k] * inverse
            table[pl.ds(coef3_at + ((g * 3 + e) * 7 + 6) * gy, gy), :] = inverse
    keep = pltpu.make_async_copy(table, table_far.at[pl.ds(0, coef3_at + size3), :], left.at[0])
    keep.start()
    keep.wait()


def coarse_levels(gx, gy, me_x, me_y, packed, table, arrivals, right2, error2, rows6):
    planes = 2 * gx
    (scale_at, _), (total_at, _), (coef_at, _), _, _, (coef3_at, _) = coarse_parts(gx, gy)

    def place(x, e, j):
        return (e * 2 * gx + x) * 2 + j

    error2[...] = jnp.zeros(error2.shape, F32)
    arrivals[0].wait()
    lane = lanes_of(gy)
    used = lane < 72
    row = lax.broadcasted_iota(jnp.int32, (gy, LANES), 0)
    first_row, last_row = row == 0, row == gy - 1
    zero = jnp.zeros((gy, LANES), F32)

    for g in range(gx):
        blocks = [packed[pl.ds(g * gy * 8 + r, gy, 8), :] for r in range(7)]
        for i in range(2):
            for e in range(3):
                for j in range(2):
                    r = (i * 3 + e) * 2 + j
                    right = blocks[r] if r < 6 else rolled(blocks[r - 6], 64, 1)
                    right = jnp.where(lane < 64, right, rolled(blocks[6], 64 - 8 * r, 1))
                    base = place(2 * g + i, e, j) * gy
                    right2[pl.ds(base, gy), :] = jnp.where(used, right, F32(0)) * table[pl.ds(scale_at + base, gy), :]

    def sweep2(value, x, e, j):
        base = place(x, e, j)
        v = value[x, j]
        near = [
            value[x + 1, j] if x + 1 < planes else None,
            value[x - 1, j] if x > 0 else None,
            value[x, 1] if j == 0 else jnp.where(last_row, zero, rolled(value[x, 0], -1, 0)),
            value[x, 0] if j == 1 else jnp.where(first_row, zero, rolled(value[x, 1], 1, 0)),
            rolled(v, -1, 1),
            rolled(v, 1, 1),
        ]
        out = 0.2 * v + right2[pl.ds(base * gy, gy), :]
        for k in range(6):
            if near[k] is not None:
                out = out + table[pl.ds(coef_at + (base * 6 + k) * gy, gy), :] * near[k]
        return out

    cells = [(x, j) for x in range(planes) for j in range(2)]
    halve = pair_matrix(0.125)
    fine = lax.broadcasted_iota(jnp.int32, (LANES, LANES), 1)
    coarse = lax.broadcasted_iota(jnp.int32, (LANES, LANES), 0)
    double = jnp.where((fine >> 1) == coarse, F32(1), F32(0))
    before, sums = [], []
    for e in range(3):
        if e == 0:
            arrivals[1].wait()
        arrivals[2 + e].wait()
        value = {(x, j): right2[pl.ds(place(x, e, j) * gy, gy), :] for x, j in cells}
        value = {(x, j): sweep2(value, x, e, j) for x, j in cells}
        before.append(value)
        resid = {
            (x, j): (sweep2(value, x, e, j) - value[x, j]) * table[pl.ds(total_at + place(x, e, j) * gy, gy), :] for x, j in cells
        }
        for g in range(gx):
            sums.append(
                (resid[2 * g, 0] + resid[2 * g, 1]) + (resid[2 * g + 1, 0] + resid[2 * g + 1, 1])
            )
    arrivals[5].wait()
    right3 = exact_dot(jnp.concatenate(sums, axis=0), halve)
    found = []
    for e in range(3):

        def coef_of(g, k):
            return table[pl.ds(coef3_at + ((g * 3 + e) * 7 + k) * gy, gy), :]

        right = [right3[(e * gx + g) * gy : (e * gx + g + 1) * gy] * coef_of(g, 6) for g in range(gx)]
        value = right
        for step in range(7):
            new = []
            for g in range(gx):
                v = value[g]
                out = 0.2 * v + right[g]
                if g + 1 < gx:
                    out = out + coef_of(g, 0) * value[g + 1]
                if g > 0:
                    out = out + coef_of(g, 1) * value[g - 1]
                out = out + coef_of(g, 2) * jnp.where(last_row, zero, rolled(v, -1, 0))
                out = out + coef_of(g, 3) * jnp.where(first_row, zero, rolled(v, 1, 0))
                out = out + coef_of(g, 4) * rolled(v, -1, 1)
                out = out + coef_of(g, 5) * rolled(v, 1, 1)
                new.append(out)
            value = new
        found.extend(value)
    refined = exact_dot(jnp.concatenate(found, axis=0), double)
    for e in range(3):
        value = {
            (x, j): before[e][x, j] + refined[(e * gx + x // 2) * gy : (e * gx + x // 2 + 1) * gy] for x, j in cells
        }
        for step in range(2):
            value = {(x, j): sweep2(value, x, e, j) for x, j in cells}
        for x, j in cells:
            error2[pl.ds((((x + 2) * 3 + e) * 2 + j) * (gy + 16) + 8, gy), :] = value[x, j]
    for plane in range(6):
        for e in range(3):
            for step, j, target in ((0, 0, 0), (0, 1, 1), (1, 0, 2), (1, 1, 3), (-1, 0, 6), (-1, 1, 7)):
                start = (((2 * me_x + plane) * 3 + e) * 2 + j) * (gy + 16) + 8 + me_y + step
                rows6[pl.ds((plane * 3 + e) * 8 + target, 1), :] = error2[pl.ds(start, 1), :]
            rows6[pl.ds((plane * 3 + e) * 8 + 4, 2), :] = jnp.zeros((2, LANES), F32)


def finish(gx, gy, table_far, coef1_far, packed, error1, right1, stat, sides0, field2, sides2, out,
           table, coef1, right2, error2, rows6, fine2, rows1, fine1, arrived):
    inner = pl.ds(18 * 16, 8 * 18 * 16)
    pieces = [(table_far, table, pl.ds(first, size)) for first, size in coarse_parts(gx, gy)]
    pieces.append((coef1_far, coef1, inner))
    arrivals = [
        pltpu.make_async_copy(far.at[rows, :], near.at[rows, :], arrived.at[i])
        for i, (far, near, rows) in enumerate(pieces)
    ]
    for copy in arrivals:
        copy.start()
    me_x, me_y = lax.axis_index("gx"), lax.axis_index("gy")
    coarse_levels(gx, gy, me_x, me_y, packed, table, arrivals, right2, error2, rows6)
    arrivals[6].wait()

    source = lax.broadcasted_iota(jnp.int32, (LANES, LANES), 0)
    target = lax.broadcasted_iota(jnp.int32, (LANES, LANES), 1)
    cell = jnp.where(target >= 96, target - LANES, target)
    wanted = (cell >= -4) & (cell < 68) & ((cell >> 1) + HALO2 == source)
    widened = exact_dot(rows6[...], jnp.where(wanted, F32(1), F32(0)))
    fine2[pl.ds(0, 144, 2), :] = widened
    fine2[pl.ds(1, 144, 2), :] = widened

    row = lax.broadcasted_iota(jnp.int32, (8, LANES), 0)
    for e in range(3):
        get = middle_coef(coef1, right1, e)
        value = {}
        for x in range(-3, 7):
            value[x] = [
                error1[pl.ds(((x + 3) * 3 + e) * 16, 16), :] + fine2[pl.ds(((x // 2 + 2) * 3 + e) * 16, 16), :]
            ]
        value = {x: swept(x, value, get, 1) for x in range(-2, 6)}
        value = {x: swept(x, value, get, 1) for x in range(-1, 5)}
        for x in range(-1, 5):
            whole = value[x][0]
            rows1[pl.ds(((x + 1) * 3 + e) * 8, 8), :] = jnp.where(row == 7, whole[8:], whole[:8])

    inner = jnp.where((target >> 1) == source, F32(1), F32(0))
    outer = jnp.where((target < 2) & (source == 64), F32(1), F32(0))
    outer = jnp.where((target >= 126) & (source == 127), F32(1), outer)
    for tile, matrix in ((0, inner), (1, outer)):
        widened = exact_dot(rows1[...], matrix)
        fine1[pl.ds(288 * tile, 144, 2), :] = widened
        fine1[pl.ds(288 * tile + 1, 144, 2), :] = widened

    for e in range(3):
        get = fine_coef(stat, sides0, e)
        value = {}
        for x in range(-2, 10):
            start = ((x // 2 + 1) * 3 + e) * 16
            value[x] = [
                field2[pl.ds(((x + 2) * 3 + e) * 16, 16), :] + fine1[pl.ds(start, 16), :],
                side_tile(sides2, (x + 2) * 16, 2 * e, 2) + fine1[pl.ds(288 + start, 16), :],
            ]
        value = {x: swept(x, value, get, 2) for x in range(-1, 9)}
        for x in range(8):
            out[e, x] = swept(x, value, get, 1)[0][:8]


def both_ways(axis, up, down):
    devices = lax.axis_size(axis)
    pairs = [(i, i + 1) for i in range(devices - 1)]
    return lax.ppermute(up, axis, pairs), lax.ppermute(down, axis, [(b, a) for a, b in pairs])


def to_all(value, devices):
    blocks = value.reshape(devices, value.shape[0] // devices, LANES)
    return lax.all_to_all(blocks, ("gx", "gy"), 0, 0).reshape(value.shape)


def per_device(couplings, diagonal, right_side, guess):
    gx, gy = lax.axis_size("gx"), lax.axis_size("gy")
    inputs = jnp.concatenate([couplings, diagonal, right_side, guess])

    stat, field, total, zup, zdown, coef1, scale1, total1 = call(
        prepare_whole, "prepare", [1344, 192, 192, Z_ROWS, Z_ROWS, 288, 48, 48], [inputs], scratch=[672, 336, 168, 88, 48]
    )
    zlow, zhigh = both_ways("gz", zup, zdown)
    xup, xdown = call(fine_x, "fine_x", [x_rows(FINE)] * 2, [stat, field, zlow, zhigh])
    (shared,) = call(share, "share", [SHARED], [zlow, zhigh, zup], scratch=[96])
    shared = lax.all_gather(shared, ("gx", "gy"), tiled=True)
    xlow, xhigh = both_ways("gx", xup, xdown)
    yup, ydown = call(fine_y, "fine_y", [y_rows(FINE)] * 2, [stat, field, zlow, zhigh, xlow, xhigh])
    ylow, yhigh = both_ways("gy", yup, ydown)
    stat, sides0, field2, middle, zup, zdown = call(
        fine_sweeps, "fine_sweeps", [FINE[0].grown_rows(), FINE[2].grown_rows(), 192, 384, 192, 192],
        [stat, field, zlow, zhigh, xlow, xhigh, ylow, yhigh, total, coef1, scale1, total1],
        scratch=[s.grown_rows() for s in FINE[1:]] + [96],
    )

    zlow, zhigh = both_ways("gz", zup, zdown)
    coef1, right1, side_coef, side_right, side_total, xup, xdown = call(
        middle_x, "middle_x", [288, 48, 288, 48, 48, x_rows(MIDDLE), x_rows(MIDDLE)], [middle, field2, zlow, zhigh]
    )
    xlow, xhigh = both_ways("gx", xup, xdown)
    level1 = [coef1, right1, field2, zlow, zhigh, side_coef, side_right]
    yup, ydown = call(middle_y, "middle_y", [y_rows(MIDDLE)] * 2, [*level1, xlow, xhigh])
    ylow, yhigh = both_ways("gy", yup, ydown)
    right1, field2, sides2, error1, packed, coef1 = call(
        middle_sweeps, "middle_sweeps", [s.grown_rows() for s in MIDDLE[1:4]] + [480, gx * gy * 8],
        [*level1, xlow, xhigh, ylow, yhigh, total1, side_total],
        far_outs=[FAR], scratch=[MIDDLE[i].grown_rows() for i in (0, 3, 4, 5, 6)] + [32, 32, 16], copies=1,
    )
    packed = to_all(packed, gx * gy)

    rows = sum(coarse_parts(gx, gy)[-1])
    (table,) = call(
        lambda *refs: coarse_coefs(gx, gy, *refs), "coarse_coefs", [], [shared], far_outs=[FAR], scratch=[rows], copies=1
    )

    vmem = pl.BlockSpec(memory_space=pltpu.VMEM)
    far = pl.BlockSpec(memory_space=pltpu.HBM)
    near = [packed, error1, right1, stat, sides0, field2, sides2]
    scratch = [rows, MIDDLE[0].grown_rows(), 12 * gx * gy, (2 * gx + 4) * 6 * (gy + 16), 144, 288, 144, 576]
    return pl.pallas_call(
        lambda *refs: finish(gx, gy, *refs),
        name="finish",
        out_shape=jax.ShapeDtypeStruct(guess.shape, F32),
        in_specs=[far] * 2 + [vmem] * len(near),
        out_specs=vmem,
        scratch_shapes=[pltpu.VMEM((rows, LANES), F32) for rows in scratch] + [pltpu.SemaphoreType.DMA((7,))],
        compiler_params=pltpu.CompilerParams(vmem_limit_bytes=GRANT),
    )(table, coef1, *near)


def solution(mesh):
    spec = P(None, "gx", "gy", "gz")
    return jax.shard_map(per_device, mesh=mesh, in_specs=(spec,) * 4, out_specs=spec, check_vma=False)
```

```python
import jax
import jax.numpy as jnp
from jax import lax
from jax.experimental import pallas as pl
from jax.experimental.pallas import tpu as pltpu
from jax.sharding import PartitionSpec as P


F32 = jnp.float32
LANES = 128
GRANT = 40 * 1024 * 1024
FAR = 49152
STATIC = 21
WIDE = 42
HALO2 = 20
SHARED = 64
MEANS = 84


def rolled(value, shift, axis):
    shift %= value.shape[axis]
    return value if shift == 0 else pltpu.roll(value, shift, axis)


def lanes_of(rows):
    return lax.broadcasted_iota(jnp.int32, (rows, LANES), 1)


def pair_matrix(weight):
    fine = lax.broadcasted_iota(jnp.int32, (LANES, LANES), 0)
    coarse = lax.broadcasted_iota(jnp.int32, (LANES, LANES), 1)
    return jnp.where((fine >> 1) == coarse, F32(weight), F32(0))


def exact_dot(left, right):
    return jnp.dot(left, right, precision=lax.Precision.HIGHEST, preferred_element_type=F32)


def call(body, name, outs, args, scratch=(), far_args=(), far_outs=(), copies=0, grant=GRANT):
    vmem = pl.BlockSpec(memory_space=pltpu.VMEM)
    far = pl.BlockSpec(memory_space=pltpu.HBM)
    semaphores = [pltpu.SemaphoreType.DMA((copies,))] if copies else []
    return pl.pallas_call(
        body,
        name=name,
        out_shape=[jax.ShapeDtypeStruct((rows, LANES), F32) for rows in (*outs, *far_outs)],
        in_specs=[far] * len(far_args) + [vmem] * len(args),
        out_specs=[vmem] * len(outs) + [far] * len(far_outs),
        scratch_shapes=[pltpu.VMEM(r if isinstance(r, tuple) else (r, LANES), F32) for r in scratch] + semaphores,
        compiler_params=pltpu.CompilerParams(vmem_limit_bytes=grant),
    )(*far_args, *args)


class Stream:
    def __init__(self, count, rows, planes, halo, reach):
        self.count, self.rows, self.planes, self.halo, self.reach = count, rows, planes, halo, reach

    def extent(self, depth):
        return self.reach - depth

    def halo_rows(self):
        return self.halo * self.count * self.rows

    def grown_rows(self):
        return (self.planes + 2 * self.halo) * self.count * 16


FINE = [Stream(STATIC, 8, 8, 2, 2), Stream(3, 8, 8, 3, 3), Stream(1, 8, 8, 3, 3)]
MIDDLE = [Stream(18, 4, 4, 3, 4), Stream(3, 4, 4, 4, 5), Stream(3, 8, 8, 2, 2), Stream(1, 8, 8, 2, 2)]
MIDDLE += [Stream(18, 4, 4, 1, 1), Stream(3, 4, 4, 2, 2)]


def x_rows(streams):
    return sum(s.halo_rows() for s in streams)


def y_pieces(streams):
    offset = 0
    pieces = []
    for index, s in enumerate(streams):
        for depth in range(1, 1 + s.halo):
            pieces.append((index, depth, offset))
            offset += (s.planes + 2 * s.extent(depth)) * s.count
    return pieces, offset


def y_rows(streams):
    total = y_pieces(streams)[1]
    return -(-total // 8) * 8


def pack_x(streams, mains, up, down):
    offset = 0
    for s, main in zip(streams, mains):
        size = s.halo_rows()
        whole = s.planes * s.count * s.rows
        up[pl.ds(offset, size), :] = main[pl.ds(whole - size, size), :]
        down[pl.ds(offset, size), :] = main[pl.ds(0, size), :]
        offset += size


def pack_y(streams, mains, low, high, up, down):
    starts = [sum(s.halo_rows() for s in streams[:i]) for i in range(len(streams))]
    pieces, total = y_pieces(streams)
    padded = y_rows(streams)
    for out, upward in ((up, True), (down, False)):
        if padded > total:
            out[pl.ds(padded - 8, 8), :] = jnp.zeros((8, LANES), F32)
        for index, depth, offset in pieces:
            s = streams[index]
            row = s.rows - depth if upward else depth - 1
            beyond = s.extent(depth)
            side = beyond * s.count
            middle = s.planes * s.count
            if beyond:
                first = starts[index] + (s.halo - beyond) * s.count * s.rows + row
                out[pl.ds(offset, side), :] = low[pl.ds(first, side, s.rows), :]
            out[pl.ds(offset + side, middle), :] = mains[index][pl.ds(row, middle, s.rows), :]
            if beyond:
                out[pl.ds(offset + side + middle, side), :] = high[pl.ds(starts[index] + row, side, s.rows), :]


def grow(streams, mains, low, high, below, above, grown):
    starts = [sum(s.halo_rows() for s in streams[:i]) for i in range(len(streams))]
    for index, s in enumerate(streams):
        out = grown[index]
        out[...] = jnp.zeros(out.shape, F32)
        edge = s.halo * s.count
        middle = s.planes * s.count
        for source, base, first, number in (
            (low, starts[index], 0, edge),
            (mains[index], 0, edge, middle),
            (high, starts[index], edge + middle, edge),
        ):
            if s.rows == 8:
                for tile in range(number):
                    out[pl.ds((first + tile) * 16, 8), :] = source[pl.ds(base + tile * 8, 8), :]
            else:
                for row in range(s.rows):
                    out[pl.ds(first * 16 + row, number, 16), :] = source[pl.ds(base + row, number, s.rows), :]
    for index, depth, offset in y_pieces(streams)[0]:
        s = streams[index]
        beyond = s.extent(depth)
        number = (s.planes + 2 * beyond) * s.count
        first = (s.halo - beyond) * s.count * 16
        grown[index][pl.ds(first + s.rows + depth - 1, number, 16), :] = above[pl.ds(offset, number), :]
        grown[index][pl.ds(first + 16 - depth, number, 16), :] = below[pl.ds(offset, number), :]


def prepare(c, d, b, g, stat, field, total, zup, zdown, coef1, scale1, total1, summed, means1, half2, sum2, sum3):
    lane = lanes_of(8)
    for x in range(8):
        up = jnp.zeros((8, LANES), F32)
        down = jnp.zeros((8, LANES), F32)
        packed = []
        for e in range(3):
            w = [c[6 * e + k, x] for k in range(6)]
            tot = d[e, x] + (((w[0] + w[1]) + (w[2] + w[3])) + (w[4] + w[5]))
            inverse = 0.8 / tot
            for k in range(6):
                packed.append((6 * e + k, w[k] * inverse))
            packed.append((18 + e, b[e, x] * inverse))
            field[pl.ds((x * 3 + e) * 8, 8), :] = g[e, x]
            total[pl.ds((x * 3 + e) * 8, 8), :] = tot * 1.25
        for a, value in packed:
            stat[pl.ds((x * STATIC + a) * 8, 8), :] = value
            inside = (lane >= 2 * a) & (lane < 2 * a + 2)
            up = jnp.where(inside, rolled(value, 2 * a + 2, 1), up)
            down = jnp.where(inside, rolled(value, 2 * a, 1), down)
        for e in range(3):
            base = 42 + 3 * e
            inside = (lane >= base) & (lane < base + 3)
            up = jnp.where(inside, rolled(g[e, x], base + 3, 1), up)
            down = jnp.where(inside, rolled(g[e, x], base, 1), down)
        zup[pl.ds(x * 8, 8), :] = up
        zdown[pl.ds(x * 8, 8), :] = down

    halve = pair_matrix(0.125)
    for x in range(4):
        for a in range(STATIC):
            one = c[a, 2 * x] + c[a, 2 * x + 1] if a < 18 else d[a - 18, 2 * x] + d[a - 18, 2 * x + 1]
            summed[pl.ds((x * STATIC + a) * 8, 8), :] = one
    means1[...] = exact_dot(summed[pl.ds(0, 336, 2), :] + summed[pl.ds(1, 336, 2), :], halve)
    for x in range(4):
        for e in range(3):
            w = [0.25 * means1[pl.ds((x * STATIC + 6 * e + k) * 4, 4), :] for k in range(6)]
            tot = means1[pl.ds((x * STATIC + 18 + e) * 4, 4), :] + (((w[0] + w[1]) + (w[2] + w[3])) + (w[4] + w[5]))
            tot = jnp.where(tot > 0, tot, F32(1))
            inverse = 0.8 / tot
            for k in range(6):
                coef1[pl.ds((x * 18 + 6 * e + k) * 4, 4), :] = w[k] * inverse
            scale1[pl.ds((x * 3 + e) * 4, 4), :] = inverse
            total1[pl.ds((x * 3 + e) * 4, 4), :] = tot * 1.25
    half2[...] = means1[pl.ds(0, 168, 2), :] + means1[pl.ds(1, 168, 2), :]
    for i in range(2):
        sum2[pl.ds(42 * i, 42), :] = half2[pl.ds(84 * i, 42), :] + half2[pl.ds(84 * i + 42, 42), :]
    sum2[pl.ds(0, MEANS), :] = exact_dot(sum2[...], halve)[:MEANS]
    sum3[pl.ds(0, 42), :] = sum2[pl.ds(0, 42), :] + sum2[pl.ds(42, 42), :]
    sum3[pl.ds(42, 6), :] = jnp.zeros((6, LANES), F32)
    means3 = exact_dot(sum3[pl.ds(0, 24, 2), :] + sum3[pl.ds(1, 24, 2), :], halve)
    sum2[pl.ds(0, STATIC), :] = sum2[pl.ds(0, STATIC), :] + rolled(means3, 32, 1)[:STATIC]
    zup[pl.ds(64, MEANS), :] = sum2[pl.ds(0, MEANS), :]
    zdown[pl.ds(64, MEANS), :] = sum2[pl.ds(0, MEANS), :]


def prepare_whole(inputs, stat, field, total, zup, zdown, coef1, scale1, total1, summed, means1, half2, sum2, sum3):
    sum2[pl.ds(80, 8), :] = jnp.zeros((8, LANES), F32)
    for out in (zup, zdown):
        out[pl.ds(144, 8), :] = jnp.zeros((8, LANES), F32)
    c, d, b, g = (inputs.at[pl.ds(first, number)] for first, number in ((0, 18), (18, 3), (21, 3), (24, 3)))
    prepare(c, d, b, g, stat, field, total, zup, zdown, coef1, scale1, total1, summed, means1, half2, sum2, sum3)


Z_ROWS = 152


def both_sides(zlow, zhigh, side):
    rows = pl.ds(0, 64)
    side[...] = jnp.where(lanes_of(64) < 64, zhigh[rows, :], rolled(zlow[rows, :], 64, 1))


def fine_x(stat, field, zlow, zhigh, side, up, down):
    both_sides(zlow, zhigh, side)
    pack_x(FINE, [stat, field, side], up, down)


def share(zlow, zhigh, zown, shared, wide):
    lane = lanes_of(MEANS)
    low, own, high = (ref[pl.ds(64, MEANS), :] for ref in (zlow, zown, zhigh))
    value = jnp.zeros((MEANS, LANES), F32)
    for source, shift, first, last in (
        (low, -12, 0, 20),
        (own, 20, 20, 52),
        (high, 52, 52, 72),
        (low, 34, 72, 82),
        (own, 50, 82, 98),
        (high, 66, 98, 108),
    ):
        value = jnp.where((lane >= first) & (lane < last), rolled(source, shift, 1), value)
    wide[pl.ds(80, 16), :] = jnp.zeros((16, LANES), F32)
    wide[pl.ds(0, MEANS), :] = value
    lane = lanes_of(48)
    body = jnp.where(lane < 64, wide[pl.ds(0, 48), :], rolled(wide[pl.ds(42, 48), :], 64, 1))
    lane = lanes_of(8)
    tail = jnp.zeros((8, LANES), F32)
    third = jnp.zeros((8, LANES), F32)
    for group in range(11):
        value = wide[pl.ds(8 * group, 8), :]
        inside = (lane >= 8 * group) & (lane < 8 * group + 8)
        tail = jnp.where(inside, rolled(value, 8 * group - 64, 1), tail)
        if group < 3:
            inside = (lane >= 36 * group) & (lane < 36 * group + 36)
            third = jnp.where(inside, rolled(value, 36 * group - 72, 1), third)
    shared[pl.ds(0, 48), :] = body
    shared[pl.ds(48, 8), :] = tail
    shared[pl.ds(56, 8), :] = third


def fine_y(stat, field, side, low, high, up, down):
    pack_y(FINE, [stat, field, side], low, high, up, down)


def z_near(tiles):
    if len(tiles) == 1:
        return [rolled(tiles[0], -1, 1)], [rolled(tiles[0], 1, 1)]
    lane = lanes_of(tiles[0].shape[0])
    ahead = [rolled(t, -1, 1) for t in tiles]
    behind = [rolled(t, 1, 1) for t in tiles]
    last, first = lane == LANES - 1, lane == 0
    plus = [jnp.where(last, ahead[1], ahead[0]), jnp.where(last, ahead[0], ahead[1])]
    minus = [jnp.where(first, behind[1], behind[0]), jnp.where(first, behind[0], behind[1])]
    return plus, minus


def swept(x, value, coef, tiles):
    plus, minus = z_near(value[x])
    out = []
    for t in range(tiles):
        v = value[x][t]
        near = [value[x + 1][t], value[x - 1][t], rolled(v, -1, 0), rolled(v, 1, 0), plus[t], minus[t]]
        terms = [coef(x, k, t) * near[k] for k in range(6)]
        out.append((0.2 * v + coef(x, 6, t)) + (((terms[0] + terms[1]) + (terms[2] + terms[3])) + (terms[4] + terms[5])))
    return out


def side_tile(sides, row, base, width):
    lane = lanes_of(16)
    packed = sides[pl.ds(row, 16), :]
    high = rolled(packed, -base, 1)
    low = rolled(packed, -width - base - 64, 1)
    return jnp.where(lane < width, high, jnp.where(lane >= LANES - width, low, F32(0)))


def fine_coef(stat, sides, e):
    cache = {}

    def coef(x, k, t):
        a = 6 * e + k if k < 6 else 18 + e
        if t == 0:
            return stat[pl.ds(((x + 2) * STATIC + a) * 16, 16), :]
        if (x, k) not in cache:
            cache[x, k] = side_tile(sides, (x + 3) * 16, 2 * a, 2)
        return cache[x, k]

    return coef


def fine_sweeps(stat0, field0, side0, low, high, below, above, total, coef1, scale1, total1,
                stat, sides, field2, middle, zup, zdown, field, sums):
    grow(FINE, [stat0, field0, side0], low, high, below, above, [stat, field, sides])
    for e in range(3):
        coef = fine_coef(stat, sides, e)
        value = {}
        for x in range(-3, 11):
            value[x] = [
                field[pl.ds(((x + 3) * 3 + e) * 16, 16), :],
                side_tile(sides, (x + 3) * 16, 42 + 3 * e, 3),
            ]
        value = {x: swept(x, value, coef, 2) for x in range(-2, 10)}
        value = {x: swept(x, value, coef, 2) for x in range(-1, 9)}
        resid = []
        for x in range(8):
            now = value[x][0]
            field2[pl.ds((x * 3 + e) * 8, 8), :] = now[:8]
            change = swept(x, value, coef, 1)[0] - now
            resid.append(change[:8] * total[pl.ds((x * 3 + e) * 8, 8), :])
        for x in range(4):
            sums[pl.ds((x * 3 + e) * 8, 8), :] = resid[2 * x] + resid[2 * x + 1]
    right = exact_dot(sums[pl.ds(0, 48, 2), :] + sums[pl.ds(1, 48, 2), :], pair_matrix(0.125))
    middle[pl.ds(0, 288), :] = coef1[...]
    middle[pl.ds(288, 48), :] = right * scale1[...]
    middle[pl.ds(336, 48), :] = total1[...]
    lane = lanes_of(128)
    up = jnp.zeros((128, LANES), F32)
    down = jnp.zeros((128, LANES), F32)
    for group in range(3):
        value = middle[pl.ds(128 * group, 128), :]
        inside = (lane >= WIDE * group) & (lane < WIDE * group + WIDE)
        up = jnp.where(inside, rolled(value, WIDE * group + WIDE - 64, 1), up)
        down = jnp.where(inside, rolled(value, WIDE * group, 1), down)
    zup[pl.ds(64, 128), :] = up
    zdown[pl.ds(64, 128), :] = down
    lane = lanes_of(8)
    for x in range(8):
        up = jnp.zeros((8, LANES), F32)
        down = jnp.zeros((8, LANES), F32)
        for e in range(3):
            value = field2[pl.ds((x * 3 + e) * 8, 8), :]
            inside = (lane >= 2 * e) & (lane < 2 * e + 2)
            up = jnp.where(inside, rolled(value, 2 * e + 2, 1), up)
            down = jnp.where(inside, rolled(value, 2 * e, 1), down)
        zup[pl.ds(x * 8, 8), :] = up
        zdown[pl.ds(x * 8, 8), :] = down


def middle_x(middle, field, zlow, zhigh, coef, right, side, side_coef, side_right, side_total, up, down, up_full, down_full):
    lane = lanes_of(128)
    low, high = zlow[pl.ds(64, 128), :], zhigh[pl.ds(64, 128), :]
    for group in range(3):
        own = middle[pl.ds(128 * group, 128), :]
        main = jnp.where((lane >= 64) & (lane < 68), rolled(high, 64 - WIDE * group, 1), own)
        main = jnp.where(lane >= 124, rolled(low, 128 - WIDE - WIDE * group, 1), main)
        wide = jnp.where(lane < 2, rolled(own, -62, 1), F32(0))
        wide = jnp.where((lane >= 2) & (lane < 2 + WIDE), rolled(high, 2 - WIDE * group, 1), wide)
        wide = jnp.where((lane >= 64) & (lane < 64 + WIDE), rolled(low, 64 - WIDE * group, 1), wide)
        wide = jnp.where((lane >= 106) & (lane < 108), rolled(own, 106, 1), wide)
        if group < 2:
            coef[pl.ds(128 * group, 128), :] = main
            side_coef[pl.ds(128 * group, 128), :] = wide
        else:
            coef[pl.ds(256, 32), :] = main[:32]
            side_coef[pl.ds(256, 32), :] = wide[:32]
            right[...] = main[32:80]
            side_right[...] = wide[32:80]
            side_total[...] = wide[80:]
    both_sides(zlow, zhigh, side)
    pack_x(MIDDLE, [coef, right, field, side, side_coef, side_right], up_full, down_full)
    squeeze(X_SQUEEZE, up_full, up)
    squeeze(X_SQUEEZE, down_full, down)


X_SQUEEZE = (216, 112, 16)
Y_SQUEEZE = (432, 216, 32)


def squeezed(total, plan):
    return total - plan[0] + plan[1] + plan[2]


def squeeze(plan, full, out):
    number, half, size = plan
    lane = lanes_of(half)
    out[pl.ds(0, half), :] = jnp.where(lane < 64, full[pl.ds(0, half), :], rolled(full[pl.ds(half, half), :], 64, 1))
    lane = lanes_of(size)
    tail = jnp.zeros((size, LANES), F32)
    for group in range(-(-number // size)):
        value = full[pl.ds(group * size, size), :]
        at = 8 * group
        tail = jnp.where((lane >= at) & (lane < at + 4), rolled(value, at - 64, 1), tail)
        tail = jnp.where((lane >= at + 4) & (lane < at + 8), rolled(value, at + 4 - 124, 1), tail)
    out[pl.ds(half, size), :] = tail
    rest = full.shape[0] - number
    out[pl.ds(half + size, rest), :] = full[pl.ds(number, rest), :]


def unsqueeze(plan, packed, full):
    number, half, size = plan
    lane = lanes_of(half)
    both = packed[pl.ds(0, half), :]
    full[pl.ds(0, half), :] = jnp.where(lane < 64, both, F32(0))
    full[pl.ds(half, number - half), :] = jnp.where(lane < 64, rolled(both, 64, 1), F32(0))[: number - half]
    for group in range(-(-number // size)):
        at = 8 * group
        rows = min(size, number - group * size)
        tail = packed[pl.ds(half, rows), :]
        lane = lanes_of(rows)
        value = full[pl.ds(group * size, rows), :]
        value = jnp.where((lane >= 64) & (lane < 68), rolled(tail, 64 - at, 1), value)
        value = jnp.where(lane >= 124, rolled(tail, 124 - at - 4, 1), value)
        full[pl.ds(group * size, rows), :] = value
    rest = full.shape[0] - number
    full[pl.ds(number, rest), :] = packed[pl.ds(half + size, rest), :]


def middle_y(coef, right, field, side, side_coef, side_right, low_packed, high_packed, low, high, up, down, up_full, down_full):
    unsqueeze(X_SQUEEZE, low_packed, low)
    unsqueeze(X_SQUEEZE, high_packed, high)
    pack_y(MIDDLE, [coef, right, field, side, side_coef, side_right], low, high, up_full, down_full)
    squeeze(Y_SQUEEZE, up_full, up)
    squeeze(Y_SQUEEZE, down_full, down)


def middle_coef(coef, right, e):
    def get(x, k, t):
        if k < 6:
            return coef[pl.ds(((x + 3) * 18 + 6 * e + k) * 16, 16), :]
        return right[pl.ds(((x + 4) * 3 + e) * 16, 16), :]

    return get


def middle_sweeps(coef0, right0, field0, side0, side_coef0, side_right0, low, high, below_packed, above_packed, total1, side_total,
                  right, field, sides, error, packed, coef_far, coef, side_coef, side_right, sums, side_sums, wide,
                  below, above, left):
    unsqueeze(Y_SQUEEZE, below_packed, below)
    unsqueeze(Y_SQUEEZE, above_packed, above)
    grow(MIDDLE, [coef0, right0, field0, side0, side_coef0, side_right0], low, high, below, above,
         [coef, right, field, sides, side_coef, side_right])
    inner = pl.ds(18 * 16, 8 * 18 * 16)
    keep = pltpu.make_async_copy(coef.at[inner, :], coef_far.at[inner, :], left.at[0])
    keep.start()
    for e in range(3):

        def side_get(x, k, t):
            if k < 6:
                return side_coef[pl.ds(((x + 1) * 18 + 6 * e + k) * 16, 16), :]
            return side_right[pl.ds(((x + 2) * 3 + e) * 16, 16), :]

        get = middle_coef(coef, right, e)
        value = {x: swept(x, {y: [get(y, 6, 0)] for y in (x - 1, x, x + 1)}, get, 1) for x in range(-3, 7)}
        for x in range(-3, 7):
            error[pl.ds(((x + 3) * 3 + e) * 16, 16), :] = value[x][0]
        beside = {x: swept(x, {y: [side_get(y, 6, 0)] for y in (x - 1, x, x + 1)}, side_get, 1) for x in range(-1, 5)}
        for known, coef_of, weight, out in ((value, get, total1, sums), (beside, side_get, side_total, side_sums)):
            resid = []
            for x in range(4):
                change = swept(x, known, coef_of, 1)[0] - known[x][0]
                resid.append(change[:4] * weight[pl.ds((x * 3 + e) * 4, 4), :])
            for i in range(2):
                out[pl.ds((i * 3 + e) * 4, 4), :] = resid[2 * i] + resid[2 * i + 1]
    sums[pl.ds(24, 8), :] = jnp.zeros((8, LANES), F32)
    side_sums[pl.ds(24, 8), :] = jnp.zeros((8, LANES), F32)
    fine = lax.broadcasted_iota(jnp.int32, (LANES, LANES), 0)
    coarse = lax.broadcasted_iota(jnp.int32, (LANES, LANES), 1)
    own = (fine < 64) & ((fine >> 1) + HALO2 == coarse)
    above_own = (fine >= 2) & (fine < 42) & ((fine >> 1) + 51 == coarse)
    below_own = (fine >= 66) & (fine < 106) & ((fine >> 1) - 33 == coarse)
    wide[...] = exact_dot(
        sums[pl.ds(0, 16, 2), :] + sums[pl.ds(1, 16, 2), :], jnp.where(own, F32(0.125), F32(0))
    ) + exact_dot(
        side_sums[pl.ds(0, 16, 2), :] + side_sums[pl.ds(1, 16, 2), :],
        jnp.where(above_own | below_own, F32(0.125), F32(0)),
    )
    spread(wide, packed)
    keep.wait()


def spread(wide, out):
    lane = lanes_of(8)
    first, second = wide[pl.ds(0, 8), :], wide[pl.ds(6, 8), :]
    block = jnp.where(lane < 64, first, rolled(second, 64, 1))
    tail = jnp.zeros((1, LANES), F32)
    lane = lanes_of(1)
    for row in range(12):
        inside = (lane >= 8 * row) & (lane < 8 * row + 8)
        tail = jnp.where(inside, rolled(wide[pl.ds(row, 1), :], 8 * row - 64, 1), tail)
    rows = lax.broadcasted_iota(jnp.int32, (8, LANES), 0)
    block = jnp.where(rows < 6, block, jnp.where(rows == 6, jnp.broadcast_to(tail, (8, LANES)), F32(0)))
    for copy in range(out.shape[0] // 8):
        out[pl.ds(copy * 8, 8), :] = block


def coarse_parts(gx, gy):
    each = 4 * gx * gy
    sizes = [3 * each, 3 * each, 6 * each, 6 * each, 6 * each, 21 * gx * gy]
    return [(sum(sizes[:i]), size) for i, size in enumerate(sizes)]


def coarse_coefs(gx, gy, shared, table_far, table, left):
    (scale_at, _), (total_at, _), (coef_at, _), _, _, (coef3_at, size3) = coarse_parts(gx, gy)
    lane = lanes_of(gy)
    used = lane < 72
    for g in range(gx):

        def rows(r):
            return shared[pl.ds(g * gy * SHARED + r, gy, SHARED), :]

        tails = [rows(48 + r) for r in range(8)]
        thirds = [rows(56 + r) for r in range(8)]

        def settle(w, d):
            tot = d + (((w[0] + w[1]) + (w[2] + w[3])) + (w[4] + w[5]))
            tot = jnp.where(tot > 0, tot, F32(1))
            return tot, 0.8 / tot

        for e in range(3):
            for j in range(2):
                pairs = {a: rows(a * 2 + j) for a in [6 * e + k for k in range(6)] + [18 + e]}
                for i in range(2):

                    def mean(a):
                        r = i * 42 + a * 2 + j
                        value = pairs[a] if i == 0 else rolled(pairs[a], 64, 1)
                        value = jnp.where(lane < 64, value, rolled(tails[r % 8], 64 - 8 * (r // 8), 1))
                        return jnp.where(used, value, F32(0))

                    w = [mean(6 * e + k) * 0.0625 for k in range(6)]
                    tot, inverse = settle(w, mean(18 + e))
                    base = (e * 2 * gx + 2 * g + i) * 2 + j
                    for k in range(6):
                        table[pl.ds(coef_at + (base * 6 + k) * gy, gy), :] = w[k] * inverse
                    table[pl.ds(scale_at + base * gy, gy), :] = inverse
                    table[pl.ds(total_at + base * gy, gy), :] = tot * 1.25

            def mean3(a):
                return jnp.where(lane < 36, rolled(thirds[a % 8], -36 * (a // 8), 1), F32(0))

            w = [mean3(6 * e + k) * 0.015625 for k in range(6)]
            tot, inverse = settle(w, mean3(18 + e))
            for k in range(6):
                table[pl.ds(coef3_at + ((g * 3 + e) * 7 + k) * gy, gy), :] = w[k] * inverse
            table[pl.ds(coef3_at + ((g * 3 + e) * 7 + 6) * gy, gy), :] = inverse
    keep = pltpu.make_async_copy(table, table_far.at[pl.ds(0, coef3_at + size3), :], left.at[0])
    keep.start()
    keep.wait()


def coarse_levels(gx, gy, me_x, me_y, packed, table, arrivals, right2, error2, rows6):
    planes = 2 * gx
    (scale_at, _), (total_at, _), (coef_at, _), _, _, (coef3_at, _) = coarse_parts(gx, gy)

    def place(x, e, j):
        return (e * 2 * gx + x) * 2 + j

    error2[...] = jnp.zeros(error2.shape, F32)
    arrivals[0].wait()
    lane = lanes_of(gy)
    used = lane < 72
    row = lax.broadcasted_iota(jnp.int32, (gy, LANES), 0)
    first_row, last_row = row == 0, row == gy - 1
    zero = jnp.zeros((gy, LANES), F32)

    for g in range(gx):
        blocks = [packed[pl.ds(g * gy * 8 + r, gy, 8), :] for r in range(7)]
        for i in range(2):
            for e in range(3):
                for j in range(2):
                    r = (i * 3 + e) * 2 + j
                    right = blocks[r] if r < 6 else rolled(blocks[r - 6], 64, 1)
                    right = jnp.where(lane < 64, right, rolled(blocks[6], 64 - 8 * r, 1))
                    base = place(2 * g + i, e, j) * gy
                    right2[pl.ds(base, gy), :] = jnp.where(used, right, F32(0)) * table[pl.ds(scale_at + base, gy), :]

    def sweep2(value, x, e, j):
        base = place(x, e, j)
        v = value[x, j]
        near = [
            value[x + 1, j] if x + 1 < planes else None,
            value[x - 1, j] if x > 0 else None,
            value[x, 1] if j == 0 else jnp.where(last_row, zero, rolled(value[x, 0], -1, 0)),
            value[x, 0] if j == 1 else jnp.where(first_row, zero, rolled(value[x, 1], 1, 0)),
            rolled(v, -1, 1),
            rolled(v, 1, 1),
        ]
        out = 0.2 * v + right2[pl.ds(base * gy, gy), :]
        for k in range(6):
            if near[k] is not None:
                out = out + table[pl.ds(coef_at + (base * 6 + k) * gy, gy), :] * near[k]
        return out

    cells = [(x, j) for x in range(planes) for j in range(2)]
    halve = pair_matrix(0.125)
    fine = lax.broadcasted_iota(jnp.int32, (LANES, LANES), 1)
    coarse = lax.broadcasted_iota(jnp.int32, (LANES, LANES), 0)
    double = jnp.where((fine >> 1) == coarse, F32(1), F32(0))
    before, sums = [], []
    for e in range(3):
        if e == 0:
            arrivals[1].wait()
        arrivals[2 + e].wait()
        value = {(x, j): right2[pl.ds(place(x, e, j) * gy, gy), :] for x, j in cells}
        value = {(x, j): sweep2(value, x, e, j) for x, j in cells}
        before.append(value)
        resid = {
            (x, j): (sweep2(value, x, e, j) - value[x, j]) * table[pl.ds(total_at + place(x, e, j) * gy, gy), :] for x, j in cells
        }
        for g in range(gx):
            sums.append(
                (resid[2 * g, 0] + resid[2 * g, 1]) + (resid[2 * g + 1, 0] + resid[2 * g + 1, 1])
            )
    arrivals[5].wait()
    right3 = exact_dot(jnp.concatenate(sums, axis=0), halve)
    found = []
    for e in range(3):

        def coef_of(g, k):
            return table[pl.ds(coef3_at + ((g * 3 + e) * 7 + k) * gy, gy), :]

        right = [right3[(e * gx + g) * gy : (e * gx + g + 1) * gy] * coef_of(g, 6) for g in range(gx)]
        value = right
        for step in range(7):
            new = []
            for g in range(gx):
                v = value[g]
                out = 0.2 * v + right[g]
                if g + 1 < gx:
                    out = out + coef_of(g, 0) * value[g + 1]
                if g > 0:
                    out = out + coef_of(g, 1) * value[g - 1]
                out = out + coef_of(g, 2) * jnp.where(last_row, zero, rolled(v, -1, 0))
                out = out + coef_of(g, 3) * jnp.where(first_row, zero, rolled(v, 1, 0))
                out = out + coef_of(g, 4) * rolled(v, -1, 1)
                out = out + coef_of(g, 5) * rolled(v, 1, 1)
                new.append(out)
            value = new
        found.extend(value)
    refined = exact_dot(jnp.concatenate(found, axis=0), double)
    for e in range(3):
        value = {
            (x, j): before[e][x, j] + refined[(e * gx + x // 2) * gy : (e * gx + x // 2 + 1) * gy] for x, j in cells
        }
        for step in range(2):
            value = {(x, j): sweep2(value, x, e, j) for x, j in cells}
        for x, j in cells:
            error2[pl.ds((((x + 2) * 3 + e) * 2 + j) * (gy + 16) + 8, gy), :] = value[x, j]
    for plane in range(6):
        for e in range(3):
            for step, j, target in ((0, 0, 0), (0, 1, 1), (1, 0, 2), (1, 1, 3), (-1, 0, 6), (-1, 1, 7)):
                start = (((2 * me_x + plane) * 3 + e) * 2 + j) * (gy + 16) + 8 + me_y + step
                rows6[pl.ds((plane * 3 + e) * 8 + target, 1), :] = error2[pl.ds(start, 1), :]
            rows6[pl.ds((plane * 3 + e) * 8 + 4, 2), :] = jnp.zeros((2, LANES), F32)


def finish(gx, gy, table_far, coef1_far, packed, error1, right1, stat, sides0, field2, sides2, out,
           table, coef1, right2, error2, rows6, fine2, rows1, fine1, arrived):
    inner = pl.ds(18 * 16, 8 * 18 * 16)
    pieces = [(table_far, table, pl.ds(first, size)) for first, size in coarse_parts(gx, gy)]
    pieces.append((coef1_far, coef1, inner))
    arrivals = [
        pltpu.make_async_copy(far.at[rows, :], near.at[rows, :], arrived.at[i])
        for i, (far, near, rows) in enumerate(pieces)
    ]
    for copy in arrivals:
        copy.start()
    me_x, me_y = lax.axis_index("gx"), lax.axis_index("gy")
    coarse_levels(gx, gy, me_x, me_y, packed, table, arrivals, right2, error2, rows6)
    arrivals[6].wait()

    source = lax.broadcasted_iota(jnp.int32, (LANES, LANES), 0)
    target = lax.broadcasted_iota(jnp.int32, (LANES, LANES), 1)
    cell = jnp.where(target >= 96, target - LANES, target)
    wanted = (cell >= -4) & (cell < 68) & ((cell >> 1) + HALO2 == source)
    widened = exact_dot(rows6[...], jnp.where(wanted, F32(1), F32(0)))
    fine2[pl.ds(0, 144, 2), :] = widened
    fine2[pl.ds(1, 144, 2), :] = widened

    row = lax.broadcasted_iota(jnp.int32, (8, LANES), 0)
    for e in range(3):
        get = middle_coef(coef1, right1, e)
        value = {}
        for x in range(-3, 7):
            value[x] = [
                error1[pl.ds(((x + 3) * 3 + e) * 16, 16), :] + fine2[pl.ds(((x // 2 + 2) * 3 + e) * 16, 16), :]
            ]
        value = {x: swept(x, value, get, 1) for x in range(-2, 6)}
        value = {x: swept(x, value, get, 1) for x in range(-1, 5)}
        for x in range(-1, 5):
            whole = value[x][0]
            rows1[pl.ds(((x + 1) * 3 + e) * 8, 8), :] = jnp.where(row == 7, whole[8:], whole[:8])

    inner = jnp.where((target >> 1) == source, F32(1), F32(0))
    outer = jnp.where((target < 2) & (source == 64), F32(1), F32(0))
    outer = jnp.where((target >= 126) & (source == 127), F32(1), outer)
    for tile, matrix in ((0, inner), (1, outer)):
        widened = exact_dot(rows1[...], matrix)
        fine1[pl.ds(288 * tile, 144, 2), :] = widened
        fine1[pl.ds(288 * tile + 1, 144, 2), :] = widened

    for e in range(3):
        get = fine_coef(stat, sides0, e)
        value = {}
        for x in range(-2, 10):
            start = ((x // 2 + 1) * 3 + e) * 16
            value[x] = [
                field2[pl.ds(((x + 2) * 3 + e) * 16, 16), :] + fine1[pl.ds(start, 16), :],
                side_tile(sides2, (x + 2) * 16, 2 * e, 2) + fine1[pl.ds(288 + start, 16), :],
            ]
        value = {x: swept(x, value, get, 2) for x in range(-1, 9)}
        for x in range(8):
            out[e, x] = swept(x, value, get, 1)[0][:8]


def both_ways(axis, up, down):
    devices = lax.axis_size(axis)
    pairs = [(i, i + 1) for i in range(devices - 1)]
    return lax.ppermute(up, axis, pairs), lax.ppermute(down, axis, [(b, a) for a, b in pairs])


def to_all(value, devices):
    blocks = value.reshape(devices, value.shape[0] // devices, LANES)
    return lax.all_to_all(blocks, ("gx", "gy"), 0, 0).reshape(value.shape)


def per_device(couplings, diagonal, right_side, guess):
    gx, gy = lax.axis_size("gx"), lax.axis_size("gy")
    inputs = jnp.concatenate([couplings, diagonal, right_side, guess])

    stat, field, total, zup, zdown, coef1, scale1, total1 = call(
        prepare_whole, "prepare", [1344, 192, 192, Z_ROWS, Z_ROWS, 288, 48, 48], [inputs], scratch=[672, 336, 168, 88, 48]
    )
    zlow, zhigh = both_ways("gz", zup, zdown)
    side, xup, xdown = call(fine_x, "fine_x", [64, x_rows(FINE), x_rows(FINE)], [stat, field, zlow, zhigh])
    (shared,) = call(share, "share", [SHARED], [zlow, zhigh, zup], scratch=[96])
    shared = lax.all_gather(shared, ("gx", "gy"), tiled=True)
    xlow, xhigh = both_ways("gx", xup, xdown)
    yup, ydown = call(fine_y, "fine_y", [y_rows(FINE)] * 2, [stat, field, side, xlow, xhigh])
    ylow, yhigh = both_ways("gy", yup, ydown)
    stat, sides0, field2, middle, zup, zdown = call(
        fine_sweeps, "fine_sweeps", [FINE[0].grown_rows(), FINE[2].grown_rows(), 192, 384, 192, 192],
        [stat, field, side, xlow, xhigh, ylow, yhigh, total, coef1, scale1, total1],
        scratch=[FINE[1].grown_rows(), 96],
    )

    zlow, zhigh = both_ways("gz", zup, zdown)
    x_full, y_full = x_rows(MIDDLE), y_rows(MIDDLE)
    x_sent, y_sent = squeezed(x_full, X_SQUEEZE), squeezed(y_full, Y_SQUEEZE)
    coef1, right1, side, side_coef, side_right, side_total, xup, xdown = call(
        middle_x, "middle_x", [288, 48, 64, 288, 48, 48, x_sent, x_sent], [middle, field2, zlow, zhigh], scratch=[x_full] * 2
    )
    xlow, xhigh = both_ways("gx", xup, xdown)
    level1 = [coef1, right1, field2, side, side_coef, side_right]
    xlow, xhigh, yup, ydown = call(
        middle_y, "middle_y", [x_full, x_full, y_sent, y_sent], [*level1, xlow, xhigh], scratch=[y_full] * 2
    )
    ylow, yhigh = both_ways("gy", yup, ydown)
    right1, field2, sides2, error1, packed, coef1 = call(
        middle_sweeps, "middle_sweeps", [s.grown_rows() for s in MIDDLE[1:4]] + [480, gx * gy * 8],
        [*level1, xlow, xhigh, ylow, yhigh, total1, side_total], far_outs=[FAR],
        scratch=[MIDDLE[i].grown_rows() for i in (0, 4, 5)] + [32, 32, 16, y_full, y_full], copies=1,
    )
    packed = to_all(packed, gx * gy)

    rows = sum(coarse_parts(gx, gy)[-1])
    (table,) = call(
        lambda *refs: coarse_coefs(gx, gy, *refs), "coarse_coefs", [], [shared], far_outs=[FAR], scratch=[rows], copies=1
    )

    vmem = pl.BlockSpec(memory_space=pltpu.VMEM)
    far = pl.BlockSpec(memory_space=pltpu.HBM)
    near = [packed, error1, right1, stat, sides0, field2, sides2]
    scratch = [rows, MIDDLE[0].grown_rows(), 12 * gx * gy, (2 * gx + 4) * 6 * (gy + 16), 144, 288, 144, 576]
    return pl.pallas_call(
        lambda *refs: finish(gx, gy, *refs),
        name="finish",
        out_shape=jax.ShapeDtypeStruct(guess.shape, F32),
        in_specs=[far] * 2 + [vmem] * len(near),
        out_specs=vmem,
        scratch_shapes=[pltpu.VMEM((rows, LANES), F32) for rows in scratch] + [pltpu.SemaphoreType.DMA((7,))],
        compiler_params=pltpu.CompilerParams(vmem_limit_bytes=GRANT),
    )(table, coef1, *near)


def solution(mesh):
    spec = P(None, "gx", "gy", "gz")
    return jax.shard_map(per_device, mesh=mesh, in_specs=(spec,) * 4, out_specs=spec, check_vma=False)
```

```python
import jax
import jax.numpy as jnp
from jax import lax
from jax.experimental import pallas as pl
from jax.experimental.pallas import tpu as pltpu
from jax.sharding import PartitionSpec as P


F32 = jnp.float32
LANES = 128
GRANT = 40 * 1024 * 1024
FAR = 49152
STATIC = 21
WIDE = 42
HALO2 = 20
SHARED = 64
MEANS = 84


def rolled(value, shift, axis):
    shift %= value.shape[axis]
    return value if shift == 0 else pltpu.roll(value, shift, axis)


def lanes_of(rows):
    return lax.broadcasted_iota(jnp.int32, (rows, LANES), 1)


def pair_matrix(weight):
    fine = lax.broadcasted_iota(jnp.int32, (LANES, LANES), 0)
    coarse = lax.broadcasted_iota(jnp.int32, (LANES, LANES), 1)
    return jnp.where((fine >> 1) == coarse, F32(weight), F32(0))


def exact_dot(left, right):
    return jnp.dot(left, right, precision=lax.Precision.HIGHEST, preferred_element_type=F32)


def call(body, name, outs, args, scratch=(), far_args=(), far_outs=(), copies=0, grant=GRANT):
    vmem = pl.BlockSpec(memory_space=pltpu.VMEM)
    far = pl.BlockSpec(memory_space=pltpu.HBM)
    semaphores = [pltpu.SemaphoreType.DMA((copies,))] if copies else []
    return pl.pallas_call(
        body,
        name=name,
        out_shape=[jax.ShapeDtypeStruct((rows, LANES), F32) for rows in (*outs, *far_outs)],
        in_specs=[far] * len(far_args) + [vmem] * len(args),
        out_specs=[vmem] * len(outs) + [far] * len(far_outs),
        scratch_shapes=[pltpu.VMEM(r if isinstance(r, tuple) else (r, LANES), F32) for r in scratch] + semaphores,
        compiler_params=pltpu.CompilerParams(vmem_limit_bytes=grant),
    )(*far_args, *args)


class Stream:
    def __init__(self, count, rows, planes, halo, reach):
        self.count, self.rows, self.planes, self.halo, self.reach = count, rows, planes, halo, reach

    def extent(self, depth):
        return self.reach - depth

    def halo_rows(self):
        return self.halo * self.count * self.rows

    def grown_rows(self):
        return (self.planes + 2 * self.halo) * self.count * 16


FINE = [Stream(STATIC, 8, 8, 2, 2), Stream(3, 8, 8, 3, 3), Stream(1, 8, 8, 3, 3)]
MIDDLE = [Stream(18, 4, 4, 3, 4), Stream(3, 4, 4, 4, 5), Stream(3, 8, 8, 2, 2), Stream(1, 8, 8, 2, 2)]
MIDDLE += [Stream(18, 4, 4, 1, 1), Stream(3, 4, 4, 2, 2)]


def x_rows(streams):
    return sum(s.halo_rows() for s in streams)


def y_pieces(streams):
    offset = 0
    pieces = []
    for index, s in enumerate(streams):
        for depth in range(1, 1 + s.halo):
            pieces.append((index, depth, offset))
            offset += (s.planes + 2 * s.extent(depth)) * s.count
    return pieces, offset


def y_rows(streams):
    total = y_pieces(streams)[1]
    return -(-total // 8) * 8


def pack_x(streams, mains, up, down):
    offset = 0
    for s, main in zip(streams, mains):
        size = s.halo_rows()
        whole = s.planes * s.count * s.rows
        up[pl.ds(offset, size), :] = main[pl.ds(whole - size, size), :]
        down[pl.ds(offset, size), :] = main[pl.ds(0, size), :]
        offset += size


def pack_y(streams, mains, low, high, up, down):
    starts = [sum(s.halo_rows() for s in streams[:i]) for i in range(len(streams))]
    pieces, total = y_pieces(streams)
    padded = y_rows(streams)
    for out, upward in ((up, True), (down, False)):
        if padded > total:
            out[pl.ds(padded - 8, 8), :] = jnp.zeros((8, LANES), F32)
        for index, depth, offset in pieces:
            s = streams[index]
            row = s.rows - depth if upward else depth - 1
            beyond = s.extent(depth)
            side = beyond * s.count
            middle = s.planes * s.count
            if beyond:
                first = starts[index] + (s.halo - beyond) * s.count * s.rows + row
                out[pl.ds(offset, side), :] = low[pl.ds(first, side, s.rows), :]
            out[pl.ds(offset + side, middle), :] = mains[index][pl.ds(row, middle, s.rows), :]
            if beyond:
                out[pl.ds(offset + side + middle, side), :] = high[pl.ds(starts[index] + row, side, s.rows), :]


def grow(streams, mains, low, high, below, above, grown):
    starts = [sum(s.halo_rows() for s in streams[:i]) for i in range(len(streams))]
    for index, s in enumerate(streams):
        out = grown[index]
        out[...] = jnp.zeros(out.shape, F32)
        edge = s.halo * s.count
        middle = s.planes * s.count
        for source, base, first, number in (
            (low, starts[index], 0, edge),
            (mains[index], 0, edge, middle),
            (high, starts[index], edge + middle, edge),
        ):
            if s.rows == 8:
                for tile in range(number):
                    out[pl.ds((first + tile) * 16, 8), :] = source[pl.ds(base + tile * 8, 8), :]
            else:
                for row in range(s.rows):
                    out[pl.ds(first * 16 + row, number, 16), :] = source[pl.ds(base + row, number, s.rows), :]
    for index, depth, offset in y_pieces(streams)[0]:
        s = streams[index]
        beyond = s.extent(depth)
        number = (s.planes + 2 * beyond) * s.count
        first = (s.halo - beyond) * s.count * 16
        grown[index][pl.ds(first + s.rows + depth - 1, number, 16), :] = above[pl.ds(offset, number), :]
        grown[index][pl.ds(first + 16 - depth, number, 16), :] = below[pl.ds(offset, number), :]


def prepare(c, d, b, g, stat, field, total, zup, zdown, coef1, scale1, total1, summed, means1, half2, sum2, sum3):
    lane = lanes_of(8)
    for x in range(8):
        up = jnp.zeros((8, LANES), F32)
        down = jnp.zeros((8, LANES), F32)
        packed = []
        for e in range(3):
            w = [c[6 * e + k, x] for k in range(6)]
            tot = d[e, x] + (((w[0] + w[1]) + (w[2] + w[3])) + (w[4] + w[5]))
            inverse = 0.8 / tot
            for k in range(6):
                packed.append((6 * e + k, w[k] * inverse))
            packed.append((18 + e, b[e, x] * inverse))
            field[pl.ds((x * 3 + e) * 8, 8), :] = g[e, x]
            total[pl.ds((x * 3 + e) * 8, 8), :] = tot * 1.25
        for a, value in packed:
            stat[pl.ds((x * STATIC + a) * 8, 8), :] = value
            inside = (lane >= 2 * a) & (lane < 2 * a + 2)
            up = jnp.where(inside, rolled(value, 2 * a + 2, 1), up)
            down = jnp.where(inside, rolled(value, 2 * a, 1), down)
        for e in range(3):
            base = 42 + 3 * e
            inside = (lane >= base) & (lane < base + 3)
            up = jnp.where(inside, rolled(g[e, x], base + 3, 1), up)
            down = jnp.where(inside, rolled(g[e, x], base, 1), down)
        zup[pl.ds(x * 8, 8), :] = up
        zdown[pl.ds(x * 8, 8), :] = down

    halve = pair_matrix(0.125)
    for x in range(4):
        for a in range(STATIC):
            one = c[a, 2 * x] + c[a, 2 * x + 1] if a < 18 else d[a - 18, 2 * x] + d[a - 18, 2 * x + 1]
            summed[pl.ds((x * STATIC + a) * 8, 8), :] = one
    means1[...] = exact_dot(summed[pl.ds(0, 336, 2), :] + summed[pl.ds(1, 336, 2), :], halve)
    for x in range(4):
        for e in range(3):
            w = [0.25 * means1[pl.ds((x * STATIC + 6 * e + k) * 4, 4), :] for k in range(6)]
            tot = means1[pl.ds((x * STATIC + 18 + e) * 4, 4), :] + (((w[0] + w[1]) + (w[2] + w[3])) + (w[4] + w[5]))
            tot = jnp.where(tot > 0, tot, F32(1))
            inverse = 0.8 / tot
            for k in range(6):
                coef1[pl.ds((x * 18 + 6 * e + k) * 4, 4), :] = w[k] * inverse
            scale1[pl.ds((x * 3 + e) * 4, 4), :] = inverse
            total1[pl.ds((x * 3 + e) * 4, 4), :] = tot * 1.25
    half2[...] = means1[pl.ds(0, 168, 2), :] + means1[pl.ds(1, 168, 2), :]
    for i in range(2):
        sum2[pl.ds(42 * i, 42), :] = half2[pl.ds(84 * i, 42), :] + half2[pl.ds(84 * i + 42, 42), :]
    sum2[pl.ds(0, MEANS), :] = exact_dot(sum2[...], halve)[:MEANS]
    sum3[pl.ds(0, 42), :] = sum2[pl.ds(0, 42), :] + sum2[pl.ds(42, 42), :]
    sum3[pl.ds(42, 6), :] = jnp.zeros((6, LANES), F32)
    means3 = exact_dot(sum3[pl.ds(0, 24, 2), :] + sum3[pl.ds(1, 24, 2), :], halve)
    sum2[pl.ds(0, STATIC), :] = sum2[pl.ds(0, STATIC), :] + rolled(means3, 32, 1)[:STATIC]
    zup[pl.ds(64, MEANS), :] = sum2[pl.ds(0, MEANS), :]
    zdown[pl.ds(64, MEANS), :] = sum2[pl.ds(0, MEANS), :]


def prepare_whole(inputs, stat, field, total, zup, zdown, coef1, scale1, total1, summed, means1, half2, sum2, sum3):
    sum2[pl.ds(80, 8), :] = jnp.zeros((8, LANES), F32)
    for out in (zup, zdown):
        out[pl.ds(144, 8), :] = jnp.zeros((8, LANES), F32)
    c, d, b, g = (inputs.at[pl.ds(first, number)] for first, number in ((0, 18), (18, 3), (21, 3), (24, 3)))
    prepare(c, d, b, g, stat, field, total, zup, zdown, coef1, scale1, total1, summed, means1, half2, sum2, sum3)


Z_ROWS = 152


def both_sides(zlow, zhigh, side):
    rows = pl.ds(0, 64)
    side[...] = jnp.where(lanes_of(64) < 64, zhigh[rows, :], rolled(zlow[rows, :], 64, 1))


def fine_x(stat, field, zlow, zhigh, side, up, down):
    both_sides(zlow, zhigh, side)
    pack_x(FINE, [stat, field, side], up, down)


def share(zlow, zhigh, zown, shared, wide):
    lane = lanes_of(MEANS)
    low, own, high = (ref[pl.ds(64, MEANS), :] for ref in (zlow, zown, zhigh))
    value = jnp.zeros((MEANS, LANES), F32)
    for source, shift, first, last in (
        (low, -12, 0, 20),
        (own, 20, 20, 52),
        (high, 52, 52, 72),
        (low, 34, 72, 82),
        (own, 50, 82, 98),
        (high, 66, 98, 108),
    ):
        value = jnp.where((lane >= first) & (lane < last), rolled(source, shift, 1), value)
    wide[pl.ds(80, 16), :] = jnp.zeros((16, LANES), F32)
    wide[pl.ds(0, MEANS), :] = value
    lane = lanes_of(48)
    body = jnp.where(lane < 64, wide[pl.ds(0, 48), :], rolled(wide[pl.ds(42, 48), :], 64, 1))
    lane = lanes_of(8)
    tail = jnp.zeros((8, LANES), F32)
    third = jnp.zeros((8, LANES), F32)
    for group in range(11):
        value = wide[pl.ds(8 * group, 8), :]
        inside = (lane >= 8 * group) & (lane < 8 * group + 8)
        tail = jnp.where(inside, rolled(value, 8 * group - 64, 1), tail)
        if group < 3:
            inside = (lane >= 36 * group) & (lane < 36 * group + 36)
            third = jnp.where(inside, rolled(value, 36 * group - 72, 1), third)
    shared[pl.ds(0, 48), :] = body
    shared[pl.ds(48, 8), :] = tail
    shared[pl.ds(56, 8), :] = third


def fine_y(stat, field, side, low, high, up, down):
    pack_y(FINE, [stat, field, side], low, high, up, down)


def z_near(tiles):
    if len(tiles) == 1:
        return [rolled(tiles[0], -1, 1)], [rolled(tiles[0], 1, 1)]
    lane = lanes_of(tiles[0].shape[0])
    ahead = [rolled(t, -1, 1) for t in tiles]
    behind = [rolled(t, 1, 1) for t in tiles]
    last, first = lane == LANES - 1, lane == 0
    plus = [jnp.where(last, ahead[1], ahead[0]), jnp.where(last, ahead[0], ahead[1])]
    minus = [jnp.where(first, behind[1], behind[0]), jnp.where(first, behind[0], behind[1])]
    return plus, minus


def swept(x, value, coef, tiles):
    plus, minus = z_near(value[x])
    out = []
    for t in range(tiles):
        v = value[x][t]
        near = [value[x + 1][t], value[x - 1][t], rolled(v, -1, 0), rolled(v, 1, 0), plus[t], minus[t]]
        terms = [coef(x, k, t) * near[k] for k in range(6)]
        out.append((0.2 * v + coef(x, 6, t)) + (((terms[0] + terms[1]) + (terms[2] + terms[3])) + (terms[4] + terms[5])))
    return out


def side_tile(sides, row, base, width):
    lane = lanes_of(16)
    packed = sides[pl.ds(row, 16), :]
    high = rolled(packed, -base, 1)
    low = rolled(packed, -width - base - 64, 1)
    return jnp.where(lane < width, high, jnp.where(lane >= LANES - width, low, F32(0)))


def fine_coef(stat, sides, e):
    cache = {}

    def coef(x, k, t):
        a = 6 * e + k if k < 6 else 18 + e
        if t == 0:
            return stat[pl.ds(((x + 2) * STATIC + a) * 16, 16), :]
        if (x, k) not in cache:
            cache[x, k] = side_tile(sides, (x + 3) * 16, 2 * a, 2)
        return cache[x, k]

    return coef


def fine_sweeps(stat0, field0, side0, low, high, below, above, total, coef1, scale1, total1,
                stat, sides, field2, middle, zup, zdown, field, sums):
    grow(FINE, [stat0, field0, side0], low, high, below, above, [stat, field, sides])
    for e in range(3):
        coef = fine_coef(stat, sides, e)
        value = {}
        for x in range(-3, 11):
            value[x] = [
                field[pl.ds(((x + 3) * 3 + e) * 16, 16), :],
                side_tile(sides, (x + 3) * 16, 42 + 3 * e, 3),
            ]
        value = {x: swept(x, value, coef, 2) for x in range(-2, 10)}
        value = {x: swept(x, value, coef, 2) for x in range(-1, 9)}
        resid = []
        for x in range(8):
            now = value[x][0]
            field2[pl.ds((x * 3 + e) * 8, 8), :] = now[:8]
            change = swept(x, value, coef, 1)[0] - now
            resid.append(change[:8] * total[pl.ds((x * 3 + e) * 8, 8), :])
        for x in range(4):
            sums[pl.ds((x * 3 + e) * 8, 8), :] = resid[2 * x] + resid[2 * x + 1]
    right = exact_dot(sums[pl.ds(0, 48, 2), :] + sums[pl.ds(1, 48, 2), :], pair_matrix(0.125))
    middle[pl.ds(0, 288), :] = coef1[...]
    middle[pl.ds(288, 48), :] = right * scale1[...]
    middle[pl.ds(336, 48), :] = total1[...]
    lane = lanes_of(128)
    up = jnp.zeros((128, LANES), F32)
    down = jnp.zeros((128, LANES), F32)
    for group in range(3):
        value = middle[pl.ds(128 * group, 128), :]
        inside = (lane >= WIDE * group) & (lane < WIDE * group + WIDE)
        up = jnp.where(inside, rolled(value, WIDE * group + WIDE - 64, 1), up)
        down = jnp.where(inside, rolled(value, WIDE * group, 1), down)
    zup[pl.ds(64, 128), :] = up
    zdown[pl.ds(64, 128), :] = down
    lane = lanes_of(8)
    for x in range(8):
        up = jnp.zeros((8, LANES), F32)
        down = jnp.zeros((8, LANES), F32)
        for e in range(3):
            value = field2[pl.ds((x * 3 + e) * 8, 8), :]
            inside = (lane >= 2 * e) & (lane < 2 * e + 2)
            up = jnp.where(inside, rolled(value, 2 * e + 2, 1), up)
            down = jnp.where(inside, rolled(value, 2 * e, 1), down)
        zup[pl.ds(x * 8, 8), :] = up
        zdown[pl.ds(x * 8, 8), :] = down


def middle_x(middle, field, zlow, zhigh, coef, right, side, side_coef, side_right, side_total, up, down, up_full, down_full):
    lane = lanes_of(128)
    low, high = zlow[pl.ds(64, 128), :], zhigh[pl.ds(64, 128), :]
    for group in range(3):
        own = middle[pl.ds(128 * group, 128), :]
        main = jnp.where((lane >= 64) & (lane < 68), rolled(high, 64 - WIDE * group, 1), own)
        main = jnp.where(lane >= 124, rolled(low, 128 - WIDE - WIDE * group, 1), main)
        wide = jnp.where(lane < 2, rolled(own, -62, 1), F32(0))
        wide = jnp.where((lane >= 2) & (lane < 2 + WIDE), rolled(high, 2 - WIDE * group, 1), wide)
        wide = jnp.where((lane >= 64) & (lane < 64 + WIDE), rolled(low, 64 - WIDE * group, 1), wide)
        wide = jnp.where((lane >= 106) & (lane < 108), rolled(own, 106, 1), wide)
        if group < 2:
            coef[pl.ds(128 * group, 128), :] = main
            side_coef[pl.ds(128 * group, 128), :] = wide
        else:
            coef[pl.ds(256, 32), :] = main[:32]
            side_coef[pl.ds(256, 32), :] = wide[:32]
            right[...] = main[32:80]
            side_right[...] = wide[32:80]
            side_total[...] = wide[80:]
    both_sides(zlow, zhigh, side)
    pack_x(MIDDLE, [coef, right, field, side, side_coef, side_right], up_full, down_full)
    squeeze(X_SQUEEZE, up_full, up)
    squeeze(X_SQUEEZE, down_full, down)


X_SQUEEZE = (216, 112, 16)
Y_SQUEEZE = (432, 216, 32)


def squeezed(total, plan):
    return total - plan[0] + plan[1] + plan[2]


def squeeze(plan, full, out):
    number, half, size = plan
    lane = lanes_of(half)
    out[pl.ds(0, half), :] = jnp.where(lane < 64, full[pl.ds(0, half), :], rolled(full[pl.ds(half, half), :], 64, 1))
    lane = lanes_of(size)
    tail = jnp.zeros((size, LANES), F32)
    for group in range(-(-number // size)):
        value = full[pl.ds(group * size, size), :]
        at = 8 * group
        tail = jnp.where((lane >= at) & (lane < at + 4), rolled(value, at - 64, 1), tail)
        tail = jnp.where((lane >= at + 4) & (lane < at + 8), rolled(value, at + 4 - 124, 1), tail)
    out[pl.ds(half, size), :] = tail
    rest = full.shape[0] - number
    out[pl.ds(half + size, rest), :] = full[pl.ds(number, rest), :]


def unsqueeze(plan, packed, full):
    number, half, size = plan
    lane = lanes_of(half)
    both = packed[pl.ds(0, half), :]
    full[pl.ds(0, half), :] = jnp.where(lane < 64, both, F32(0))
    full[pl.ds(half, number - half), :] = jnp.where(lane < 64, rolled(both, 64, 1), F32(0))[: number - half]
    for group in range(-(-number // size)):
        at = 8 * group
        rows = min(size, number - group * size)
        tail = packed[pl.ds(half, rows), :]
        lane = lanes_of(rows)
        value = full[pl.ds(group * size, rows), :]
        value = jnp.where((lane >= 64) & (lane < 68), rolled(tail, 64 - at, 1), value)
        value = jnp.where(lane >= 124, rolled(tail, 124 - at - 4, 1), value)
        full[pl.ds(group * size, rows), :] = value
    rest = full.shape[0] - number
    full[pl.ds(number, rest), :] = packed[pl.ds(half + size, rest), :]


def middle_y(coef, right, field, side, side_coef, side_right, low_packed, high_packed, low, high, up, down, up_full, down_full):
    unsqueeze(X_SQUEEZE, low_packed, low)
    unsqueeze(X_SQUEEZE, high_packed, high)
    pack_y(MIDDLE, [coef, right, field, side, side_coef, side_right], low, high, up_full, down_full)
    squeeze(Y_SQUEEZE, up_full, up)
    squeeze(Y_SQUEEZE, down_full, down)


def middle_coef(coef, right, e):
    def get(x, k, t):
        if k < 6:
            return coef[pl.ds(((x + 3) * 18 + 6 * e + k) * 16, 16), :]
        return right[pl.ds(((x + 4) * 3 + e) * 16, 16), :]

    return get


def middle_sweeps(coef0, right0, field0, side0, side_coef0, side_right0, low, high, below_packed, above_packed, total1, side_total,
                  right, field, sides, error, packed, coef_far, coef, side_coef, side_right, sums, side_sums, wide,
                  below, above, left):
    unsqueeze(Y_SQUEEZE, below_packed, below)
    unsqueeze(Y_SQUEEZE, above_packed, above)
    grow(MIDDLE, [coef0, right0, field0, side0, side_coef0, side_right0], low, high, below, above,
         [coef, right, field, sides, side_coef, side_right])
    inner = pl.ds(18 * 16, 8 * 18 * 16)
    keep = pltpu.make_async_copy(coef.at[inner, :], coef_far.at[inner, :], left.at[0])
    keep.start()
    for e in range(3):

        def side_get(x, k, t):
            if k < 6:
                return side_coef[pl.ds(((x + 1) * 18 + 6 * e + k) * 16, 16), :]
            return side_right[pl.ds(((x + 2) * 3 + e) * 16, 16), :]

        get = middle_coef(coef, right, e)
        value = {x: swept(x, {y: [get(y, 6, 0)] for y in (x - 1, x, x + 1)}, get, 1) for x in range(-3, 7)}
        for x in range(-3, 7):
            error[pl.ds(((x + 3) * 3 + e) * 16, 16), :] = value[x][0]
        beside = {x: swept(x, {y: [side_get(y, 6, 0)] for y in (x - 1, x, x + 1)}, side_get, 1) for x in range(-1, 5)}
        for known, coef_of, weight, out in ((value, get, total1, sums), (beside, side_get, side_total, side_sums)):
            resid = []
            for x in range(4):
                change = swept(x, known, coef_of, 1)[0] - known[x][0]
                resid.append(change[:4] * weight[pl.ds((x * 3 + e) * 4, 4), :])
            for i in range(2):
                out[pl.ds((i * 3 + e) * 4, 4), :] = resid[2 * i] + resid[2 * i + 1]
    sums[pl.ds(24, 8), :] = jnp.zeros((8, LANES), F32)
    side_sums[pl.ds(24, 8), :] = jnp.zeros((8, LANES), F32)
    fine = lax.broadcasted_iota(jnp.int32, (LANES, LANES), 0)
    coarse = lax.broadcasted_iota(jnp.int32, (LANES, LANES), 1)
    own = (fine < 64) & ((fine >> 1) + HALO2 == coarse)
    above_own = (fine >= 2) & (fine < 42) & ((fine >> 1) + 51 == coarse)
    below_own = (fine >= 66) & (fine < 106) & ((fine >> 1) - 33 == coarse)
    wide[...] = exact_dot(
        sums[pl.ds(0, 16, 2), :] + sums[pl.ds(1, 16, 2), :], jnp.where(own, F32(0.125), F32(0))
    ) + exact_dot(
        side_sums[pl.ds(0, 16, 2), :] + side_sums[pl.ds(1, 16, 2), :],
        jnp.where(above_own | below_own, F32(0.125), F32(0)),
    )
    spread(wide, packed)
    keep.wait()


def spread(wide, out):
    lane = lanes_of(8)
    first, second = wide[pl.ds(0, 8), :], wide[pl.ds(6, 8), :]
    block = jnp.where(lane < 64, first, rolled(second, 64, 1))
    tail = jnp.zeros((1, LANES), F32)
    lane = lanes_of(1)
    for row in range(12):
        inside = (lane >= 8 * row) & (lane < 8 * row + 8)
        tail = jnp.where(inside, rolled(wide[pl.ds(row, 1), :], 8 * row - 64, 1), tail)
    rows = lax.broadcasted_iota(jnp.int32, (8, LANES), 0)
    block = jnp.where(rows < 6, block, jnp.where(rows == 6, jnp.broadcast_to(tail, (8, LANES)), F32(0)))
    for copy in range(out.shape[0] // 8):
        out[pl.ds(copy * 8, 8), :] = block


def coarse_parts(gx, gy):
    each = 4 * gx * gy
    sizes = [3 * each, 3 * each, 6 * each, 6 * each, 6 * each, 7 * gx * gy]
    return [(sum(sizes[:i]), size) for i, size in enumerate(sizes)]


def coarse_coefs(gx, gy, shared, table_far, table, left):
    parts = coarse_parts(gx, gy)
    (scale_at, _), (total_at, _), (coef_at, _), _, _, (coef3_at, _) = parts
    lane = lanes_of(gy)
    used = lane < 72
    keeps = [
        pltpu.make_async_copy(table.at[pl.ds(first, size), :], table_far.at[pl.ds(first, size), :], left.at[i])
        for i, (first, size) in enumerate(parts)
    ]

    def settle(w, d):
        tot = d + (((w[0] + w[1]) + (w[2] + w[3])) + (w[4] + w[5]))
        tot = jnp.where(tot > 0, tot, F32(1))
        return tot, 0.8 / tot

    def rows(g, r):
        return shared[pl.ds(g * gy * SHARED + r, gy, SHARED), :]

    for g in range(gx):
        thirds = [rows(g, 56 + r) for r in range(8)]
        mixed = [jnp.zeros((gy, LANES), F32)] * 7
        for e in range(3):

            def mean3(a):
                return rolled(thirds[a % 8], 36 * e - 36 * (a // 8), 1)

            w = [mean3(6 * e + k) * 0.015625 for k in range(6)]
            tot, inverse = settle(w, mean3(18 + e))
            inside = (lane >= 36 * e) & (lane < 36 * e + 36)
            found = [w[k] * inverse for k in range(6)] + [inverse]
            mixed = [jnp.where(inside, new, old) for new, old in zip(found, mixed)]
        for k in range(7):
            table[pl.ds(coef3_at + (g * 7 + k) * gy, gy), :] = mixed[k]
    keeps[5].start()
    for e in range(3):
        for g in range(gx):
            tails = [rows(g, 48 + r) for r in range(8)]
            for j in range(2):
                pairs = {a: rows(g, a * 2 + j) for a in [6 * e + k for k in range(6)] + [18 + e]}
                for i in range(2):

                    def mean(a):
                        r = i * 42 + a * 2 + j
                        value = pairs[a] if i == 0 else rolled(pairs[a], 64, 1)
                        value = jnp.where(lane < 64, value, rolled(tails[r % 8], 64 - 8 * (r // 8), 1))
                        return jnp.where(used, value, F32(0))

                    w = [mean(6 * e + k) * 0.0625 for k in range(6)]
                    tot, inverse = settle(w, mean(18 + e))
                    base = (e * 2 * gx + 2 * g + i) * 2 + j
                    for k in range(6):
                        table[pl.ds(coef_at + (base * 6 + k) * gy, gy), :] = w[k] * inverse
                    table[pl.ds(scale_at + base * gy, gy), :] = inverse
                    table[pl.ds(total_at + base * gy, gy), :] = tot * 1.25
        keeps[2 + e].start()
    keeps[0].start()
    keeps[1].start()
    for keep in keeps:
        keep.wait()


def coarse_levels(gx, gy, me_x, me_y, packed, table, arrivals, right2, error2, rows6):
    planes = 2 * gx
    (scale_at, _), (total_at, _), (coef_at, _), _, _, (coef3_at, _) = coarse_parts(gx, gy)

    def place(x, e, j):
        return (e * 2 * gx + x) * 2 + j

    error2[...] = jnp.zeros(error2.shape, F32)
    arrivals[0].wait()
    lane = lanes_of(gy)
    used = lane < 72
    row = lax.broadcasted_iota(jnp.int32, (gy, LANES), 0)
    first_row, last_row = row == 0, row == gy - 1
    zero = jnp.zeros((gy, LANES), F32)

    for g in range(gx):
        blocks = [packed[pl.ds(g * gy * 8 + r, gy, 8), :] for r in range(7)]
        for i in range(2):
            for e in range(3):
                for j in range(2):
                    r = (i * 3 + e) * 2 + j
                    right = blocks[r] if r < 6 else rolled(blocks[r - 6], 64, 1)
                    right = jnp.where(lane < 64, right, rolled(blocks[6], 64 - 8 * r, 1))
                    base = place(2 * g + i, e, j) * gy
                    right2[pl.ds(base, gy), :] = jnp.where(used, right, F32(0)) * table[pl.ds(scale_at + base, gy), :]

    def sweep2(value, x, e, j):
        base = place(x, e, j)
        v = value[x, j]
        near = [
            value[x + 1, j] if x + 1 < planes else None,
            value[x - 1, j] if x > 0 else None,
            value[x, 1] if j == 0 else jnp.where(last_row, zero, rolled(value[x, 0], -1, 0)),
            value[x, 0] if j == 1 else jnp.where(first_row, zero, rolled(value[x, 1], 1, 0)),
            rolled(v, -1, 1),
            rolled(v, 1, 1),
        ]
        out = 0.2 * v + right2[pl.ds(base * gy, gy), :]
        for k in range(6):
            if near[k] is not None:
                out = out + table[pl.ds(coef_at + (base * 6 + k) * gy, gy), :] * near[k]
        return out

    cells = [(x, j) for x in range(planes) for j in range(2)]
    source = lax.broadcasted_iota(jnp.int32, (LANES, LANES), 0)
    target = lax.broadcasted_iota(jnp.int32, (LANES, LANES), 1)
    halves = [jnp.where((source < 72) & ((source >> 1) + 36 * e == target), F32(0.125), F32(0)) for e in range(3)]
    doubles = [jnp.where((target < 72) & ((target >> 1) + 36 * e == source), F32(1), F32(0)) for e in range(3)]
    before, sums = [], []
    for e in range(3):
        if e == 0:
            arrivals[1].wait()
        arrivals[2 + e].wait()
        value = {(x, j): right2[pl.ds(place(x, e, j) * gy, gy), :] for x, j in cells}
        value = {(x, j): sweep2(value, x, e, j) for x, j in cells}
        before.append(value)
        resid = {
            (x, j): (sweep2(value, x, e, j) - value[x, j]) * table[pl.ds(total_at + place(x, e, j) * gy, gy), :] for x, j in cells
        }
        for g in range(gx):
            sums.append(
                (resid[2 * g, 0] + resid[2 * g, 1]) + (resid[2 * g + 1, 0] + resid[2 * g + 1, 1])
            )
    arrivals[5].wait()
    right3 = sum(exact_dot(jnp.concatenate(sums[e * gx : (e + 1) * gx], axis=0), halves[e]) for e in range(3))

    def coef_of(g, k):
        return table[pl.ds(coef3_at + (g * 7 + k) * gy, gy), :]

    right = [right3[g * gy : (g + 1) * gy] * coef_of(g, 6) for g in range(gx)]
    value = right
    for step in range(7):
        new = []
        for g in range(gx):
            v = value[g]
            out = 0.2 * v + right[g]
            if g + 1 < gx:
                out = out + coef_of(g, 0) * value[g + 1]
            if g > 0:
                out = out + coef_of(g, 1) * value[g - 1]
            out = out + coef_of(g, 2) * jnp.where(last_row, zero, rolled(v, -1, 0))
            out = out + coef_of(g, 3) * jnp.where(first_row, zero, rolled(v, 1, 0))
            out = out + coef_of(g, 4) * rolled(v, -1, 1)
            out = out + coef_of(g, 5) * rolled(v, 1, 1)
            new.append(out)
        value = new
    found = jnp.concatenate(value, axis=0)
    refined = [exact_dot(found, doubles[e]) for e in range(3)]
    for e in range(3):
        value = {
            (x, j): before[e][x, j] + refined[e][(x // 2) * gy : (x // 2 + 1) * gy] for x, j in cells
        }
        for step in range(2):
            value = {(x, j): sweep2(value, x, e, j) for x, j in cells}
        for x, j in cells:
            error2[pl.ds((((x + 2) * 3 + e) * 2 + j) * (gy + 16) + 8, gy), :] = value[x, j]
    for plane in range(6):
        for e in range(3):
            for step, j, target in ((0, 0, 0), (0, 1, 1), (1, 0, 2), (1, 1, 3), (-1, 0, 6), (-1, 1, 7)):
                start = (((2 * me_x + plane) * 3 + e) * 2 + j) * (gy + 16) + 8 + me_y + step
                rows6[pl.ds((plane * 3 + e) * 8 + target, 1), :] = error2[pl.ds(start, 1), :]
            rows6[pl.ds((plane * 3 + e) * 8 + 4, 2), :] = jnp.zeros((2, LANES), F32)


def finish(gx, gy, table_far, coef1_far, packed, error1, right1, stat, sides0, field2, sides2, out,
           table, coef1, right2, error2, rows6, fine2, rows1, fine1, arrived):
    inner = pl.ds(18 * 16, 8 * 18 * 16)
    pieces = [(table_far, table, pl.ds(first, size)) for first, size in coarse_parts(gx, gy)]
    pieces.append((coef1_far, coef1, inner))
    arrivals = [
        pltpu.make_async_copy(far.at[rows, :], near.at[rows, :], arrived.at[i])
        for i, (far, near, rows) in enumerate(pieces)
    ]
    for copy in arrivals:
        copy.start()
    me_x, me_y = lax.axis_index("gx"), lax.axis_index("gy")
    coarse_levels(gx, gy, me_x, me_y, packed, table, arrivals, right2, error2, rows6)
    arrivals[6].wait()

    source = lax.broadcasted_iota(jnp.int32, (LANES, LANES), 0)
    target = lax.broadcasted_iota(jnp.int32, (LANES, LANES), 1)
    cell = jnp.where(target >= 96, target - LANES, target)
    wanted = (cell >= -4) & (cell < 68) & ((cell >> 1) + HALO2 == source)
    widened = exact_dot(rows6[...], jnp.where(wanted, F32(1), F32(0)))
    fine2[pl.ds(0, 144, 2), :] = widened
    fine2[pl.ds(1, 144, 2), :] = widened

    row = lax.broadcasted_iota(jnp.int32, (8, LANES), 0)
    for e in range(3):
        get = middle_coef(coef1, right1, e)
        value = {}
        for x in range(-3, 7):
            value[x] = [
                error1[pl.ds(((x + 3) * 3 + e) * 16, 16), :] + fine2[pl.ds(((x // 2 + 2) * 3 + e) * 16, 16), :]
            ]
        value = {x: swept(x, value, get, 1) for x in range(-2, 6)}
        value = {x: swept(x, value, get, 1) for x in range(-1, 5)}
        for x in range(-1, 5):
            whole = value[x][0]
            rows1[pl.ds(((x + 1) * 3 + e) * 8, 8), :] = jnp.where(row == 7, whole[8:], whole[:8])

    inner = jnp.where((target >> 1) == source, F32(1), F32(0))
    outer = jnp.where((target < 2) & (source == 64), F32(1), F32(0))
    outer = jnp.where((target >= 126) & (source == 127), F32(1), outer)
    for tile, matrix in ((0, inner), (1, outer)):
        widened = exact_dot(rows1[...], matrix)
        fine1[pl.ds(288 * tile, 144, 2), :] = widened
        fine1[pl.ds(288 * tile + 1, 144, 2), :] = widened

    for e in range(3):
        get = fine_coef(stat, sides0, e)
        value = {}
        for x in range(-2, 10):
            start = ((x // 2 + 1) * 3 + e) * 16
            value[x] = [
                field2[pl.ds(((x + 2) * 3 + e) * 16, 16), :] + fine1[pl.ds(start, 16), :],
                side_tile(sides2, (x + 2) * 16, 2 * e, 2) + fine1[pl.ds(288 + start, 16), :],
            ]
        value = {x: swept(x, value, get, 2) for x in range(-1, 9)}
        for x in range(8):
            out[e, x] = swept(x, value, get, 1)[0][:8]


def both_ways(axis, up, down):
    devices = lax.axis_size(axis)
    pairs = [(i, i + 1) for i in range(devices - 1)]
    return lax.ppermute(up, axis, pairs), lax.ppermute(down, axis, [(b, a) for a, b in pairs])


def to_all(value, devices):
    blocks = value.reshape(devices, value.shape[0] // devices, LANES)
    return lax.all_to_all(blocks, ("gx", "gy"), 0, 0).reshape(value.shape)


def per_device(couplings, diagonal, right_side, guess):
    gx, gy = lax.axis_size("gx"), lax.axis_size("gy")
    inputs = jnp.concatenate([couplings, diagonal, right_side, guess])

    stat, field, total, zup, zdown, coef1, scale1, total1 = call(
        prepare_whole, "prepare", [1344, 192, 192, Z_ROWS, Z_ROWS, 288, 48, 48], [inputs], scratch=[672, 336, 168, 88, 48]
    )
    zlow, zhigh = both_ways("gz", zup, zdown)
    side, xup, xdown = call(fine_x, "fine_x", [64, x_rows(FINE), x_rows(FINE)], [stat, field, zlow, zhigh])
    (shared,) = call(share, "share", [SHARED], [zlow, zhigh, zup], scratch=[96])
    shared = lax.all_gather(shared, ("gx", "gy"), tiled=True)
    xlow, xhigh = both_ways("gx", xup, xdown)
    yup, ydown = call(fine_y, "fine_y", [y_rows(FINE)] * 2, [stat, field, side, xlow, xhigh])
    ylow, yhigh = both_ways("gy", yup, ydown)
    stat, sides0, field2, middle, zup, zdown = call(
        fine_sweeps, "fine_sweeps", [FINE[0].grown_rows(), FINE[2].grown_rows(), 192, 384, 192, 192],
        [stat, field, side, xlow, xhigh, ylow, yhigh, total, coef1, scale1, total1],
        scratch=[FINE[1].grown_rows(), 96],
    )

    zlow, zhigh = both_ways("gz", zup, zdown)
    x_full, y_full = x_rows(MIDDLE), y_rows(MIDDLE)
    x_sent, y_sent = squeezed(x_full, X_SQUEEZE), squeezed(y_full, Y_SQUEEZE)
    coef1, right1, side, side_coef, side_right, side_total, xup, xdown = call(
        middle_x, "middle_x", [288, 48, 64, 288, 48, 48, x_sent, x_sent], [middle, field2, zlow, zhigh], scratch=[x_full] * 2
    )
    xlow, xhigh = both_ways("gx", xup, xdown)
    level1 = [coef1, right1, field2, side, side_coef, side_right]
    xlow, xhigh, yup, ydown = call(
        middle_y, "middle_y", [x_full, x_full, y_sent, y_sent], [*level1, xlow, xhigh], scratch=[y_full] * 2
    )
    ylow, yhigh = both_ways("gy", yup, ydown)
    right1, field2, sides2, error1, packed, coef1 = call(
        middle_sweeps, "middle_sweeps", [s.grown_rows() for s in MIDDLE[1:4]] + [480, gx * gy * 8],
        [*level1, xlow, xhigh, ylow, yhigh, total1, side_total], far_outs=[FAR],
        scratch=[MIDDLE[i].grown_rows() for i in (0, 4, 5)] + [32, 32, 16, y_full, y_full], copies=1,
    )
    packed = to_all(packed, gx * gy)

    rows = sum(coarse_parts(gx, gy)[-1])
    (table,) = call(
        lambda *refs: coarse_coefs(gx, gy, *refs), "coarse_coefs", [], [shared], far_outs=[FAR], scratch=[rows], copies=6
    )

    vmem = pl.BlockSpec(memory_space=pltpu.VMEM)
    far = pl.BlockSpec(memory_space=pltpu.HBM)
    near = [packed, error1, right1, stat, sides0, field2, sides2]
    scratch = [rows, MIDDLE[0].grown_rows(), 12 * gx * gy, (2 * gx + 4) * 6 * (gy + 16), 144, 288, 144, 576]
    return pl.pallas_call(
        lambda *refs: finish(gx, gy, *refs),
        name="finish",
        out_shape=jax.ShapeDtypeStruct(guess.shape, F32),
        in_specs=[far] * 2 + [vmem] * len(near),
        out_specs=vmem,
        scratch_shapes=[pltpu.VMEM((rows, LANES), F32) for rows in scratch] + [pltpu.SemaphoreType.DMA((7,))],
        compiler_params=pltpu.CompilerParams(vmem_limit_bytes=GRANT),
    )(table, coef1, *near)


def solution(mesh):
    spec = P(None, "gx", "gy", "gz")
    return jax.shard_map(per_device, mesh=mesh, in_specs=(spec,) * 4, out_specs=spec, check_vma=False)
```
